128 devices in a mesh: dp: 32 (over x, z, core), fsdp: 4 (over y).
Axes of the slice: x: 4, y: 4, z: 4, core: 2. Of those that a mesh axis runs over, the one named last changes fastest.
Arguments:
- atoms: bfloat16 [64, 640, 128], P('dp', 'fsdp'), may hold values from -6 to 6
- atom_cond: bfloat16 [64, 640, 128], P('dp', 'fsdp'), may hold values from -6 to 6
- atom_pairs: bfloat16 [640, 128, 16], P('fsdp'), may hold values from -6 to 6
- atom_counts: int32 [64, 512], P('dp'), may hold values from 1 to 24, as said below
- tokens: bfloat16 [64, 512, 768], P('dp', 'fsdp'), may hold values from -6 to 6
- token_cond: bfloat16 [64, 512, 384], P('dp', 'fsdp'), may hold values from -6 to 6
- token_pairs: bfloat16 [512, 512, 128], P('fsdp'), may hold values from -6 to 6
- cotangent: bfloat16 [64, 512, 768], P('dp', 'fsdp'), may hold values from -6 to 6
- atom_mod: bfloat16 [128, 512], replicated, may hold values from -0.5 to 0.5
- atom_mod_bias: bfloat16 [512], replicated, may hold values from -3 to 3
- atom_heads_in: bfloat16 [128, 512], replicated, may hold values from -0.5 to 0.5
- atom_heads_out: bfloat16 [128, 128], replicated, may hold values from -1.5 to 1.5
- atom_pair_proj: bfloat16 [16, 4], replicated, may hold values from -1.5 to 1.5
- atom_gate_up: bfloat16 [128, 512], replicated, may hold values from -0.5 to 0.5
- atom_down: bfloat16 [256, 128], replicated, may hold values from -0.375 to 0.375
- pool_proj: bfloat16 [128, 768], P('fsdp'), may hold values from -0.5 to 0.5
- token_mod: bfloat16 [384, 3072], P('fsdp'), may hold values from -0.3125 to 0.3125
- token_mod_bias: bfloat16 [3072], replicated, may hold values from -3 to 3
- token_heads_in: bfloat16 [768, 3072], P('fsdp'), may hold values from -0.21875 to 0.21875
- token_heads_out: bfloat16 [768, 768], P('fsdp'), may hold values from -0.875 to 0.875
- token_pair_proj: bfloat16 [128, 16], replicated, may hold values from -0.5 to 0.5
- token_gate_up: bfloat16 [768, 3072], P('fsdp'), may hold values from -0.21875 to 0.21875
- token_down: bfloat16 [1536, 768], P('fsdp'), may hold values from -0.15625 to 0.15625
Outputs:
- output_tokens: float32 [64, 512, 768], P('dp', 'fsdp')
- grad_tokens: float32 [64, 512, 768], P('dp', 'fsdp')
- grad_atoms: float32 [64, 640, 128], P('dp', 'fsdp')
- grad_atom_mod: float32 [128, 512], replicated
- grad_atom_mod_bias: float32 [512], replicated
- grad_atom_heads_in: float32 [128, 512], replicated
- grad_atom_heads_out: float32 [128, 128], replicated
- grad_atom_pair_proj: float32 [16, 4], replicated
- grad_atom_gate_up: float32 [128, 512], replicated
- grad_atom_down: float32 [256, 128], replicated
- grad_pool_proj: float32 [128, 768], P('fsdp')
- grad_token_mod: float32 [384, 3072], P('fsdp')
- grad_token_mod_bias: float32 [3072], replicated
- grad_token_heads_in: float32 [768, 3072], P('fsdp')
- grad_token_heads_out: float32 [768, 768], P('fsdp')
- grad_token_pair_proj: float32 [128, 16], replicated
- grad_token_gate_up: float32 [768, 3072], P('fsdp')
- grad_token_down: float32 [1536, 768], P('fsdp')
The draws below stay inside these ranges and needn't reach their ends.
Inputs may be any that keep to these rules, and one draw needn't show every extreme that they name: `atom_counts`: each row sums to 640; every token owns at least one atom; tokens below 448 own exactly one atom each, and in every row some token owns exactly 24.
All inputs are finite; a program needn't handle non-finite values.
Results may differ from the reference program's by a relative error of at most 0.02.
Values may be sent and summed in bfloat16 or wider, within the bound.
A program may use at most 256 MiB of HBM per device.

```python
import jax
import jax.numpy as jnp
from jax import lax

TOK_S = 512
ATOM_S = 640
MAXA = 24
A = 128
HA = 4
CP = 16
FA = 256
WQ = 32
WK = 128
D = 768
H = 16
CS = 384
CZ = 128
F = 1536
SAMPLES = 64


def draw_atom_counts(key, part):
    key = jax.random.fold_in(key, 11)
    polymer = TOK_S // 8
    extra_total = ATOM_S - TOK_S
    rest_total = extra_total - (MAXA - 1)
    others = polymer - 1
    level = rest_total // others
    spare = rest_total % others
    spread_most = min(level, MAXA - 2 - level)
    base = level + (jnp.arange(others, dtype=jnp.int32) < spare).astype(jnp.int32)
    pair_count = others // 2
    key_shift, key_order = jax.random.split(key)
    shifts = jax.random.randint(key_shift, (SAMPLES, pair_count), 0, spread_most + 1, dtype=jnp.int32)
    paired = jnp.stack([shifts, -shifts], axis=-1).reshape(SAMPLES, 2 * pair_count)
    paired = jnp.pad(paired, ((0, 0), (0, others - 2 * pair_count)))
    extras = jnp.concatenate([jnp.full((SAMPLES, 1), MAXA - 1, jnp.int32), base[None, :] + paired], axis=1)
    extras = jax.random.permutation(key_order, extras, axis=1, independent=True)
    extras = jnp.concatenate([jnp.zeros((SAMPLES, TOK_S - polymer), jnp.int32), extras], axis=1)
    return (extras + 1).astype(jnp.int32)


def levels(rng, extent, cuts, least, high):
    def one(position, shards_of):
        draws = jax.random.uniform(jax.random.fold_in(jax.random.fold_in(rng, 6), position), (shards_of,), jnp.float32, least / len(cuts), high / len(cuts))
        return jnp.repeat(jnp.exp(draws), extent[position] // shards_of).reshape((-1,) + (1,) * (len(extent) - position - 1))

    gain = one(*cuts[0])
    for cut in cuts[1:]:
        gain = gain * one(*cut)
    return gain


def gaussian(own_key, extent, spread, most, cuts=(), held_as=jnp.bfloat16):
    entries = jax.random.normal(own_key, extent, jnp.float32) * spread
    if len(cuts) > 0:
        entries = levels(own_key, extent, cuts, -0.22, 0.18) * entries
    return jnp.clip(entries, min=-most, max=most).astype(held_as)


def setup_inputs(seed: int = 0) -> dict:
    streams_of = jax.random.split(jax.random.key(seed), 24)
    return {
        "atoms": gaussian(streams_of[0], (SAMPLES, ATOM_S, A), 1.0, 6.0, ((0, 32), (1, 4))),
        "atom_cond": gaussian(streams_of[1], (SAMPLES, ATOM_S, A), 1.0, 6.0, ((0, 32), (1, 4))),
        "atom_pairs": gaussian(streams_of[2], (ATOM_S, WK, CP), 1.0, 6.0, ((0, 4),)),
        "atom_counts": draw_atom_counts(jax.random.fold_in(streams_of[23], 71), 0),
        "tokens": gaussian(streams_of[4], (SAMPLES, TOK_S, D), 1.0, 6.0, ((0, 32), (1, 4))),
        "token_cond": gaussian(streams_of[5], (SAMPLES, TOK_S, CS), 1.0, 6.0, ((0, 32), (1, 4))),
        "token_pairs": gaussian(streams_of[6], (TOK_S, TOK_S, CZ), 1.0, 6.0, ((0, 4),)),
        "cotangent": gaussian(streams_of[7], (SAMPLES, TOK_S, D), 1.0, 6.0, ((0, 32), (1, 4))),
        "atom_mod": gaussian(streams_of[8], (A, 4 * A), A ** -0.5, 0.5),
        "atom_mod_bias": gaussian(streams_of[9], (4 * A,), 0.5, 3.0),
        "atom_heads_in": gaussian(streams_of[10], (A, 4 * A), A ** -0.5, 0.5),
        "atom_heads_out": gaussian(streams_of[11], (A, A), (A // 8) ** -0.5, 1.5),
        "atom_pair_proj": gaussian(streams_of[12], (CP, HA), CP ** -0.5, 1.5),
        "atom_gate_up": gaussian(streams_of[13], (A, 2 * FA), A ** -0.5, 0.5),
        "atom_down": gaussian(streams_of[14], (FA, A), FA ** -0.5, 0.375),
        "pool_proj": gaussian(streams_of[15], (A, D), A ** -0.5, 0.5, ((0, 4),)),
        "token_mod": gaussian(streams_of[16], (CS, 4 * D), CS ** -0.5, 0.3125, ((0, 4),)),
        "token_mod_bias": gaussian(streams_of[17], (4 * D,), 0.5, 3.0),
        "token_heads_in": gaussian(streams_of[18], (D, 4 * D), D ** -0.5, 0.21875, ((0, 4),)),
        "token_heads_out": gaussian(streams_of[19], (D, D), (D // 16) ** -0.5, 0.875, ((0, 4),)),
        "token_pair_proj": gaussian(streams_of[20], (CZ, H), CZ ** -0.5, 0.5),
        "token_gate_up": gaussian(streams_of[21], (D, 2 * F), D ** -0.5, 0.21875, ((0, 4),)),
        "token_down": gaussian(streams_of[22], (F, D), F ** -0.5, 0.15625, ((0, 4),)),
    }


epsilon = 1e-05
highest = lax.Precision.HIGHEST
masked = -1e+30

@jax.custom_vjp
def low(v):
    return lax.optimization_barrier(v.astype(jnp.bfloat16)).astype(jnp.float32)

@jax.custom_vjp
def low_back(v):
    return v

def low_keep(v):
    return (low(v), None)

def low_pass(kept, grad):
    return (grad,)

def back_keep(v):
    return (v, None)

def back_low(kept, grad):
    return (low(grad),)
low.defvjp(low_keep, low_pass)
low_back.defvjp(back_keep, back_low)

def rounded(value):
    return low_back(low(value))

def matmul(left, right):
    return jnp.dot(left, right, precision=highest)

def adaln(hidden, cond, w_mod, b_mod):
    channels = hidden.shape[-1]
    modulate = low_back(matmul(cond, w_mod) + b_mod)
    center = hidden - lax.optimization_barrier(jnp.mean(hidden, axis=-1, keepdims=True))
    normal = center * lax.rsqrt(lax.optimization_barrier(jnp.mean(center * center, axis=-1, keepdims=True)) + epsilon)
    normed = normal * jax.nn.sigmoid(modulate[:, :channels]) + modulate[:, channels:2 * channels]
    return (normed, modulate[:, 2 * channels:3 * channels], modulate[:, 3 * channels:])

def atom_attend(packed, pairs, w_pair):
    atom_rows = packed.shape[0]
    channels = packed.shape[1] // 3
    head_size = channels // HA
    block_count = atom_rows // WQ
    reach_count = WK // WQ
    rim_size = (WK - WQ) // 2
    queries = packed[:, :channels].reshape(block_count, WQ, HA, head_size)
    padded = jnp.pad(packed[:, channels:], ((rim_size, rim_size), (0, 0)))
    pieces = padded.reshape(block_count + reach_count - 1, WQ, 2 * channels)
    windows = jnp.concatenate([pieces[i:i + block_count] for i in range(reach_count)], axis=1)
    keys = windows[..., :channels].reshape(block_count, WK, HA, head_size)
    values = windows[..., channels:].reshape(block_count, WK, HA, head_size)
    bias = jnp.einsum('bqkc,ch->bhqk', pairs.reshape(block_count, WQ, WK, CP), w_pair, precision=highest)
    scores = low_back(jnp.einsum('bqhd,bkhd->bhqk', queries, keys, precision=highest) * head_size ** (-0.5) + bias)
    place = WQ * jnp.arange(block_count)[:, None] - rim_size + jnp.arange(WK)[None, :]
    valid = (place >= 0) & (place < atom_rows)
    scores = jnp.where(valid[:, None, None, :], scores, masked)
    weights = low(jax.nn.softmax(scores, axis=-1))
    mixed = jnp.einsum('bhqk,bkhd->bqhd', weights, values, precision=highest)
    return low_back(mixed.reshape(atom_rows, channels))

def token_attend(packed, pairs, w_pair):
    channels = packed.shape[1] // 3
    head_size = channels // H
    queries = packed[:, :channels].reshape(-1, H, head_size)
    keys = packed[:, channels:2 * channels].reshape(-1, H, head_size)
    values = packed[:, 2 * channels:].reshape(-1, H, head_size)
    bias = jnp.einsum('qkc,ch->hqk', pairs, w_pair, precision=highest)
    scores = low_back(jnp.einsum('qhd,khd->hqk', queries, keys, precision=highest) * head_size ** (-0.5) + bias)
    weights = low(jax.nn.softmax(scores, axis=-1))
    mixed = jnp.einsum('hqk,khd->qhd', weights, values, precision=highest)
    return low_back(mixed.reshape(-1, channels))

def block(hidden, cond, weights, attend):
    w_mod, b_mod, w_in, w_out, w_gate_up, w_down = weights
    channels = hidden.shape[-1]
    normed, gate_att, gate_ff = adaln(hidden, cond, w_mod, b_mod)
    normed = low(normed)
    packed = rounded(matmul(normed, w_in))
    mixed = attend(packed[:, :3 * channels])
    gated = low(mixed * jax.nn.sigmoid(packed[:, 3 * channels:]))
    branch = low_back(matmul(gated, w_out))
    both = rounded(matmul(normed, w_gate_up))
    half_size = w_gate_up.shape[1] // 2
    hidden_units = low(jax.nn.silu(both[:, :half_size]) * both[:, half_size:])
    trans = low_back(matmul(hidden_units, w_down))
    return hidden + jax.nn.sigmoid(gate_att) * branch + jax.nn.sigmoid(gate_ff) * trans

def sample_forward(params, atom_pairs, token_pairs, sample):
    atoms, atom_cond, atom_counts, tokens, token_cond = sample
    atom_weights = (params[0], params[1], params[2], params[3], params[5], params[6])
    token_weights = (params[8], params[9], params[10], params[11], params[13], params[14])
    atom_out = block(atoms, atom_cond.astype(jnp.float32), atom_weights, lambda packed: atom_attend(packed, atom_pairs, params[4]))
    ends = jnp.cumsum(atom_counts, dtype=jnp.int32)
    starts = ends - atom_counts
    place = jnp.arange(ATOM_S, dtype=jnp.int32)
    member = ((place[None, :] >= starts[:, None]) & (place[None, :] < ends[:, None])).astype(jnp.float32)
    pooled = matmul(member, low(atom_out)) / atom_counts[:, None].astype(jnp.float32)
    pooled = low(low_back(pooled))
    middle = tokens + low_back(matmul(pooled, params[7]))
    return block(middle, token_cond.astype(jnp.float32), token_weights, lambda packed: token_attend(packed, token_pairs, params[12]))

def reference(atoms, atom_cond, atom_pairs, atom_counts, tokens, token_cond, token_pairs, cotangent, atom_mod, atom_mod_bias, atom_heads_in, atom_heads_out, atom_pair_proj, atom_gate_up, atom_down, pool_proj, token_mod, token_mod_bias, token_heads_in, token_heads_out, token_pair_proj, token_gate_up, token_down):
    params = tuple((weight.astype(jnp.float32) for weight in (atom_mod, atom_mod_bias, atom_heads_in, atom_heads_out, atom_pair_proj, atom_gate_up, atom_down, pool_proj, token_mod, token_mod_bias, token_heads_in, token_heads_out, token_pair_proj, token_gate_up, token_down)))
    atom_pair_wide = atom_pairs.astype(jnp.float32)
    token_pair_wide = token_pairs.astype(jnp.float32)

    def forward(atoms_in, tokens_in, weights):
        stepper = jax.checkpoint(lambda sample: sample_forward(weights, atom_pair_wide, token_pair_wide, sample))
        return lax.map(stepper, (atoms_in, atom_cond, atom_counts, tokens_in, token_cond))
    output, pull = jax.vjp(forward, atoms.astype(jnp.float32), tokens.astype(jnp.float32), params)
    grad_atoms, grad_tokens, grads = pull(cotangent.astype(jnp.float32))
    return (output, grad_tokens, grad_atoms, grads[0], grads[1], grads[2], grads[3], grads[4], grads[5], grads[6], grads[7], grads[8], grads[9], grads[10], grads[11], grads[12], grads[13], grads[14])
```

```python
import functools
import math
import types
import typing

import jax
import jax.numpy as jnp
from jax import lax
from jax.experimental import pallas as pl
from jax.experimental.pallas import tpu as pltpu
from jax.sharding import Mesh, PartitionSpec as P

MESH = pl.DeviceIdType.MESH
DP = ("x", "z", "c")
HA = 4
CP = 16
WQ = 32
WK = 128
H = 16

epsilon = 1e-05
masked = -1e30


def dot(left, right):
    return jnp.dot(left, right, preferred_element_type=jnp.float32)


def dot_nt(left, right):
    return lax.dot_general(left, right, (((1,), (1,)), ((), ())), preferred_element_type=jnp.float32)


def dot_tn(left, right):
    return lax.dot_general(left, right, (((0,), (0,)), ((), ())), preferred_element_type=jnp.float32)


def low(value):
    return value.astype(jnp.bfloat16)


def wide(value):
    return value.astype(jnp.float32)


def normalize(hidden):
    center = hidden - jnp.mean(hidden, axis=-1, keepdims=True)
    inverse = lax.rsqrt(jnp.mean(center * center, axis=-1, keepdims=True) + epsilon)
    return center * inverse, inverse


def lane_mask(first, last, width, dtype):
    lane = lax.broadcasted_iota(jnp.int32, (1, width), 1)
    return jnp.where((lane >= first) & (lane < last), 1.0, 0.0).astype(dtype)


def vmem(count):
    return [pl.BlockSpec(memory_space=pltpu.VMEM)] * count


def hbm(count):
    return [pl.BlockSpec(memory_space=pl.ANY)] * count


def params(megabytes, **more):
    return pltpu.CompilerParams(vmem_limit_bytes=megabytes * 1024 * 1024, **more)


HEAD = 48
GROUP = 8
SPAN = HEAD * GROUP


class Whole:
    def __init__(self, ref):
        self.ref = ref

    def __getitem__(self, index):
        some = self.ref[...] if index is Ellipsis else self.ref[:, :, index[1]]
        return some.reshape(-1, some.shape[-1])

    def blocks(self, first, count):
        return self.ref[pl.ds(first, count)].reshape(-1, self.ref.shape[-1])


def token_block(r, me, ready, rows_ready, flush):
    tokens, cond, pooled, cotangent, bias, b_mod = r.tokens, r.tcond, r.pooled, r.cotangent, r.bias, r.b_mod
    w_pool, w_mod, w_in = Whole(r.w_pool), Whole(r.w_mod), Whole(r.w_in)
    w_out, w_gu, w_down = Whole(r.w_out), Whole(r.w_gu), Whole(r.w_down)
    output, dkv, dqg, dbranch, dtrans = r.output, r.dkv, r.dqg, r.dbranch, r.dtrans
    dgu, dgates, dx_far, dx_own, normal, squash = r.dgu, r.dgates, r.dx_far, r.dx_own, r.normal, r.squash
    inverse, ssum, kv, probs, dscores = r.inverse, r.ssum, r.kv, r.probs, r.dscores
    stack_do, stack_q, gate_att, mixed, qg = r.stack_do, r.stack_q, r.gate_att, r.mixed, r.qg
    ssum[...] = jnp.zeros_like(ssum)
    scale = HEAD ** (-0.5)

    def rows_of(ref, y):
        return ref[y].reshape(256, ref.shape[-1])

    def modulation(c, k):
        part = pl.ds(k * 768, 768)
        bias = wide(b_mod[...])
        bias = jnp.concatenate([bias[i : i + 1] for i in range(6 * k, 6 * k + 6)], axis=1)
        return dot(c, w_mod[:, part]) + bias

    def normed(y, own):
        hidden = wide(rows_of(tokens, y)) + dot(rows_of(pooled, y), w_pool[...])
        c = rows_of(cond, y)
        n, inv = normalize(hidden)
        sq = jax.nn.sigmoid(modulation(c, 0))
        x = low(n * sq + modulation(c, 1))
        r.x_turned[:, pl.ds(pl.multiple_of(y * 256, 256), 256)] = x.T
        kv[y] = low(dot(x, w_in[:, pl.ds(768, 1536)])).reshape(2, 128, 1536)
        if own:
            r.x_own[...] = x
            output[...] = hidden.reshape(2, 128, 768)
            normal[...] = n
            squash[...] = sq
            inverse[...] = jnp.broadcast_to(inv, inverse.shape)
            gate_att[...] = jax.nn.sigmoid(modulation(c, 2))
            dx_own[...] = jax.nn.sigmoid(modulation(c, 3))
            qg[:, :, pl.ds(0, 768)] = low(dot(x, w_in[:, pl.ds(0, 768)])).reshape(2, 128, 768)
            qg[:, :, pl.ds(768, 768)] = low(dot(x, w_in[:, pl.ds(2304, 768)])).reshape(2, 128, 768)

    normed(me, True)
    rows_ready()

    @pl.loop(1, 4)
    def _(k):
        normed(lax.rem(me + k, 4), False)

    flush(r.x_turned, r.normal, r.squash, r.inverse)

    def windows():
        for j in range(GROUP):
            first, last = HEAD * j, HEAD * (j + 1)
            t0, t1 = first // 128, (last - 1) // 128 + 1
            yield j, slice(t0 * 128, t1 * 128), first - t0 * 128, last - t0 * 128, range(t0, t1)

    def group_of(ref, s, at):
        return ref[:, s, :, pl.ds(pl.multiple_of(at, 128), SPAN)].reshape(512, SPAN)

    @pl.loop(0, 2)
    def _(s):
        @pl.loop(0, 2)
        def _(half):
            lanes = pl.ds(pl.multiple_of(half * SPAN, 128), SPAN)
            q = qg[s, :, lanes]
            k = group_of(kv, s, half * SPAN)
            v = group_of(kv, s, 768 + half * SPAN)
            tiles = [None] * 3
            for j, span, a, b, covers in windows():
                width = span.stop - span.start
                masked_q = q[:, span] * lane_mask(a, b, width, jnp.bfloat16)
                score = dot_nt(masked_q, k[:, span]) * scale + wide(bias[half * GROUP + j])
                score = jnp.exp(score - jnp.max(score, axis=-1, keepdims=True))
                p = low(score * (1.0 / jnp.sum(score, axis=-1, keepdims=True)))
                probs[s, half * GROUP + j] = p
                o = dot(p, v[:, span]) * lane_mask(a, b, width, jnp.float32)
                for t in covers:
                    piece = o[:, t * 128 - span.start : (t + 1) * 128 - span.start]
                    tiles[t] = piece if tiles[t] is None else tiles[t] + piece
            mixed[s, :, lanes] = jnp.concatenate(tiles, axis=1)

    mix = mixed[...].reshape(256, 768)
    sg = jax.nn.sigmoid(wide(qg[:, :, pl.ds(768, 768)].reshape(256, 768)))
    gated = low(mix * sg)
    r.gated_turned[...] = gated.T
    ready(OUT)
    branch = dot(gated, w_out[...])
    dy = wide(cotangent[...].reshape(256, 768))
    sga = gate_att[...]
    dgates[:, pl.ds(0, 768)] = low(dy * branch * sga * (1.0 - sga))
    dbranch[...] = low(dy * sga)
    output[...] += (sga * branch).reshape(2, 128, 768)

    ready(GU)
    x = r.x_own[...]
    for k in range(4):
        part = pl.ds(k * 768, 768)
        dgu[:, part] = low(dot(x, w_gu[:, part]))
    ready(DOWN)
    trans = None
    for k in range(2):
        a = wide(dgu[:, pl.ds(k * 768, 768)])
        b = wide(dgu[:, pl.ds(1536 + k * 768, 768)])
        inner = low(a * jax.nn.sigmoid(a) * b)
        r.inner_turned[pl.ds(k * 768, 768), :] = inner.T
        some = dot(inner, w_down.blocks(2 * k, 2))
        trans = some if trans is None else trans + some
    flush(r.gated_turned, r.dbranch, r.inner_turned)
    sgf = dx_own[...]
    output[...] += (sgf * trans).reshape(2, 128, 768)
    dgates[:, pl.ds(768, 768)] = low(dy * trans * sgf * (1.0 - sgf))
    dtrans[...] = low(dy * sgf)

    flush(r.output, r.dgates, r.dtrans)
    for k in range(2):
        dinner = dot_nt(dtrans[...], w_down.blocks(2 * k, 2))
        a = wide(dgu[:, pl.ds(k * 768, 768)])
        b = wide(dgu[:, pl.ds(1536 + k * 768, 768)])
        sq = jax.nn.sigmoid(a)
        dgu[:, pl.ds(k * 768, 768)] = low(dinner * b * sq * (1.0 + a * (1.0 - sq)))
        dgu[:, pl.ds(1536 + k * 768, 768)] = low(dinner * a * sq)
    flush(r.dgu)
    dgated = dot_nt(dbranch[...], w_out[...])
    mix = mixed[...].reshape(256, 768)
    sg = jax.nn.sigmoid(wide(qg[:, :, pl.ds(768, 768)].reshape(256, 768)))
    dqg[:, :, pl.ds(768, 768)] = low(dgated * mix * sg * (1.0 - sg)).reshape(2, 128, 768)
    mixed[...] = (dgated * sg).reshape(2, 128, 768)

    @pl.loop(0, 2)
    def _(s):
        @pl.loop(0, 2)
        def _(half):
            lanes = pl.ds(pl.multiple_of(half * SPAN, 128), SPAN)
            q = qg[s, :, lanes]
            do = low(mixed[s, :, lanes])
            k = group_of(kv, s, half * SPAN)
            v = group_of(kv, s, 768 + half * SPAN)
            tiles = [None] * 3
            for j, span, a, b, covers in windows():
                width = span.stop - span.start
                whole = lane_mask(span.start + a, span.start + b, SPAN, jnp.bfloat16)
                stack_q[j] = q * whole
                stack_do[j] = do * whole
                masked_do = do[:, span] * lane_mask(a, b, width, jnp.bfloat16)
                dp = dot_nt(masked_do, v[:, span])
                p = wide(probs[s, half * GROUP + j])
                ds = low(p * (dp - jnp.sum(p * dp, axis=-1, keepdims=True)))
                dscores[j] = ds
                ssum[half * GROUP + j] += ds
                dq = dot(ds, k[:, span]) * (lane_mask(a, b, width, jnp.float32) * scale)
                for t in covers:
                    piece = dq[:, t * 128 - span.start : (t + 1) * 128 - span.start]
                    tiles[t] = piece if tiles[t] is None else tiles[t] + piece
            dqg[s, :, lanes] = low(jnp.concatenate(tiles, axis=1))
            grads = dot_tn(dscores[...].reshape(1024, 512), stack_q[...].reshape(1024, SPAN)) * scale
            dkv[:, s, :, lanes] = low(grads).reshape(4, 128, SPAN)
            group = probs[s, pl.ds(half * GROUP, GROUP)].reshape(1024, 512)
            grads = dot_tn(group, stack_do[...].reshape(1024, SPAN))
            lanes = pl.ds(pl.multiple_of(768 + half * SPAN, 128), SPAN)
            dkv[:, s, :, lanes] = low(grads).reshape(4, 128, SPAN)

    flush(r.dqg, r.dkv, r.ssum)

    @pl.loop(0, 4)
    def _(y):
        dx_far[y] = low(dot_nt(rows_of(dkv, y), w_in[:, pl.ds(768, 1536)]))

    flush(r.dx_far)
    dx = dot_nt(dgu[...], w_gu[...])
    dx = dx + dot_nt(dqg[:, :, pl.ds(0, 768)].reshape(256, 768), w_in[:, pl.ds(0, 768)])
    dx_own[...] = dx + dot_nt(dqg[:, :, pl.ds(768, 768)].reshape(256, 768), w_in[:, pl.ds(2304, 768)])
    flush(r.dx_own)


RIM = (WK - WQ) // 2
ATOM = 128
OWN = 160
REACH = 112
REGION = OWN + 2 * REACH
A_HEAD = ATOM // HA


def atom_modulation(c, w_mod, b_mod, k):
    return dot(c, w_mod[:, pl.ds(k * ATOM, ATOM)]) + wide(b_mod[...])[k : k + 1]


def stacked_heads(rows, dtype):
    return jnp.concatenate(
        [rows * lane_mask(A_HEAD * h, A_HEAD * (h + 1), ATOM, dtype) for h in range(HA)], axis=0
    )


def unstacked_heads(rows):
    total = None
    for h in range(HA):
        own = rows[WQ * h : WQ * (h + 1)] * lane_mask(A_HEAD * h, A_HEAD * (h + 1), ATOM, jnp.float32)
        total = own if total is None else total + own
    return total


def window_probs(stacked, keys, bias, first_key, count):
    place = first_key + lax.broadcasted_iota(jnp.int32, (1, WK), 1)
    valid = (place >= 0) & (place < count)
    scores = dot_nt(stacked, keys) * A_HEAD ** (-0.5) + wide(bias)
    scores = jnp.where(valid, scores, masked)
    scores = jnp.exp(scores - jnp.max(scores, axis=-1, keepdims=True))
    return scores * (1.0 / jnp.sum(scores, axis=-1, keepdims=True))


def token_ranges(counts):
    wide_counts = jnp.concatenate([wide(counts[...]), jnp.zeros((6, 512), jnp.float32)], axis=0)
    row = lax.broadcasted_iota(jnp.int32, (512, 512), 0)
    lane = lax.broadcasted_iota(jnp.int32, (512, 512), 1)
    before = low(jnp.where(lane < row, 1.0, 0.0))
    until = low(jnp.where(lane <= row, 1.0, 0.0))
    some = low(wide_counts)
    return dot_nt(before, some), dot_nt(until, some), dot_nt(some, before), dot_nt(some, until)


def atom_row_bias(w_pair, pairs, bias):
    w = wide(w_pair[...])
    stacked = jnp.concatenate([jnp.broadcast_to(w[h : h + 1], (WQ, CP)) for h in range(HA)], axis=0)
    row = lax.broadcasted_iota(jnp.int32, (CP, 512), 0)
    lane = lax.broadcasted_iota(jnp.int32, (CP, 512), 1)
    spread = dot(low(stacked), low(jnp.where(row == lax.rem(lane, CP), 1.0, 0.0)))
    weight = low(spread * same_query())
    for b in range(OWN // WQ):
        some = pairs[pl.ds(b * WQ, WQ)].reshape(WQ * CP, WK)
        bias[b + 2] = low(dot(weight, some))


def same_query():
    row = lax.broadcasted_iota(jnp.int32, (128, 512), 0)
    lane = lax.broadcasted_iota(jnp.int32, (128, 512), 1)
    return jnp.where(lax.rem(row, WQ) == lax.div(lane, CP), 1.0, 0.0)


def atom_forward(s, me, atoms, cond, bias, w_mod, b_mod, w_in, w_out, w_gu, w_down, out, packed, mixed):
    region = pl.ds(REACH - RIM, OWN + 2 * RIM)
    own = slice(RIM, RIM + OWN)
    hidden = wide(atoms[s, region, :])
    c = cond[s, region, :]
    normal, _ = normalize(hidden)
    squash = jax.nn.sigmoid(atom_modulation(c, w_mod, b_mod, 0))
    x = low(normal * squash + atom_modulation(c, w_mod, b_mod, 1))
    packed[...] = low(dot(x, w_in[...]))
    results = []
    for w in range(OWN // WQ):
        at = w * WQ
        q = packed[pl.ds(at + RIM, WQ), pl.ds(0, ATOM)]
        k = packed[pl.ds(at, WK), pl.ds(ATOM, ATOM)]
        v = packed[pl.ds(at, WK), pl.ds(2 * ATOM, ATOM)]
        stacked = stacked_heads(q, jnp.bfloat16)
        p = window_probs(stacked, k, bias[w + 2], me * OWN + at - RIM, 4 * OWN)
        results.append(unstacked_heads(dot(low(p), v)))
    for w, result in enumerate(results):
        mixed[pl.ds(w * WQ, WQ), :] = result
    hidden, c, x = hidden[own], c[own], x[own]
    gate = jax.nn.sigmoid(wide(packed[pl.ds(RIM, OWN), pl.ds(3 * ATOM, ATOM)]))
    branch = dot(low(mixed[...] * gate), w_out[...])
    both = low(dot(x, w_gu[...]))
    a, b = wide(both[:, :256]), wide(both[:, 256:])
    trans = dot(low(a * jax.nn.sigmoid(a) * b), w_down[...])
    total = hidden + jax.nn.sigmoid(atom_modulation(c, w_mod, b_mod, 2)) * branch
    out[me, s] = low(total + jax.nn.sigmoid(atom_modulation(c, w_mod, b_mod, 3)) * trans)


def pool_atoms(s, rows, ranges, pooled):
    total = 4 * OWN
    place = wide(lax.broadcasted_iota(jnp.int32, (1, total), 1))
    start, end = ranges[0][:, s : s + 1], ranges[1][:, s : s + 1]
    member = jnp.where((place >= start) & (place < end), 1.0, 0.0)
    sums = dot(low(member), rows[:, s].reshape(total, ATOM)) / (end - start)
    pooled[:, s] = low(sums).reshape(4, 128, ATOM)


def atom_backward(
    s,
    me,
    atoms,
    cond,
    bias,
    grad_pooled,
    ranges,
    w_mod,
    b_mod,
    w_in,
    w_out,
    w_gu,
    w_down,
    grad_atoms,
    small,
    ssum,
    packed,
    mixed,
    grad_mixed,
    dkv,
    dq,
):
    total = 640
    first = me * OWN - REACH
    own = slice(REACH, REACH + OWN)
    scale = A_HEAD ** (-0.5)

    def add_small(block, value):
        for k in range(value.shape[0] // 128):
            for n in range(value.shape[1] // 128):
                tile = value[k * 128 : (k + 1) * 128, n * 128 : (n + 1) * 128]
                at = block + k + n
                small[at // 4, at % 4] += tile.reshape(16, 8, 128)

    hidden = wide(atoms[s])
    c = cond[s]
    normal, inverse = normalize(hidden)
    squash = jax.nn.sigmoid(atom_modulation(c, w_mod, b_mod, 0))
    x = low(normal * squash + atom_modulation(c, w_mod, b_mod, 1))
    packed[...] = low(dot(x, w_in[...]))

    place = wide(first + lax.broadcasted_iota(jnp.int32, (REGION, 1), 0))
    start, end = ranges[2][s : s + 1], ranges[3][s : s + 1]
    member = jnp.where((place >= start) & (place < end), 1.0, 0.0)
    owner = jnp.sum(member * (end - start), axis=-1, keepdims=True)
    dy = dot(low(member), grad_pooled[:, pl.ds(s * 128, 128)].reshape(512, ATOM)) / jnp.maximum(owner, 1.0)
    sga = jax.nn.sigmoid(atom_modulation(c, w_mod, b_mod, 2))
    dbranch = low(dy * sga)
    dgated = dot_nt(dbranch, w_out[...])
    gate = jax.nn.sigmoid(wide(packed[:, pl.ds(3 * ATOM, ATOM)]))
    grad_mixed[...] = low(dgated * gate)
    dkv[...] = jnp.zeros_like(dkv)

    def window(w, own):
        at = pl.multiple_of(w * WQ, WQ)
        query = pl.ds(at + RIM, WQ)
        q = stacked_heads(packed[query, pl.ds(0, ATOM)], jnp.bfloat16)
        k = packed[pl.ds(at, WK), pl.ds(ATOM, ATOM)]
        v = packed[pl.ds(at, WK), pl.ds(2 * ATOM, ATOM)]
        do = stacked_heads(grad_mixed[query, :], jnp.bfloat16)
        p = window_probs(q, k, bias[w], first + at, total)
        dp = dot_nt(do, v)
        ds = low(p * (dp - jnp.sum(p * dp, axis=-1, keepdims=True)))
        out = [dot_tn(ds, q) * scale, dot_tn(low(p), do)]
        if own:
            out += [unstacked_heads(dot(low(p), v)), unstacked_heads(dot(ds, k)) * scale, wide(ds)]
        return out

    for group in ((0, 1, 7, 8), (2, 3, 4, 5, 6)):
        results = {w: window(w, 2 <= w < 7) for w in group}
        for w, result in results.items():
            keys = pl.ds(w * WQ, WK)
            dkv[keys, pl.ds(0, ATOM)] += result[0]
            dkv[keys, pl.ds(ATOM, ATOM)] += result[1]
            if 2 <= w < 7:
                rows = pl.ds((w - 2) * WQ, WQ)
                mixed[rows, :] = result[2]
                dq[rows, :] = result[3]
                ssum[w - 2] += result[4]

    x, c, hidden, normal, inverse = x[own], c[own], hidden[own], normal[own], inverse[own]
    squash, dy, sga, dbranch, dgated = squash[own], dy[own], sga[own], dbranch[own], dgated[own]
    gate = gate[own]
    gated = low(mixed[...] * gate)
    branch = dot(gated, w_out[...])
    both = low(dot(x, w_gu[...]))
    a, b = wide(both[:, :256]), wide(both[:, 256:])
    sq = jax.nn.sigmoid(a)
    inner = low(a * sq * b)
    trans = dot(inner, w_down[...])
    sgf = jax.nn.sigmoid(atom_modulation(c, w_mod, b_mod, 3))
    dga = dy * branch * sga * (1.0 - sga)
    dgf = dy * trans * sgf * (1.0 - sgf)
    dtrans = low(dy * sgf)
    dinner = dot_nt(dtrans, w_down[...])
    dgu = low(jnp.concatenate([dinner * b * sq * (1.0 + a * (1.0 - sq)), dinner * a * sq], axis=1))
    dg = dgated * mixed[...] * gate * (1.0 - gate)
    dpacked = low(jnp.concatenate([dq[...], dkv[pl.ds(REACH, OWN), :], dg], axis=1))
    dx = dot_nt(dpacked, w_in[...]) + dot_nt(dgu, w_gu[...])
    dn = dx * squash
    dscale = dx * normal * squash * (1.0 - squash)
    dmod = low(jnp.concatenate([dscale, dx, dga, dgf], axis=1))
    grad_atoms[s] = dy + inverse * (
        dn
        - jnp.mean(dn, axis=-1, keepdims=True)
        - normal * jnp.mean(dn * normal, axis=-1, keepdims=True)
    )
    add_small(0, dot_tn(c, dmod))
    add_small(4, dot_tn(x, dpacked))
    add_small(8, dot_tn(gated, dbranch))
    add_small(9, dot_tn(x, dgu))
    add_small(13, dot_tn(inner, dtrans))
    sums = jnp.sum(wide(dmod), axis=0, keepdims=True)
    for n in range(4):
        small[3, 3, 0, pl.ds(n, 1), :] += sums[:, n * 128 : (n + 1) * 128]


RING = 4


class Ring:
    def __init__(self, axis):
        self.axis = axis
        self.me = lax.axis_index(axis)
        self.up = lax.rem(self.me + 1, RING)
        self.down = lax.rem(self.me + 3, RING)
        self.far = lax.rem(self.me + 2, RING)


class Copies:
    def __init__(self, send, recv):
        self.send, self.recv, self.used = send, recv, 0

    def start(self, axis, place, src, dst):
        made = pltpu.make_async_remote_copy(
            src_ref=src,
            dst_ref=dst,
            send_sem=self.send.at[self.used],
            recv_sem=self.recv.at[self.used],
            device_id={axis: place},
            device_id_type=MESH,
        )
        made.start()
        self.used += 1
        return made


def meet(rings, core=None):
    barrier = pltpu.get_barrier_semaphore()
    for ring in rings:
        for place in (ring.up, ring.down, ring.far):
            pl.semaphore_signal(barrier, 1, device_id={ring.axis: place}, device_id_type=MESH)
    if core is not None:
        pl.semaphore_signal(barrier, 1, device_id={"c": 1 - core}, device_id_type=MESH)
    pl.semaphore_wait(barrier, 3 * len(rings) + (core is not None))


def run_stages(parts):
    for k in range(max(len(stages) for stages in parts)):
        for stages in parts:
            if k < len(stages):
                stages[k]()


def nothing():
    pass


def add_into(target, others):
    def one(index):
        total = target[index]
        if len(others) > 1:
            total = total.astype(jnp.float32)
        for other in others:
            total = total + other[index].astype(total.dtype)
        target[index] = total.astype(target.dtype)

    lead = target.shape[:-3]
    if not lead:
        one(Ellipsis)
        return

    @pl.loop(0, math.prod(lead))
    def _(k):
        index, rest = [], k
        for size in reversed(lead):
            index.append(lax.rem(rest, size))
            rest = lax.div(rest, size)
        one(tuple(reversed(index)))


def scatter_stages(ring, copies, held, first, second):
    half = held.shape[1] // 2
    low_part, high_part = pl.ds(0, half), pl.ds(half, held.shape[1] - half)
    r1, r2 = first
    r3, r4 = second
    up, down, far = ring.up, ring.down, ring.far
    made = {}

    def send(k, src, dst, to):
        made[k] = copies.start(ring.axis, to, src, dst)

    def begin():
        send(1, held.at[far, low_part], r1, up)
        send(2, held.at[far, high_part], r2, down)
        send(3, held.at[up, high_part], r3.at[high_part], up)
        send(4, held.at[down, low_part], r4.at[low_part], down)

    def middle():
        made[1].wait_recv()
        add_into(held.at[up, low_part], [r1])
        send(5, held.at[up, low_part], r3.at[low_part], up)
        made[2].wait_recv()
        add_into(held.at[down, high_part], [r2])
        send(6, held.at[down, high_part], r4.at[high_part], down)

    def end():
        for k in (3, 4, 5, 6):
            made[k].wait_recv()
        add_into(held.at[ring.me], [r3, r4])
        for k in range(1, 7):
            made[k].wait_send()

    return [begin, middle, end]


def spread_stages(ring, copies, view, parts, landed=None):
    low_parts, high_parts = parts
    made = {}

    def send(k, place, some, to):
        made[k] = [copies.start(ring.axis, to, view(place, p), view(place, p)) for p in some]

    def arrived(*what):
        for k, place, some in what:
            for one in made[k]:
                one.wait_recv()
            tell(place, some)

    def tell(place, some):
        if landed is not None:
            for p in some:
                landed(place, p)

    def begin():
        send(0, ring.me, low_parts, ring.up)
        send(1, ring.me, high_parts, ring.down)
        send(2, ring.me, high_parts, ring.up)
        send(3, ring.me, low_parts, ring.down)
        tell(ring.me, (*low_parts, *high_parts))

    def middle():
        arrived((0, ring.down, low_parts))
        send(4, ring.down, low_parts, ring.up)
        arrived((1, ring.up, high_parts))
        send(5, ring.up, high_parts, ring.down)

    def end():
        arrived((2, ring.down, high_parts), (3, ring.up, low_parts))
        arrived((4, ring.far, low_parts), (5, ring.far, high_parts))
        for some in made.values():
            for one in some:
                one.wait_send()

    return [begin, middle, end]


def direct_stages(ring, copies, *views):
    made = []

    def begin():
        for place in (ring.up, ring.down, ring.far):
            for view in views:
                made.append(copies.start(ring.axis, place, view(ring.me), view(ring.me)))

    def end():
        for one in made:
            one.wait()

    return [begin, end]


IN, GU, MOD, DOWN, OUT, POOL = MATRICES = range(6)


class Front(typing.NamedTuple):
    given: object
    pairs: object
    cotangent: object
    counts: object
    atom_pairs: object
    aw_pair: object
    aw_mod: object
    ab_mod: object
    aw_in: object
    aw_out: object
    aw_gu: object
    aw_down: object
    b_mod: object
    w_pair: object
    w_pool_out: object
    results: object
    peer: object
    atoms: object
    acond: object
    abias: object
    pooled: object
    output: object
    x_turned: object
    dkv: object
    dqg: object
    gated_turned: object
    inner_turned: object
    dbranch: object
    dtrans: object
    dgu: object
    dgates: object
    dx_far: object
    dx_own: object
    normal: object
    squash: object
    inverse: object
    ssum: object
    w_in: object
    w_gu: object
    w_mod: object
    w_down: object
    w_out: object
    w_pool: object
    atom_out: object
    tcond: object
    tokens: object
    x_own: object
    pair_weight: object
    bias: object
    pair_rows: object
    pair_bufs: object
    packed: object
    amixed: object
    kv: object
    probs: object
    dscores: object
    stack_do: object
    stack_q: object
    gate_att: object
    mixed: object
    qg: object
    load: object
    pair_sems: object
    flush_sems: object
    send: object
    recv: object


FIRST_RESULT = 17


def columns(start, width):
    return pl.ds(pl.multiple_of(start, 128), width)


def rows(start, count):
    return pl.ds(pl.multiple_of(start, 16), count)


def matrix_stages(copies, full, core, x, y, z):
    moved = {name: [] for name in MATRICES}

    def block(far):
        return lax.rem(y.me + far, RING)

    def to_core(name, one):
        moved[name].append(copies.start("c", 1 - core, one, one))

    def in_y(name, first, cut, count, span, last=False):
        def view(place, p):
            return full[name].at[place, rows(first + p[0], p[1]), span]

        def landed(place, p):
            if place is not y.me:
                to_core(name, view(place, p))

        return spread_stages(y, copies, view, ([(0, cut)], [(cut, count - cut)]), landed if last else None)

    def in_plane(ring, name, place_of, count, width, last):
        def view(place, p):
            far, row, height, column, breadth = p
            first, start = place_of(place)
            return full[name].at[block(far), rows(first + row, height), columns(start + column, breadth)]

        if count >= 32:
            cut = (count // 2 + 15) // 16 * 16
            halves = (0, cut, 0, width), (cut, count - cut, 0, width)
        else:
            cut = width // 256 * 128
            halves = (0, count, 0, cut), (0, count, cut, width - cut)
        parts = [(1, 0, count, 0, width), (2, *halves[0])], [(3, 0, count, 0, width), (2, *halves[1])]
        return spread_stages(ring, copies, view, parts, (lambda place, p: to_core(name, view(place, p))) if last else None)

    def in_both(name, first_ring):
        ref, mid = full[name], core * 1536
        pieces = direct_stages(
            y,
            copies,
            lambda place: ref.at[place, rows(32 * x.me, 32), columns(mid + z.me * 384, 384)],
            lambda place: ref.at[place, rows(128 + 16 * x.me, 16), columns(mid + z.me * 384, 384)],
        )

        def x_then_z(base, height):
            one = in_plane(x, name, lambda p: (base + height * p, mid + z.me * 384), height, 384, False)
            return one, in_plane(z, name, lambda p: (base, mid + p * 384), 4 * height, 384, True)

        def z_then_x(base, height):
            one = in_plane(z, name, lambda p: (base + height * x.me, mid + p * 384), height, 384, False)
            return one, in_plane(x, name, lambda p: (base + height * p, mid), height, 1536, True)

        if first_ring is x:
            big, little = x_then_z(0, 32), z_then_x(128, 16)
        else:
            big, little = z_then_x(0, 32), x_then_z(128, 16)
        return [pieces, *([both_steps(p, q) for p, q in zip(a, b, strict=True)] for a, b in zip(big, little, strict=True))]

    def both_steps(p, q):
        def run():
            p()
            q()

        return run

    steps = {
        IN: in_both(IN, x),
        GU: in_both(GU, z),
        MOD: [
            in_y(MOD, 0, 48, 96, columns(core * 1536 + x.me * 384, 384)),
            in_plane(x, MOD, lambda place: (0, core * 1536 + place * 384), 96, 384, True),
        ],
        DOWN: [
            in_y(DOWN, 96 * z.me, 48, 96, columns(core * 384, 384)),
            in_plane(z, DOWN, lambda place: (96 * place, core * 384), 96, 384, True),
        ],
        OUT: [
            in_y(OUT, 48 * x.me, 32, 48, columns(core * 384, 384)),
            in_plane(x, OUT, lambda place: (48 * place, core * 384), 48, 384, True),
        ],
        POOL: [in_y(POOL, 0, 16, 32, columns(core * 384, 384), True)],
    }
    return steps, moved


def forward_kernel(spec, *refs):
    it = iter(refs)
    r = Front(*[next(it) if n is None else [next(it) for _ in range(n)] for n in spec])
    core = lax.axis_index("c")
    x, z, y = Ring("x"), Ring("z"), Ring("fsdp")
    me = y.me
    copies = Copies(r.send, r.recv)

    matrices = (r.w_in, r.w_gu, r.w_mod, r.w_down, r.w_out, r.w_pool)
    middle = pl.ds(REACH, OWN)
    targets = [ref.at[me] for ref in matrices] + [r.atoms.at[:, middle], r.acond.at[:, middle]]
    targets += [r.tcond.at[me], r.tokens.at[me]]
    loads = []
    for k, target in enumerate(targets):
        loads.append(pltpu.make_async_copy(r.given[k], target, r.load.at[k]))
        loads[-1].start()

    def fetch(chunk, slot):
        src = r.pairs.at[pl.ds(pl.multiple_of(core * 64 + chunk * 8, 8), 8)]
        return pltpu.make_async_copy(src, r.pair_bufs.at[slot], r.pair_sems.at[slot])

    for slot in range(2):
        fetch(slot, slot).start()
    meet((x, z, y), core)

    jobs, moved = matrix_stages(copies, matrices, core, x, y, z)
    late = []
    for ref in (r.tcond, r.tokens):
        parts = ([pl.ds(0, 1)], [pl.ds(1, 1)])
        late.append(spread_stages(y, copies, lambda place, p, ref=ref: ref.at[place, p], parts))
    atom_out = direct_stages(y, copies, lambda place: r.atom_out.at[place])
    halo = []

    def halo_begin():
        for ref in (r.atoms, r.acond):
            first, last = ref.at[:, pl.ds(REACH, REACH)], ref.at[:, pl.ds(OWN, REACH)]
            halo.append(copies.start("fsdp", y.up, last, ref.at[:, pl.ds(0, REACH)]))
            halo.append(copies.start("fsdp", y.down, first, ref.at[:, pl.ds(REACH + OWN, REACH)]))
        halo.append(copies.start("fsdp", y.up, r.abias.at[pl.ds(5, 2)], r.abias.at[pl.ds(0, 2)]))
        halo.append(copies.start("fsdp", y.down, r.abias.at[pl.ds(2, 2)], r.abias.at[pl.ds(7, 2)]))

    def halo_end():
        for one in halo:
            one.wait()

    def step(kind, stage, *which):
        for name in which:
            jobs[name][kind][stage]()

    def cores(name):
        for one in moved[name]:
            one.wait()

    def bias_steps(first, last):
        pair_rows, pair_bufs = r.pair_rows, r.pair_bufs

        @pl.loop(first, last)
        def _(i):
            for slot in range(2):
                fetch(2 * i + slot, slot).wait()
                for q in range(0, 8, 2):
                    both = jnp.concatenate([pair_bufs[slot, q], pair_bufs[slot, q + 1]], axis=1)
                    value = dot_nt(r.pair_weight[...], both)
                    pair_rows[:, 8 * slot + q, :] = value[:16]
                    pair_rows[:, 8 * slot + q + 1, :] = value[16:]

                @pl.when(i < 3)
                def _():
                    fetch(2 * i + 2 + slot, slot).start()

            r.bias[:, rows(core * 64 + i * 16, 16), :] = low(pair_rows[...])

    flushed, staged = [], r[FIRST_RESULT:]

    def flush(*which):
        for ref in which:
            k = next(i for i, one in enumerate(staged) if one is ref)
            flushed.append(pltpu.make_async_copy(ref, r.results[k], r.flush_sems.at[k]))
            flushed[-1].start()
            hand_over(ref)

    theirs = (r.x_turned, r.gated_turned, r.inner_turned, r.dbranch, r.dtrans, r.dgu, r.dgates)

    def hand_over(ref):
        for k, one in enumerate(theirs):
            if one is ref:
                width = ref.shape[-1] // 2
                some = ref if k < 3 else ref.at[:, columns((1 - core) * width, width)]
                flushed.append(copies.start("c", 1 - core, some, r.peer[k]))

    for name in (IN, GU, MOD):
        loads[name].wait()
        step(0, 0, name)
    atom_row_bias(r.aw_pair, r.atom_pairs, r.abias)
    for k in (6, 7):
        loads[k].wait()
    halo_begin()
    for name in (POOL, OUT, DOWN):
        loads[name].wait()
        step(0, 0, name)
    for k in (8, 9):
        loads[k].wait()
    flushed.append(copies.start("c", 1 - core, r.tcond.at[me], r.peer[7]))
    step(0, 1, IN)
    step(1, 0, IN)
    step(0, 1, GU)
    step(1, 0, GU)
    turned = wide(r.w_pair[...])
    blank = jnp.zeros_like(turned)
    r.pair_weight[pl.ds(0, 16), :] = low(jnp.concatenate([turned, blank], axis=1))
    r.pair_weight[pl.ds(16, 16), :] = low(jnp.concatenate([blank, turned], axis=1))
    step(0, 1, MOD)
    step(1, 1, IN)
    step(0, 1, POOL, OUT, DOWN)
    for steps in late:
        steps[0]()
    step(0, 2, MOD)
    step(1, 0, MOD)
    ranges = token_ranges(r.counts)
    step(1, 2, IN)
    step(2, 0, IN)
    halo_end()
    atom_weights = (r.aw_mod, r.ab_mod, r.aw_in, r.aw_out, r.aw_gu, r.aw_down)
    atom_room = (r.atom_out, r.packed, r.amixed)
    atom_forward(0, me, r.atoms, r.acond, r.abias, *atom_weights, *atom_room)
    step(1, 1, MOD, GU)
    for name in (OUT, DOWN):
        step(0, 2, name)
        step(1, 0, name)
    atom_forward(1, me, r.atoms, r.acond, r.abias, *atom_weights, *atom_room)
    atom_out[0]()
    flush(r.atoms, r.acond, r.abias)
    step(2, 1, IN)
    step(1, 2, GU)
    step(2, 0, GU)
    bias_steps(0, 2)
    step(1, 2, MOD)
    step(0, 2, POOL)
    step(1, 1, OUT, DOWN)
    for steps in late:
        steps[1]()
    atom_out[1]()
    bias_steps(2, 4)
    half_bias = r.bias.at[:, rows(core * 64, 64), :]
    bias_moved = copies.start("c", 1 - core, half_bias, half_bias)
    for s in range(2):
        pool_atoms(s, r.atom_out, ranges, r.pooled)
    flush(r.pooled)
    flushed.append(copies.start("c", 1 - core, r.pooled.at[me], r.peer[8]))
    step(2, 2, IN)
    step(2, 1, GU)
    step(1, 2, OUT, DOWN)
    for name in (POOL, MOD, IN):
        cores(name)
    keep = pltpu.make_async_copy(r.w_pool, r.w_pool_out, r.flush_sems.at[len(r.results)])
    keep.start()
    flushed.append(keep)

    def rows_ready():
        for steps in late:
            steps[2]()
        step(2, 2, GU)
        bias_moved.wait()

    token_block(r, me, cores, rows_ready, flush)
    for one in flushed:
        one.wait()
    assert copies.used == FRONT_COPIES


FRONT_COPIES = 317


def forward_pass(given, pairs, cotangent, counts, atom_pairs, aw_pair, atom_weights, b_mod, w_pair):
    bf, f32 = jnp.bfloat16, jnp.float32
    full = [((4, *a.shape), a.dtype) for a in given]
    results = (
        ((2, REGION, ATOM), bf),
        ((2, REGION, ATOM), bf),
        ((9, 128, 128), bf),
        ((4, 2, 128, 128), bf),
        ((2, 128, 768), f32),
        ((768, 1024), bf),
        ((4, 2, 128, 1536), bf),
        ((2, 128, 1536), bf),
        ((768, 256), bf),
        ((1536, 256), bf),
        ((256, 768), bf),
        ((256, 768), bf),
        ((256, 3072), bf),
        ((256, 1536), bf),
        ((4, 256, 768), bf),
        ((256, 768), f32),
        ((256, 768), f32),
        ((256, 768), f32),
        ((256, 128), f32),
        ((16, 128, 512), bf),
    )
    peer = (
        ((768, 1024), bf),
        ((768, 256), bf),
        ((1536, 256), bf),
        ((256, 384), bf),
        ((256, 384), bf),
        ((256, 1536), bf),
        ((256, 768), bf),
        ((2, 128, 384), bf),
        ((2, 128, 128), bf),
    )
    outs = (full[5], *results, *peer)
    scratch = (
        *results,
        *full[:6],
        full[6],
        *full[8:],
        ((256, 768), bf),
        ((32, 256), bf),
        ((16, 128, 512), bf),
        ((16, 16, 512), f32),
        ((2, 8, 512, 128), bf),
        ((OWN + 2 * RIM, 512), bf),
        ((OWN, ATOM), f32),
        ((4, 2, 128, 1536), bf),
        ((2, 16, 128, 512), bf),
        ((8, 128, 512), bf),
        ((8, 128, SPAN), bf),
        ((8, 128, SPAN), bf),
        ((256, 768), f32),
        ((2, 128, 768), f32),
        ((2, 128, 1536), bf),
    )
    semaphores = [
        pltpu.SemaphoreType.DMA((n,)) for n in (10, 2, len(results) + 1, FRONT_COPIES, FRONT_COPIES)
    ]
    spec = [10] + [None] * 13 + [None, len(results), len(peer)] + [None] * (len(scratch) + len(semaphores))
    return pl.pallas_call(
        functools.partial(forward_kernel, spec),
        out_shape=[jax.ShapeDtypeStruct(*o) for o in outs],
        in_specs=hbm(11) + vmem(12),
        out_specs=hbm(len(outs)),
        scratch_shapes=[pltpu.VMEM(*s) for s in scratch] + semaphores,
        compiler_params=params(62, collective_id=1, has_side_effects=True),
        name="forward_pass",
    )(*given, pairs, cotangent, counts, atom_pairs, aw_pair, *atom_weights, b_mod, w_pair)


class Region:
    def __init__(self, t, x, z, y, done):
        self.t, self.done = t, {ring.axis: ring.me for ring in done}
        self.x, self.z, self.y = x, z, y

    def index(self, ring, place, half):
        known = {**self.done, ring.axis: place}
        split, out = half, []
        for one in (self.y, self.z):
            if one.axis in known:
                out.append(known[one.axis])
            elif split < 2:
                out.append(pl.ds(2 * split, 2))
                split = 2
            else:
                out.append(pl.ds(0, 4))
        inner = self.x.axis in known
        start, count = (known[self.x.axis] * self.t, self.t) if inner else (0, 4 * self.t)
        if split < 2:
            cut = count // 2
            start, count = (start, cut) if split == 0 else (start + cut, count - cut)
        return (*out, pl.ds(start, count))

    def shapes(self, ring):
        known = {*self.done, ring.axis}
        lead = [4 for one in (self.y, self.z) if one.axis not in known]
        whole = (*lead, self.t if self.x.axis in known else 4 * self.t)
        cut = whole[0] // 2
        return (cut, *whole[1:]), (whole[0] - cut, *whole[1:]), whole, whole


def region_stages(copies, ring, region, part, rooms):
    r1, r2, r3, r4 = rooms
    up, down, far = ring.up, ring.down, ring.far
    cut = r1.shape[0]
    halves = (pl.ds(0, cut), pl.ds(cut, r3.shape[0] - cut))
    made = {}

    def piece(place, half=2):
        return part.at[region.index(ring, place, half)]

    def send(k, src, dst, to):
        made[k] = copies.start(ring.axis, to, src, dst)

    def begin():
        send(1, piece(far, 0), r1, up)
        send(2, piece(far, 1), r2, down)
        send(3, piece(up, 1), r3.at[halves[1]], up)
        send(4, piece(down, 0), r4.at[halves[0]], down)

    def middle():
        made[1].wait_recv()
        add_into(piece(up, 0), [r1])
        send(5, piece(up, 0), r3.at[halves[0]], up)
        made[2].wait_recv()
        add_into(piece(down, 1), [r2])
        send(6, piece(down, 1), r4.at[halves[1]], down)

    def end():
        for k in (3, 4, 5, 6):
            made[k].wait_recv()
        add_into(piece(ring.me), [r3, r4])
        for k in range(1, 7):
            made[k].wait_send()

    return [begin, middle, end]


def direct_region_stages(copies, ring, region, part, rooms):
    made = []

    def begin():
        for place, room in zip((ring.up, ring.down, ring.far), rooms, strict=False):
            made.append(copies.start(ring.axis, place, part.at[region.index(ring, place, 2)], room))

    def end():
        for one in made:
            one.wait_recv()
        add_into(part.at[region.index(ring, ring.me, 2)], list(rooms[:3]))
        for one in made:
            one.wait_send()

    return [begin, end]


def part_stages(copies, core, x, z, y, order, t, part, out, rooms, direct=2):
    stages, done = [], []
    for k, ring in enumerate(order):
        region = Region(t, x, z, y, done)
        kind = direct_region_stages if k >= direct else region_stages
        stages += kind(copies, ring, region, part, rooms[4 * k : 4 * k + 4])
        done.append(ring)
    base = core * (4 * t)
    halves = (((0, 2),), ((2, 2),))
    pair = (((0, 2 * t),), ((2 * t, 2 * t),))

    def keep():
        out[z.me, pl.ds(base + x.me * t, t)] = part[y.me, z.me, pl.ds(x.me * t, t)]

    stages.append(keep)
    if order[0] is z:
        stages += direct_stages(x, copies, lambda place: out.at[z.me, pl.ds(base + place * t, t)])
        if direct < 2:
            return stages + direct_stages(z, copies, lambda place: out.at[place, pl.ds(base, 4 * t)])
        return stages + spread_stages(
            z, copies, lambda place, p: out.at[place, pl.ds(base + p[0], p[1])], pair
        )
    stages += direct_stages(z, copies, lambda place: out.at[place, pl.ds(base + x.me * t, t)])
    if direct < 2:
        return stages + direct_stages(x, copies, lambda place: out.at[:, pl.ds(base + place * t, t)])
    return stages + spread_stages(
        x, copies, lambda place, p: out.at[pl.ds(*p), pl.ds(base + place * t, t)], halves
    )


def swap_stages(copies, core, refs):
    made = []

    def begin():
        for ref in refs:
            made.append(copies.start("c", 1 - core, ref, ref))

    def end():
        for one in made:
            one.wait()

    return [begin, end]


def room_shapes(t, order, tile, dtype, direct=2):
    place = {axis: types.SimpleNamespace(axis=axis, me=0) for axis in order}
    x, z, y = [place[axis] for axis in ("x", "z", "fsdp")]
    shapes, done = [], []
    for axis in order:
        rooms = Region(t, x, z, y, done).shapes(place[axis])
        if order.index(axis) >= direct:
            rooms = (rooms[2],) * 3 + ((1,),)
        shapes += [pltpu.VMEM((*shape, *tile), dtype) for shape in rooms]
        done.append(place[axis])
    return shapes


COPIES = 153
ORDER_GU = ("x", "z", "fsdp")
ORDER_IN = ("z", "fsdp", "x")
ORDER_DO = ("fsdp", "x", "z")
ORDER_ME = ("z", "fsdp", "x")
ORDER_ML = ("x", "fsdp", "z")
ORDER_SM = ("fsdp", "x", "z")
ORDERS = (ORDER_GU, ORDER_IN, ORDER_DO, ORDER_ME, ORDER_ML)
SIZES = (9, 9, 7, 3, 3)


class Back(typing.NamedTuple):
    x_turned: object
    gated_turned: object
    inner_turned: object
    dkv: object
    dqg: object
    dbranch: object
    dtrans: object
    dgu: object
    dgates: object
    dx_far: object
    ssum: object
    pairs: object
    peer_given: object
    dx_own: object
    normal: object
    squash: object
    inverse: object
    cotangent: object
    w_pool: object
    tcond: object
    pooled: object
    atoms: object
    acond: object
    abias: object
    counts: object
    aw_mod: object
    ab_mod: object
    aw_in: object
    aw_out: object
    aw_gu: object
    aw_down: object
    atom_pairs: object
    tiles: object
    small_sums: object
    grad_tokens_out: object
    grad_atoms_out: object
    own: object
    peer: object
    parts: object
    outs: object
    rooms: object
    small: object
    small_low: object
    small_peer: object
    small_out: object
    small_rooms: object
    held: object
    dx_rooms: object
    spread: object
    dmod: object
    dmid: object
    grad_tokens: object
    grad_atoms: object
    packed: object
    mixed: object
    grad_mixed: object
    akv: object
    aq: object
    ascores: object
    pair_rows: object
    pair_bufs: object
    scores: object
    scores_peer: object
    pair_sum: object
    load: object
    pair_sems: object
    keep: object
    send: object
    recv: object


class Rows(typing.NamedTuple):
    x: object
    gated: object
    inner: object
    dkv: object
    dqg: object
    dbranch: object
    dtrans: object
    dgu: object
    dgates: object
    cond: object
    pooled: object
    dmod: object
    dmid: object


def backward_kernel(spec, *refs):
    it = iter(refs)
    r = Back(*[next(it) if n is None else [next(it) for _ in range(n)] for n in spec])
    core = lax.axis_index("c")
    x, z, y = Ring("x"), Ring("z"), Ring("fsdp")
    me = y.me
    copies = Copies(r.send, r.recv)
    own, peer = Rows(*r.own, None, None), Rows(*r.peer)
    span_of = {ref.shape[-1]: columns(core * (ref.shape[-1] // 2), ref.shape[-1] // 2) for ref in own[3:9]}

    def half(ref, whose):
        width = ref.shape[-1] // 2
        lead = (slice(None),) * (len(ref.shape) - 1)
        return ref.at[(*lead, columns(whose * width, width))]

    sources = (r.x_turned, r.gated_turned, r.inner_turned, r.dkv, r.dqg, r.dbranch, r.dtrans, r.dgu, r.dgates)
    sources = (*sources, r.tcond, r.pooled.at[me])
    given = dict(zip((0, 1, 2, 5, 6, 7, 8, 9, 10), r.peer_given, strict=True))
    loads = [pltpu.make_async_copy(r.dx_far, r.held, r.load.at[0])]
    loads[0].start()
    moved = {}
    for k in (4, 3, 0, 7, 8, 9, 2, 6, 1, 5, 10):
        loads.append(pltpu.make_async_copy(sources[k], own[k], r.load.at[k + 1]))
        loads[-1].start()
        if k in given:
            moved[k] = pltpu.make_async_copy(given[k], peer[k], r.load.at[k + 12])
            moved[k].start()

    def fetch(chunk, slot):
        first = pl.ds(pl.multiple_of(core * 64 + chunk * 8, 8), 8)
        return pltpu.make_async_copy(r.pairs.at[first], r.pair_bufs.at[slot], r.pair_sems.at[slot])

    for slot in range(2):
        fetch(slot, slot).start()
    scores_load = pltpu.make_async_copy(r.ssum, r.scores, r.pair_sems.at[2])
    scores_load.start()
    r.small[...] = jnp.zeros_like(r.small)
    r.pair_sum[...] = jnp.zeros_like(r.pair_sum)
    meet((x, z, y), core)

    def pair_steps(first, last):
        for i in range(first, last):
            span = pl.ds(16 * i, 16)
            r.pair_rows[...] = wide(r.scores[:, rows(core * 64 + 16 * i, 16)]) + wide(r.scores_peer[:, span])
            total = jnp.zeros(r.pair_sum.shape, jnp.float32)
            for slot in range(2):
                fetch(2 * i + slot, slot).wait()
                for q in range(0, 8, 2):
                    at = 8 * slot + q
                    both = jnp.concatenate([r.pair_bufs[slot, q], r.pair_bufs[slot, q + 1]], axis=1)
                    left = jnp.concatenate([r.pair_rows[:, at, :], r.pair_rows[:, at + 1, :]], axis=0)
                    total = total + dot(low(left), both)
                if i < 3:
                    fetch(2 * i + 2 + slot, slot).start()
            r.pair_sum[...] += total

    loads[0].wait()
    dx_stages = scatter_stages(y, copies, r.held, r.dx_rooms[:2], r.dx_rooms[2:])
    dx_stages[0]()

    scores_load.wait()
    scores_moved = copies.start("c", 1 - core, r.scores.at[:, rows((1 - core) * 64, 64)], r.scores_peer)
    for one in loads[1:]:
        one.wait()
    for k in (4, 3):
        moved[k] = copies.start("c", 1 - core, half(own[k], 1 - core), peer[k])

    def ready(*which):
        for k in which:
            moved[k].wait()

    mine = columns(me * 256, 256)
    part_gu, part_in, part_do, part_me, part_ml = r.parts

    def place_columns(part, value, first, row_tiles, step, offset=0):
        value = low(value)
        for n in range(value.shape[1] // 128):
            tiles = value[:, n * 128 : (n + 1) * 128].reshape(4, 4, row_tiles, 16, 128)
            part[:, :, pl.ds((first + n) * step + offset, row_tiles)] = tiles

    def flat(ref):
        return ref[...].reshape(-1, ref.shape[-1])

    def mine_of(ref):
        some = ref[(*(slice(None),) * (len(ref.shape) - 1), span_of[ref.shape[-1]])]
        return some.reshape(-1, some.shape[-1])

    def weights_gu():
        ready(0, 7)
        for k in range(2):
            span = pl.ds(k * 768, 768)
            some = own.dgu[:, columns(core * 1536 + k * 768, 768)]
            value = dot(own.x[:, mine], some) + dot(peer.x[:, mine], peer.dgu[:, span])
            place_columns(part_gu, value, 6 * k, 3, 3)

    def weights_do():
        ready(1, 2, 5, 6)
        value = dot(own.inner[...], mine_of(own.dtrans)) + dot(peer.inner[...], peer.dtrans[...])
        place_columns(part_do, value, 0, 6, 9)
        value = dot(own.gated[...], mine_of(own.dbranch)) + dot(peer.gated[...], peer.dbranch[...])
        place_columns(part_do, value, 0, 3, 9, 6)

    def weights_in():
        ready(3, 4)
        value = dot(own.x[:, mine], mine_of(own.dqg)) + dot(peer.x[:, mine], flat(peer.dqg))
        place_columns(part_in, value, 6 * core, 3, 3)
        value = dot(own.x[...], mine_of(own.dkv)) + dot(peer.x[...], flat(peer.dkv))
        place_columns(part_in, value, 6 * (1 - core), 3, 3)

    def finish():
        dx = r.dx_own[...] + wide(r.held[me])
        n, sq = r.normal[...], r.squash[...]
        dn = dx * sq
        r.dmod[:, pl.ds(0, 768)] = low(dx * n * sq * (1.0 - sq))
        r.dmod[:, pl.ds(768, 768)] = low(dx)
        grad = wide(r.cotangent[...].reshape(256, 768)) + r.inverse[:, :1] * (
            dn - jnp.mean(dn, axis=-1, keepdims=True) - n * jnp.mean(dn * n, axis=-1, keepdims=True)
        )
        r.grad_tokens[...] = grad.reshape(2, 128, 768)
        r.dmid[...] = low(grad)
        r.spread[me] = low(dot_nt(r.dmid[...], flat(r.w_pool)))

    def place_mod(part, value):
        value = low(value)
        for n in range(6):
            tiles = value[:, n * 128 : (n + 1) * 128].reshape(4, 6, 16, 128)
            for k in range(2):
                at = 6 * n + 3 * k
                part[:, at // 9, pl.ds(at % 9, 3)] = tiles[:, 3 * k : 3 * k + 3]

    def weights_me():
        ready(8, 9)
        own_turned, peer_turned = flat(own.cond).T, flat(peer.cond).T
        place_mod(part_me, dot(own_turned, mine_of(own.dgates)) + dot(peer_turned, peer.dgates[...]))

    def weights_ml():
        ready(10)
        for one in moved_late:
            one.wait()
        own_turned, peer_turned = flat(own.cond).T, flat(peer.cond).T
        span = columns(core * 768, 768)
        place_mod(part_ml, dot(own_turned, r.dmod[:, span]) + dot(peer_turned, peer.dmod[...]))
        span = columns(core * 384, 384)
        left = (flat(own.pooled).T, flat(peer.pooled).T)
        value = low(dot(left[0], r.dmid[:, span]) + dot(left[1], peer.dmid[...]))
        for n in range(3):
            part_ml[:, n, pl.ds(9, 2)] = value[:, n * 128 : (n + 1) * 128].reshape(4, 2, 16, 128)

    stages = []
    rings = {"x": x, "z": z, "fsdp": y}
    for k, order in enumerate(ORDERS):
        order = [rings[axis] for axis in order]
        rooms = r.rooms[12 * k : 12 * k + 12]
        direct = 1 if k == 4 else 2
        some = part_stages(copies, core, x, z, y, order, SIZES[k], r.parts[k], r.outs[k], rooms, direct)
        stages.append(some)
        span = pl.ds(core * 4 * SIZES[k], 4 * SIZES[k])
        stages[-1] += swap_stages(copies, core, [r.outs[k].at[:, span]])
    s_gu, s_in, s_do, s_me, s_ml = stages

    kept = []

    def out_copy(src, dst):
        kept.append(pltpu.make_async_copy(src, dst, r.keep.at[len(kept)]))
        kept[-1].start()

    def go(*which):
        for some in which:
            some.pop(0)()

    room = (r.packed, r.mixed, r.grad_mixed, r.akv, r.aq)
    weights = (r.aw_mod, r.ab_mod, r.aw_in, r.aw_out, r.aw_gu, r.aw_down)
    ranges = token_ranges(r.counts)
    r.ascores[...] = jnp.zeros_like(r.ascores)

    def atoms_of(s):
        rows_in = (r.atoms, r.acond, r.abias, r.spread, ranges)
        atom_backward(s, me, *rows_in, *weights, r.grad_atoms, r.small, r.ascores, *room)

    weights_gu()
    go(s_gu)
    scores_moved.wait()
    pair_steps(0, 4)
    dx_stages[1]()
    weights_in()
    go(s_in)
    weights_me()
    go(s_me)
    dx_stages[2]()
    finish()
    moved_late = [
        copies.start("c", 1 - core, half(r.dmod, 1 - core), peer.dmod),
        copies.start("c", 1 - core, half(r.dmid, 1 - core), peer.dmid),
    ]
    spread = direct_stages(y, copies, lambda place: r.spread.at[place])
    spread[0]()
    out_copy(r.grad_tokens, r.grad_tokens_out)
    weights_do()
    go(s_do, s_gu)
    spread[1]()
    atoms_of(0)
    go(s_gu, s_gu, s_in)
    atoms_of(1)
    out_copy(r.grad_atoms, r.grad_atoms_out)
    r.small[3, 3, 1] = atom_pair_grad(r.ascores, r.atom_pairs)
    total = r.pair_sum[:16, :128] + r.pair_sum[16:, 128:]
    r.small[3, 3, pl.ds(3, 2)] = total.reshape(2, 8, 128)
    sums = jnp.sum(wide(r.dmod[...]), axis=0, keepdims=True)
    sums = jnp.concatenate([sums, jnp.sum(wide(own.dgates[...]), axis=0, keepdims=True)], axis=1)
    for n in range(24):
        r.small[3, 3, 5 + n // 8, pl.ds(n % 8, 1), :] = sums[:, n * 128 : (n + 1) * 128]

    order = [rings[axis] for axis in ORDER_SM]
    r.small_low[...] = low(r.small[...].reshape(4, 4, 8, 16, 128))
    theirs, ours = r.small_low.at[:, :, pl.ds((1 - core) * 4, 4)], r.small_low.at[:, :, pl.ds(core * 4, 4)]
    small_moved = []

    def small_begin():
        small_moved.append(copies.start("c", 1 - core, theirs, r.small_peer))

    def small_merge():
        small_moved[0].wait()
        add_into(ours, [r.small_peer])

    s_small = [small_begin, small_merge]
    s_small += part_stages(
        copies, core, x, z, y, order, 1, ours, r.small_out.at[me], r.small_rooms, 0
    )
    span = pl.ds(core * 4, 4)
    s_small += direct_stages(y, copies, lambda place: r.small_out.at[place, :, span])
    s_small += swap_stages(copies, core, [r.small_out.at[:, :, span]])
    s_small.pop(0)()
    go(s_in, s_in, s_do, s_me)
    weights_ml()
    go(s_ml)
    for k, some in enumerate(stages):
        some.append(lambda k=k: out_copy(r.outs[k], r.tiles[k]))
    s_small.append(lambda: out_copy(r.small_out, r.small_sums))
    run_stages([s_small, s_ml, s_gu, s_in, s_do, s_me])
    for one in kept:
        one.wait()
    assert copies.used == COPIES


def atom_pair_grad(scores, pairs):
    total = jnp.zeros((128, 512), jnp.float32)
    for b in range(OWN // WQ):
        some = pairs[pl.ds(b * WQ, WQ)].reshape(WQ * CP, WK)
        total = total + dot_nt(low(scores[b]), some)
    total = total * same_query()
    heads = [jnp.sum(total[h * WQ : (h + 1) * WQ], axis=0, keepdims=True) for h in range(HA)]
    heads = jnp.concatenate([*heads, jnp.zeros((8 - HA, 512), jnp.float32)], axis=0)
    row = lax.broadcasted_iota(jnp.int32, (512, 128), 0)
    lane = lax.broadcasted_iota(jnp.int32, (512, 128), 1)
    pick = low(jnp.where(lax.rem(row, CP) == lane, 1.0, 0.0))
    return dot(low(heads), pick)


def backward_pass(in_hbm, peer_given, in_vmem):
    bf, f32 = jnp.bfloat16, jnp.float32
    tile = (16, 128)
    rows_own = [
        ((768, 1024), bf),
        ((768, 256), bf),
        ((1536, 256), bf),
        ((4, 2, 128, 1536), bf),
        ((2, 128, 1536), bf),
        ((256, 768), bf),
        ((256, 768), bf),
        ((256, 3072), bf),
        ((256, 1536), bf),
        ((2, 128, 384), bf),
        ((2, 128, 128), bf),
    ]
    rows_peer = [
        ((*shape[:-1], shape[-1] // 2) if 3 <= k <= 8 else shape, dtype)
        for k, (shape, dtype) in enumerate(rows_own)
    ]
    sums = [((4, 8 * t, *tile), bf) for t in SIZES]
    outs = [*sums, ((4, 4, 8, *tile), bf), ((2, 128, 768), f32), ((2, OWN, ATOM), f32)]
    groups = [
        rows_own,
        [*rows_peer, ((256, 768), bf), ((256, 384), bf)],
        [((4, 4, 4 * t, *tile), bf) for t in SIZES],
        sums,
        [
            room
            for t, order in zip(SIZES, ORDERS, strict=True)
            for room in room_shapes(t, order, tile, bf, 1 if order is ORDER_ML else 2)
        ],
        ((4, 4, 16, 8, 128), f32),
        ((4, 4, 8, *tile), bf),
        ((4, 4, 4, *tile), bf),
        ((4, 4, 8, *tile), bf),
        room_shapes(1, ORDER_SM, tile, bf, 0),
        ((4, 256, 768), bf),
        [((128, 768), bf), ((128, 768), bf), ((256, 768), bf), ((256, 768), bf)],
        ((4, 256, 128), bf),
        ((256, 1536), bf),
        ((256, 768), bf),
        outs[-2],
        outs[-1],
        ((REGION, 512), bf),
        ((OWN, ATOM), f32),
        ((REGION, ATOM), bf),
        ((REGION, 2 * ATOM), f32),
        ((OWN, ATOM), f32),
        ((OWN // WQ, 128, WK), f32),
        ((16, 16, 512), f32),
        ((2, 8, 512, 128), bf),
        ((16, 128, 512), bf),
        ((16, 64, 512), bf),
        ((32, 256), f32),
    ]
    spec = [None] * len(in_hbm) + [len(peer_given)] + [None] * len(in_vmem) + [len(SIZES), None, None, None]
    scratch = []
    for group in groups:
        some = group if isinstance(group, list) else [group]
        spec.append(len(some) if isinstance(group, list) else None)
        scratch += [one if not isinstance(one, tuple) else pltpu.VMEM(*one) for one in some]
    spec += [None] * 5
    scratch += [pltpu.SemaphoreType.DMA((n,)) for n in (23, 3, 8, COPIES, COPIES)]
    return pl.pallas_call(
        functools.partial(backward_kernel, spec),
        out_shape=[jax.ShapeDtypeStruct(*o) for o in outs],
        in_specs=hbm(len(in_hbm) + len(peer_given)) + vmem(len(in_vmem)),
        out_specs=hbm(len(outs)),
        scratch_shapes=scratch,
        compiler_params=params(62, collective_id=0, has_side_effects=True),
        name="backward_pass",
    )(*in_hbm, *peer_given, *in_vmem)


class Final(typing.NamedTuple):
    tiles: object
    small: object
    plain: object
    big: object
    mod: object
    bias: object
    heads_in: object
    heads_out: object
    pair: object
    gate_up: object
    down: object
    token_pair: object
    token_bias: object
    plain_out: object
    stage: object
    sems: object
    plain_sems: object


def unpack_kernel(spec, *refs):
    it = iter(refs)
    r = Final(*[next(it) if n is None else [next(it) for _ in range(n)] for n in spec])
    kept = []
    for k, (src, dst) in enumerate(zip(r.plain, r.plain_out, strict=True)):
        kept.append(pltpu.make_async_copy(src, dst, r.plain_sems.at[k]))
        kept[-1].start()

    def out_copy(k):
        kept.append(pltpu.make_async_copy(r.stage[k], r.big[k], r.sems.at[k]))
        kept[-1].start()

    for k in range(2):
        for n in range(24):
            r.stage[k][:, pl.ds(n * 128, 128)] = wide(r.tiles[k][:, pl.ds(3 * n, 3)].reshape(192, 128))
        out_copy(k)
    for n in range(6):
        at = n // 3 * 28 + n % 3 * 9
        r.stage[2][:, pl.ds(n * 128, 128)] = wide(r.tiles[2][:, pl.ds(at, 6)].reshape(384, 128))
        r.stage[3][:, pl.ds(n * 128, 128)] = wide(r.tiles[2][:, pl.ds(at + 6, 3)].reshape(192, 128))
    out_copy(2)
    out_copy(3)
    for n in range(24):
        source = r.tiles[4 - n // 12]
        for part in range(2):
            at = n % 6 * 6 + 3 * part
            tiles = source[at // 9, pl.ds(n % 12 // 6 * 12 + at % 9, 3)].reshape(48, 128)
            r.stage[4][pl.ds(48 * part, 48), pl.ds(n * 128, 128)] = wide(tiles)
    for n in range(6):
        tiles = r.tiles[4][n % 3, pl.ds(n // 3 * 12 + 9, 2)].reshape(32, 128)
        r.stage[5][:, pl.ds(n * 128, 128)] = wide(tiles)
    out_copy(4)
    out_copy(5)

    def block(k):
        return wide(r.small[k // 4, k % 4]).reshape(128, 128)

    for target, first in ((r.mod, 0), (r.heads_in, 4), (r.gate_up, 9)):
        for n in range(4):
            target[:, pl.ds(n * 128, 128)] = block(first + n)
    r.heads_out[...] = block(8)
    r.down[pl.ds(0, 128), :] = block(13)
    r.down[pl.ds(128, 128), :] = block(14)
    rest = block(15)
    r.bias[...] = rest[:4]
    r.pair[...] = rest[8 : 8 + HA, :CP]
    r.token_pair[...] = rest[24:40]
    r.token_bias[...] = rest[40:64]
    for one in kept:
        one.wait()


def unpack(tiles, small, plain):
    f32 = jnp.float32
    big = [((192, 3072), f32), ((192, 3072), f32), ((384, 768), f32), ((192, 768), f32), ((96, 3072), f32)]
    big.append(((32, 768), f32))
    rest = [((128, 512), f32), ((4, 128), f32), ((128, 512), f32), ((128, 128), f32), ((HA, CP), f32)]
    rest += [((128, 512), f32), ((256, 128), f32), ((H, 128), f32), ((24, 128), f32)]
    outs = big + rest + [(one.shape, one.dtype) for one in plain]
    spec = [len(tiles), None, len(plain), len(big)] + [None] * len(rest) + [len(plain), len(big), None, None]
    return pl.pallas_call(
        functools.partial(unpack_kernel, spec),
        out_shape=[jax.ShapeDtypeStruct(*o) for o in outs],
        in_specs=vmem(len(tiles) + 1 + len(plain)),
        out_specs=hbm(len(big)) + vmem(len(rest)) + hbm(len(plain)),
        scratch_shapes=[
            *[pltpu.VMEM(*o) for o in big],
            pltpu.SemaphoreType.DMA((len(big),)),
            pltpu.SemaphoreType.DMA((len(plain),)),
        ],
        compiler_params=params(60),
        name="unpack",
    )(*tiles, small, *plain)


def per_device(
    atoms,
    atom_cond,
    atom_pairs,
    atom_counts,
    tokens,
    token_cond,
    token_pairs,
    cotangent,
    atom_mod,
    atom_mod_bias,
    atom_heads_in,
    atom_heads_out,
    atom_pair_proj,
    atom_gate_up,
    atom_down,
    pool_proj,
    token_mod,
    token_mod_bias,
    token_heads_in,
    token_heads_out,
    token_pair_proj,
    token_gate_up,
    token_down,
):
    given = (token_heads_in, token_gate_up, token_mod, token_down, token_heads_out, pool_proj)
    given = (*given, atoms, atom_cond, token_cond, tokens)
    atom_bias = atom_mod_bias.reshape(4, 128)
    atom_weights = (atom_mod, atom_bias, atom_heads_in, atom_heads_out, atom_gate_up, atom_down)
    turned_pairs = atom_pairs.transpose(0, 2, 1)
    (
        w_pool,
        all_atoms,
        all_atom_cond,
        all_bias,
        pooled,
        output,
        x_turned,
        dkv,
        dqg,
        gated_turned,
        inner_turned,
        dbranch,
        dtrans,
        dgu,
        dgates,
        dx_far,
        dx_own,
        normal,
        squash,
        inverse,
        score_sum,
        *peer_given,
    ) = forward_pass(
        given,
        token_pairs,
        cotangent,
        atom_counts,
        turned_pairs,
        atom_pair_proj.T,
        atom_weights,
        token_mod_bias.reshape(24, 128),
        token_pair_proj.T,
    )
    in_hbm = (x_turned, gated_turned, inner_turned, dkv, dqg, dbranch, dtrans, dgu, dgates, dx_far)
    in_vmem = (dx_own, normal, squash, inverse, cotangent, w_pool, token_cond, pooled)
    in_vmem = (*in_vmem, all_atoms, all_atom_cond, all_bias, atom_counts)
    *tiles, small, grad_tokens, grad_atoms = backward_pass(
        (*in_hbm, score_sum, token_pairs), peer_given, (*in_vmem, *atom_weights, turned_pairs)
    )
    (
        grad_gu,
        grad_in,
        grad_down,
        grad_out,
        grad_mod,
        grad_pool,
        grad_atom_mod,
        grad_atom_bias,
        grad_atom_in,
        grad_atom_out,
        grad_atom_pair,
        grad_atom_gu,
        grad_atom_down,
        grad_token_pair,
        grad_token_bias,
        output,
        grad_tokens,
        grad_atoms,
    ) = unpack(tiles, small, (output, grad_tokens, grad_atoms))
    return (
        output,
        grad_tokens,
        grad_atoms,
        grad_atom_mod,
        grad_atom_bias.reshape(512),
        grad_atom_in,
        grad_atom_out,
        grad_atom_pair.T,
        grad_atom_gu,
        grad_atom_down,
        grad_pool,
        grad_mod,
        grad_token_bias.reshape(3072),
        grad_in,
        grad_out,
        grad_token_pair.T,
        grad_gu,
        grad_down,
    )


def solution(mesh):
    shape = (4, 4, 2, 4) if mesh.devices.size == 128 else (1, 1, 1, mesh.devices.size)
    mesh = Mesh(mesh.devices.reshape(shape), (*DP, "fsdp"))
    in_specs = (
        P(DP, "fsdp", None),
        P(DP, "fsdp", None),
        P("fsdp", None, None),
        P(DP, None),
        P(DP, "fsdp", None),
        P(DP, "fsdp", None),
        P("fsdp", None, None),
        P(DP, "fsdp", None),
        P(),
        P(),
        P(),
        P(),
        P(),
        P(),
        P(),
        P("fsdp", None),
        P("fsdp", None),
        P(),
        P("fsdp", None),
        P("fsdp", None),
        P(),
        P("fsdp", None),
        P("fsdp", None),
    )
    out_specs = (
        P(DP, "fsdp", None),
        P(DP, "fsdp", None),
        P(DP, "fsdp", None),
        P(),
        P(),
        P(),
        P(),
        P(),
        P(),
        P(),
        P("fsdp", None),
        P("fsdp", None),
        P(),
        P("fsdp", None),
        P("fsdp", None),
        P(),
        P("fsdp", None),
        P("fsdp", None),
    )
    return jax.shard_map(
        per_device, mesh=mesh, in_specs=in_specs, out_specs=out_specs, check_vma=False
    )
```

```python
import functools
import math
import types
import typing

import jax
import jax.numpy as jnp
from jax import lax
from jax.experimental import pallas as pl
from jax.experimental.pallas import tpu as pltpu
from jax.sharding import Mesh, PartitionSpec as P

MESH = pl.DeviceIdType.MESH
DP = ("x", "z", "c")
HA = 4
CP = 16
WQ = 32
WK = 128
H = 16

epsilon = 1e-05
masked = -1e30


def dot(left, right):
    return jnp.dot(left, right, preferred_element_type=jnp.float32)


def dot_nt(left, right):
    return lax.dot_general(left, right, (((1,), (1,)), ((), ())), preferred_element_type=jnp.float32)


def dot_tn(left, right):
    return lax.dot_general(left, right, (((0,), (0,)), ((), ())), preferred_element_type=jnp.float32)


def low(value):
    return value.astype(jnp.bfloat16)


def wide(value):
    return value.astype(jnp.float32)


def normalize(hidden):
    center = hidden - jnp.mean(hidden, axis=-1, keepdims=True)
    inverse = lax.rsqrt(jnp.mean(center * center, axis=-1, keepdims=True) + epsilon)
    return center * inverse, inverse


def lane_mask(first, last, width, dtype):
    lane = lax.broadcasted_iota(jnp.int32, (1, width), 1)
    return jnp.where((lane >= first) & (lane < last), 1.0, 0.0).astype(dtype)


def vmem(count):
    return [pl.BlockSpec(memory_space=pltpu.VMEM)] * count


def hbm(count):
    return [pl.BlockSpec(memory_space=pl.ANY)] * count


def params(megabytes, **more):
    return pltpu.CompilerParams(vmem_limit_bytes=megabytes * 1024 * 1024, **more)


HEAD = 48
GROUP = 8
SPAN = HEAD * GROUP


class Whole:
    def __init__(self, ref):
        self.ref = ref

    def __getitem__(self, index):
        some = self.ref[...] if index is Ellipsis else self.ref[:, :, index[1]]
        return some.reshape(-1, some.shape[-1])

    def blocks(self, first, count):
        return self.ref[pl.ds(first, count)].reshape(-1, self.ref.shape[-1])


def token_block(r, me, steps, flush):
    tokens, cond, pooled, cotangent, bias, b_mod = r.tokens, r.tcond, r.pooled, r.cotangent, r.bias, r.b_mod
    w_pool, w_mod, w_in = Whole(r.w_pool), Whole(r.w_mod), Whole(r.w_in)
    w_out, w_gu, w_down = Whole(r.w_out), Whole(r.w_gu), Whole(r.w_down)
    output, dkv, dqg, dbranch, dtrans = r.output, r.dkv, r.dqg, r.dbranch, r.dtrans
    dgu, dgates, dx_own, normal, squash = r.dgu, r.dgates, r.gate_att, r.normal, r.squash
    inverse, probs, gate_att, mixed = r.inverse, r.probs, r.gate_att, r.mixed
    kv, qg, ssum = dkv, dqg, bias
    scale = HEAD ** (-0.5)

    def rows_of(ref, y):
        return ref[y].reshape(256, ref.shape[-1])

    def modulation(c, k):
        part = pl.ds(k * 768, 768)
        bias = wide(b_mod[...])
        bias = jnp.concatenate([bias[i : i + 1] for i in range(6 * k, 6 * k + 6)], axis=1)
        return dot(c, w_mod[:, part]) + bias

    def normed(y, own):
        hidden = wide(rows_of(tokens, y)) + dot(rows_of(pooled, y), w_pool[...])
        c = rows_of(cond, y)
        n, inv = normalize(hidden)
        sq = jax.nn.sigmoid(modulation(c, 0))
        x = low(n * sq + modulation(c, 1))
        kv[y] = low(dot(x, w_in[:, pl.ds(768, 1536)])).reshape(2, 128, 1536)
        turned = x.T
        if own:
            r.x_own[...] = x
            r.x_mine[...] = turned
            output[...] = hidden.reshape(2, 128, 768)
            normal[...] = n
            squash[...] = sq
            inverse[...] = jnp.broadcast_to(inv, inverse.shape)
            gate_att[...] = jax.nn.sigmoid(modulation(c, 2))
            mixed[...] = jax.nn.sigmoid(modulation(c, 3)).reshape(2, 128, 768)
            qg[:, :, pl.ds(0, 768)] = low(dot(x, w_in[:, pl.ds(0, 768)])).reshape(2, 128, 768)
            qg[:, :, pl.ds(768, 768)] = low(dot(x, w_in[:, pl.ds(2304, 768)])).reshape(2, 128, 768)
        r.x_turned[:, pl.ds(pl.multiple_of(y * 256, 256), 256)] = turned

    normed(me, True)
    steps.own_done()

    x = r.x_own[...]
    for k in range(4):
        part = pl.ds(k * 768, 768)
        dgu[:, part] = low(dot(x, w_gu[:, part]))
    steps.transition()
    dy = wide(cotangent[...].reshape(256, 768))
    trans = None
    for k in range(2):
        a = wide(dgu[:, pl.ds(k * 768, 768)])
        b = wide(dgu[:, pl.ds(1536 + k * 768, 768)])
        inner = low(a * jax.nn.sigmoid(a) * b)
        r.inner_turned[pl.ds(k * 768, 768), :] = inner.T
        some = dot(inner, w_down.blocks(2 * k, 2))
        trans = some if trans is None else trans + some
    sgf = mixed[...].reshape(256, 768)
    output[...] += (sgf * trans).reshape(2, 128, 768)
    dgates[:, pl.ds(768, 768)] = low(dy * trans * sgf * (1.0 - sgf))
    dtrans[...] = low(dy * sgf)
    for k in range(2):
        dinner = dot_nt(dtrans[...], w_down.blocks(2 * k, 2))
        a = wide(dgu[:, pl.ds(k * 768, 768)])
        b = wide(dgu[:, pl.ds(1536 + k * 768, 768)])
        sq = jax.nn.sigmoid(a)
        dgu[:, pl.ds(k * 768, 768)] = low(dinner * b * sq * (1.0 + a * (1.0 - sq)))
        dgu[:, pl.ds(1536 + k * 768, 768)] = low(dinner * a * sq)
    flush(r.inner_turned, dtrans)
    steps.swap_gu()
    steps.rows_ready()

    @pl.loop(1, 4)
    def _(k):
        normed(lax.rem(me + k, 4), False)

    flush(r.x_turned)
    steps.weights_gu()
    steps.gu(1)

    def windows():
        for j in range(GROUP):
            first, last = HEAD * j, HEAD * (j + 1)
            t0, t1 = first // 128, (last - 1) // 128 + 1
            yield j, slice(t0 * 128, t1 * 128), first - t0 * 128, last - t0 * 128, range(t0, t1)

    def group_of(ref, s, at):
        return ref[:, s, :, pl.ds(pl.multiple_of(at, 128), SPAN)].reshape(512, SPAN)

    @pl.loop(0, 2)
    def _(s):
        @pl.loop(0, 2)
        def _(half):
            lanes = pl.ds(pl.multiple_of(half * SPAN, 128), SPAN)
            q = qg[s, :, lanes]
            k = group_of(kv, s, half * SPAN)
            v = group_of(kv, s, 768 + half * SPAN)
            tiles = [None] * 3
            for j, span, a, b, covers in windows():
                width = span.stop - span.start
                masked_q = q[:, span] * lane_mask(a, b, width, jnp.bfloat16)
                score = dot_nt(masked_q, k[:, span]) * scale + wide(bias[half * GROUP + j])
                score = jnp.exp(score - jnp.max(score, axis=-1, keepdims=True))
                p = low(score * (1.0 / jnp.sum(score, axis=-1, keepdims=True)))
                probs[s, half * GROUP + j] = p
                o = dot(p, v[:, span]) * lane_mask(a, b, width, jnp.float32)
                for t in covers:
                    piece = o[:, t * 128 - span.start : (t + 1) * 128 - span.start]
                    tiles[t] = piece if tiles[t] is None else tiles[t] + piece
            mixed[s, :, lanes] = jnp.concatenate(tiles, axis=1)

    mix = mixed[...].reshape(256, 768)
    sg = jax.nn.sigmoid(wide(qg[:, :, pl.ds(768, 768)].reshape(256, 768)))
    gated = low(mix * sg)
    r.gated_turned[...] = gated.T
    branch = dot(gated, w_out[...])
    sga = gate_att[...]
    dgates[:, pl.ds(0, 768)] = low(dy * branch * sga * (1.0 - sga))
    dbranch[...] = low(dy * sga)
    output[...] += (sga * branch).reshape(2, 128, 768)
    flush(r.gated_turned, dbranch, output, dgates)
    steps.gu(1)
    ssum[...] = jnp.zeros_like(ssum)
    dgated = dot_nt(dbranch[...], w_out[...])
    dqg[:, :, pl.ds(768, 768)] = low(dgated * mix * sg * (1.0 - sg)).reshape(2, 128, 768)
    mixed[...] = (dgated * sg).reshape(2, 128, 768)

    def attend_back(s, half):
        lanes = pl.ds(pl.multiple_of(half * SPAN, 128), SPAN)
        q = qg[s, :, lanes]
        do = low(mixed[s, :, lanes])
        k = group_of(kv, s, half * SPAN)
        v = group_of(kv, s, 768 + half * SPAN)
        q_turned, do_turned = q.T, do.T
        tiles = [None] * 3
        for j, span, a, b, covers in windows():
            width = span.stop - span.start
            masked_do = do[:, span] * lane_mask(a, b, width, jnp.bfloat16)
            dp = dot_nt(masked_do, v[:, span])
            p_low = probs[s, half * GROUP + j]
            p = wide(p_low)
            ds = low(p * (dp - jnp.sum(p * dp, axis=-1, keepdims=True)))
            ssum[half * GROUP + j] += ds
            head = slice(HEAD * j, HEAD * (j + 1))
            r.turned[0, head] = low(dot(q_turned[head], ds) * scale)
            r.turned[1, head] = low(dot(do_turned[head], p_low))
            dq = dot(ds, k[:, span]) * (lane_mask(a, b, width, jnp.float32) * scale)
            for t in covers:
                piece = dq[:, t * 128 - span.start : (t + 1) * 128 - span.start]
                tiles[t] = piece if tiles[t] is None else tiles[t] + piece
        dqg[s, :, lanes] = low(jnp.concatenate(tiles, axis=1))
        for i in range(2):
            lanes = pl.ds(pl.multiple_of(768 * i + half * SPAN, 128), SPAN)
            dkv[:, s, :, lanes] = r.turned[i].T.reshape(4, 128, SPAN)

    def far_rows(s):
        some = dkv[:, s].reshape(512, 1536)
        for k in range(2):
            weight = r.w_in[pl.ds(2 * k, 2), :, pl.ds(768, 1536)].reshape(384, 1536)
            r.held[s, :, :, pl.ds(k * 384, 384)] = low(dot_nt(some, weight)).reshape(4, 128, 384)

    def finish(s):
        part = pl.ds(s * 128, 128)
        dx = dx_own[part, :] + wide(r.held[s, me])
        n, sq = normal[part, :], squash[part, :]
        dn = dx * sq
        r.dmod[part, pl.ds(0, 768)] = low(dx * n * sq * (1.0 - sq))
        r.dmod[part, pl.ds(768, 768)] = low(dx)
        grad = wide(cotangent[s]) + inverse[part, :1] * (
            dn - jnp.mean(dn, axis=-1, keepdims=True) - n * jnp.mean(dn * n, axis=-1, keepdims=True)
        )
        r.grad_tokens[s] = grad
        r.dmid[part, :] = low(grad)
        r.spread[me, part] = low(dot_nt(low(grad), w_pool[...]))

    for some in steps.scatter:
        some[3]()

    @pl.loop(0, 2)
    def _(s):
        @pl.loop(0, 2)
        def _(half):
            attend_back(s, half)

        far_rows(s)

        @pl.when(s == 0)
        def _():
            steps.scatter[0][0]()
            steps.gu(2)

    steps.scatter[1][0]()
    steps.scores()
    steps.gu(2)
    steps.scatter[0][1]()
    flush(dqg, dkv)
    dx = dot_nt(dgu[...], w_gu[...])
    dx = dx + dot_nt(dqg[:, :, pl.ds(0, 768)].reshape(256, 768), w_in[:, pl.ds(0, 768)])
    dx_own[...] = dx + dot_nt(dqg[:, :, pl.ds(768, 768)].reshape(256, 768), w_in[:, pl.ds(2304, 768)])
    steps.scatter[1][1]()
    steps.gu(3)
    steps.scatter[0][2]()
    finish(0)
    steps.spread[0][0]()
    steps.pairs(0, 2)
    steps.gu(2)
    steps.pairs(2, 4)
    steps.scatter[1][2]()
    finish(1)
    steps.spread[1][0]()
    steps.gu(2)
    flush(r.dmod, r.dmid, r.grad_tokens, r.pair_sum)
    for some in steps.spread:
        some[1]()
    steps.gu(1)
    flush(r.spread, r.gu_out)


class Steps(typing.NamedTuple):
    own_done: object
    transition: object
    rows_ready: object
    swap_gu: object
    weights_gu: object
    gu: object
    scatter: object
    scores: object
    spread: object
    pairs: object


RIM = (WK - WQ) // 2
ATOM = 128
OWN = 160
REACH = 112
REGION = OWN + 2 * REACH
A_HEAD = ATOM // HA


def atom_modulation(c, w_mod, b_mod, k):
    return dot(c, w_mod[:, pl.ds(k * ATOM, ATOM)]) + wide(b_mod[...])[k : k + 1]


def stacked_heads(rows, dtype):
    return jnp.concatenate(
        [rows * lane_mask(A_HEAD * h, A_HEAD * (h + 1), ATOM, dtype) for h in range(HA)], axis=0
    )


def unstacked_heads(rows):
    total = None
    for h in range(HA):
        own = rows[WQ * h : WQ * (h + 1)] * lane_mask(A_HEAD * h, A_HEAD * (h + 1), ATOM, jnp.float32)
        total = own if total is None else total + own
    return total


def window_probs(stacked, keys, bias, first_key, count):
    place = first_key + lax.broadcasted_iota(jnp.int32, (1, WK), 1)
    valid = (place >= 0) & (place < count)
    scores = dot_nt(stacked, keys) * A_HEAD ** (-0.5) + wide(bias)
    scores = jnp.where(valid, scores, masked)
    scores = jnp.exp(scores - jnp.max(scores, axis=-1, keepdims=True))
    return scores * (1.0 / jnp.sum(scores, axis=-1, keepdims=True))


def token_ranges(counts):
    wide_counts = jnp.concatenate([wide(counts[...]), jnp.zeros((6, 512), jnp.float32)], axis=0)
    row = lax.broadcasted_iota(jnp.int32, (512, 512), 0)
    lane = lax.broadcasted_iota(jnp.int32, (512, 512), 1)
    before = low(jnp.where(lane < row, 1.0, 0.0))
    until = low(jnp.where(lane <= row, 1.0, 0.0))
    some = low(wide_counts)
    return dot_nt(before, some), dot_nt(until, some), dot_nt(some, before), dot_nt(some, until)


def atom_row_bias(w_pair, pairs, bias):
    w = wide(w_pair[...])
    stacked = jnp.concatenate([jnp.broadcast_to(w[h : h + 1], (WQ, CP)) for h in range(HA)], axis=0)
    row = lax.broadcasted_iota(jnp.int32, (CP, 512), 0)
    lane = lax.broadcasted_iota(jnp.int32, (CP, 512), 1)
    spread = dot(low(stacked), low(jnp.where(row == lax.rem(lane, CP), 1.0, 0.0)))
    weight = low(spread * same_query())
    for b in range(OWN // WQ):
        some = pairs[pl.ds(b * WQ, WQ)].reshape(WQ * CP, WK)
        bias[b + 2] = low(dot(weight, some))


def same_query():
    row = lax.broadcasted_iota(jnp.int32, (128, 512), 0)
    lane = lax.broadcasted_iota(jnp.int32, (128, 512), 1)
    return jnp.where(lax.rem(row, WQ) == lax.div(lane, CP), 1.0, 0.0)


def atom_forward(s, me, atoms, cond, bias, w_mod, b_mod, w_in, w_out, w_gu, w_down, out, packed, mixed):
    region = pl.ds(REACH - RIM, OWN + 2 * RIM)
    own = slice(RIM, RIM + OWN)
    hidden = wide(atoms[s, region, :])
    c = cond[s, region, :]
    normal, _ = normalize(hidden)
    squash = jax.nn.sigmoid(atom_modulation(c, w_mod, b_mod, 0))
    x = low(normal * squash + atom_modulation(c, w_mod, b_mod, 1))
    packed[...] = low(dot(x, w_in[...]))
    results = []
    for w in range(OWN // WQ):
        at = w * WQ
        q = packed[pl.ds(at + RIM, WQ), pl.ds(0, ATOM)]
        k = packed[pl.ds(at, WK), pl.ds(ATOM, ATOM)]
        v = packed[pl.ds(at, WK), pl.ds(2 * ATOM, ATOM)]
        stacked = stacked_heads(q, jnp.bfloat16)
        p = window_probs(stacked, k, bias[w + 2], me * OWN + at - RIM, 4 * OWN)
        results.append(unstacked_heads(dot(low(p), v)))
    for w, result in enumerate(results):
        mixed[pl.ds(w * WQ, WQ), :] = result
    hidden, c, x = hidden[own], c[own], x[own]
    gate = jax.nn.sigmoid(wide(packed[pl.ds(RIM, OWN), pl.ds(3 * ATOM, ATOM)]))
    branch = dot(low(mixed[...] * gate), w_out[...])
    both = low(dot(x, w_gu[...]))
    a, b = wide(both[:, :256]), wide(both[:, 256:])
    trans = dot(low(a * jax.nn.sigmoid(a) * b), w_down[...])
    total = hidden + jax.nn.sigmoid(atom_modulation(c, w_mod, b_mod, 2)) * branch
    out[me, s] = low(total + jax.nn.sigmoid(atom_modulation(c, w_mod, b_mod, 3)) * trans)


def pool_atoms(s, rows, ranges, pooled):
    total = 4 * OWN
    place = wide(lax.broadcasted_iota(jnp.int32, (1, total), 1))
    start, end = ranges[0][:, s : s + 1], ranges[1][:, s : s + 1]
    member = jnp.where((place >= start) & (place < end), 1.0, 0.0)
    sums = dot(low(member), rows[:, s].reshape(total, ATOM)) / (end - start)
    pooled[:, s] = low(sums).reshape(4, 128, ATOM)


def atom_backward(
    s,
    me,
    atoms,
    cond,
    bias,
    grad_pooled,
    ranges,
    w_mod,
    b_mod,
    w_in,
    w_out,
    w_gu,
    w_down,
    grad_atoms,
    small,
    ssum,
    packed,
    mixed,
    grad_mixed,
    dkv,
    dq,
):
    total = 640
    first = me * OWN - REACH
    own = slice(REACH, REACH + OWN)
    scale = A_HEAD ** (-0.5)

    def add_small(block, value):
        for k in range(value.shape[0] // 128):
            for n in range(value.shape[1] // 128):
                tile = value[k * 128 : (k + 1) * 128, n * 128 : (n + 1) * 128]
                at = block + k + n
                small[at // 4, at % 4] += tile.reshape(16, 8, 128)

    hidden = wide(atoms[s])
    c = cond[s]
    normal, inverse = normalize(hidden)
    squash = jax.nn.sigmoid(atom_modulation(c, w_mod, b_mod, 0))
    x = low(normal * squash + atom_modulation(c, w_mod, b_mod, 1))
    packed[...] = low(dot(x, w_in[...]))

    place = wide(first + lax.broadcasted_iota(jnp.int32, (REGION, 1), 0))
    start, end = ranges[2][s : s + 1], ranges[3][s : s + 1]
    member = jnp.where((place >= start) & (place < end), 1.0, 0.0)
    owner = jnp.sum(member * (end - start), axis=-1, keepdims=True)
    dy = dot(low(member), grad_pooled[:, pl.ds(s * 128, 128)].reshape(512, ATOM)) / jnp.maximum(owner, 1.0)
    sga = jax.nn.sigmoid(atom_modulation(c, w_mod, b_mod, 2))
    dbranch = low(dy * sga)
    dgated = dot_nt(dbranch, w_out[...])
    gate = jax.nn.sigmoid(wide(packed[:, pl.ds(3 * ATOM, ATOM)]))
    grad_mixed[...] = low(dgated * gate)
    dkv[...] = jnp.zeros_like(dkv)

    def window(w, own):
        at = pl.multiple_of(w * WQ, WQ)
        query = pl.ds(at + RIM, WQ)
        q = stacked_heads(packed[query, pl.ds(0, ATOM)], jnp.bfloat16)
        k = packed[pl.ds(at, WK), pl.ds(ATOM, ATOM)]
        v = packed[pl.ds(at, WK), pl.ds(2 * ATOM, ATOM)]
        do = stacked_heads(grad_mixed[query, :], jnp.bfloat16)
        p = window_probs(q, k, bias[w], first + at, total)
        dp = dot_nt(do, v)
        ds = low(p * (dp - jnp.sum(p * dp, axis=-1, keepdims=True)))
        out = [dot_tn(ds, q) * scale, dot_tn(low(p), do)]
        if own:
            out += [unstacked_heads(dot(low(p), v)), unstacked_heads(dot(ds, k)) * scale, wide(ds)]
        return out

    for group in ((0, 1, 7, 8), (2, 3, 4, 5, 6)):
        results = {w: window(w, 2 <= w < 7) for w in group}
        for w, result in results.items():
            keys = pl.ds(w * WQ, WK)
            dkv[keys, pl.ds(0, ATOM)] += result[0]
            dkv[keys, pl.ds(ATOM, ATOM)] += result[1]
            if 2 <= w < 7:
                rows = pl.ds((w - 2) * WQ, WQ)
                mixed[rows, :] = result[2]
                dq[rows, :] = result[3]
                ssum[w - 2] += result[4]

    x, c, hidden, normal, inverse = x[own], c[own], hidden[own], normal[own], inverse[own]
    squash, dy, sga, dbranch, dgated = squash[own], dy[own], sga[own], dbranch[own], dgated[own]
    gate = gate[own]
    gated = low(mixed[...] * gate)
    branch = dot(gated, w_out[...])
    both = low(dot(x, w_gu[...]))
    a, b = wide(both[:, :256]), wide(both[:, 256:])
    sq = jax.nn.sigmoid(a)
    inner = low(a * sq * b)
    trans = dot(inner, w_down[...])
    sgf = jax.nn.sigmoid(atom_modulation(c, w_mod, b_mod, 3))
    dga = dy * branch * sga * (1.0 - sga)
    dgf = dy * trans * sgf * (1.0 - sgf)
    dtrans = low(dy * sgf)
    dinner = dot_nt(dtrans, w_down[...])
    dgu = low(jnp.concatenate([dinner * b * sq * (1.0 + a * (1.0 - sq)), dinner * a * sq], axis=1))
    dg = dgated * mixed[...] * gate * (1.0 - gate)
    dpacked = low(jnp.concatenate([dq[...], dkv[pl.ds(REACH, OWN), :], dg], axis=1))
    dx = dot_nt(dpacked, w_in[...]) + dot_nt(dgu, w_gu[...])
    dn = dx * squash
    dscale = dx * normal * squash * (1.0 - squash)
    dmod = low(jnp.concatenate([dscale, dx, dga, dgf], axis=1))
    grad_atoms[s] = dy + inverse * (
        dn
        - jnp.mean(dn, axis=-1, keepdims=True)
        - normal * jnp.mean(dn * normal, axis=-1, keepdims=True)
    )
    add_small(0, dot_tn(c, dmod))
    add_small(4, dot_tn(x, dpacked))
    add_small(8, dot_tn(gated, dbranch))
    add_small(9, dot_tn(x, dgu))
    add_small(13, dot_tn(inner, dtrans))
    sums = jnp.sum(wide(dmod), axis=0, keepdims=True)
    for n in range(4):
        small[3, 3, 0, pl.ds(n, 1), :] += sums[:, n * 128 : (n + 1) * 128]


RING = 4


class Ring:
    def __init__(self, axis):
        self.axis = axis
        self.me = lax.axis_index(axis)
        self.up = lax.rem(self.me + 1, RING)
        self.down = lax.rem(self.me + 3, RING)
        self.far = lax.rem(self.me + 2, RING)


class Copies:
    def __init__(self, send, recv):
        self.send, self.recv, self.used = send, recv, 0

    def make(self, axis, place, src, dst):
        made = pltpu.make_async_remote_copy(
            src_ref=src,
            dst_ref=dst,
            send_sem=self.send.at[self.used],
            recv_sem=self.recv.at[self.used],
            device_id={axis: place},
            device_id_type=MESH,
        )
        self.used += 1
        return made

    def start(self, *what):
        made = self.make(*what)
        made.start()
        return made


def meet(rings, core=None):
    barrier = pltpu.get_barrier_semaphore()
    for ring in rings:
        for place in (ring.up, ring.down, ring.far):
            pl.semaphore_signal(barrier, 1, device_id={ring.axis: place}, device_id_type=MESH)
    if core is not None:
        pl.semaphore_signal(barrier, 1, device_id={"c": 1 - core}, device_id_type=MESH)
    pl.semaphore_wait(barrier, 3 * len(rings) + (core is not None))


def run_stages(parts):
    for k in range(max(len(stages) for stages in parts)):
        for stages in parts:
            if k < len(stages):
                stages[k]()


def nothing():
    pass


def add_into(target, others):
    def one(index):
        total = target[index]
        if len(others) > 1:
            total = total.astype(jnp.float32)
        for other in others:
            total = total + other[index].astype(total.dtype)
        target[index] = total.astype(target.dtype)

    lead = target.shape[:-3]

    def nest(index):
        if len(index) == len(lead):
            one(index or Ellipsis)
            return

        @pl.loop(0, lead[len(index)])
        def _(i):
            nest((*index, i))

    nest(())


def scatter_stages(ring, copies, held, first, second):
    half = held.shape[1] // 2
    low_part, high_part = pl.ds(0, half), pl.ds(half, held.shape[1] - half)
    r1, r2 = first
    r3, r4 = second
    up, down, far = ring.up, ring.down, ring.far
    made = {}

    def send(k, src, dst, to):
        made[k] = copies.start(ring.axis, to, src, dst)

    def prepare():
        made[1] = copies.make(ring.axis, up, held.at[far, low_part], r1)
        made[2] = copies.make(ring.axis, down, held.at[far, high_part], r2)
        made[3] = copies.make(ring.axis, up, held.at[up, high_part], r3.at[high_part])
        made[4] = copies.make(ring.axis, down, held.at[down, low_part], r4.at[low_part])

    def begin():
        for k in (1, 2, 3, 4):
            made[k].start()

    def middle():
        made[1].wait_recv()
        add_into(held.at[up, low_part], [r1])
        send(5, held.at[up, low_part], r3.at[low_part], up)
        made[2].wait_recv()
        add_into(held.at[down, high_part], [r2])
        send(6, held.at[down, high_part], r4.at[high_part], down)

    def end():
        for k in (3, 4, 5, 6):
            made[k].wait_recv()
        add_into(held.at[ring.me], [r3, r4])
        for k in range(1, 7):
            made[k].wait_send()

    return [begin, middle, end, prepare]


def spread_stages(ring, copies, view, parts, landed=None):
    low_parts, high_parts = parts
    made = {}

    def send(k, place, some, to):
        made[k] = [copies.start(ring.axis, to, view(place, p), view(place, p)) for p in some]

    def arrived(*what):
        for k, place, some in what:
            for one in made[k]:
                one.wait_recv()
            tell(place, some)

    def tell(place, some):
        if landed is not None:
            for p in some:
                landed(place, p)

    def begin():
        send(0, ring.me, low_parts, ring.up)
        send(1, ring.me, high_parts, ring.down)
        send(2, ring.me, high_parts, ring.up)
        send(3, ring.me, low_parts, ring.down)
        tell(ring.me, (*low_parts, *high_parts))

    def middle():
        arrived((0, ring.down, low_parts))
        send(4, ring.down, low_parts, ring.up)
        arrived((1, ring.up, high_parts))
        send(5, ring.up, high_parts, ring.down)

    def end():
        arrived((2, ring.down, high_parts), (3, ring.up, low_parts))
        arrived((4, ring.far, low_parts), (5, ring.far, high_parts))
        for some in made.values():
            for one in some:
                one.wait_send()

    return [begin, middle, end]


def direct_stages(ring, copies, *views):
    made = []

    def begin():
        for place in (ring.up, ring.down, ring.far):
            for view in views:
                made.append(copies.start(ring.axis, place, view(ring.me), view(ring.me)))

    def end():
        for one in made:
            one.wait()

    return [begin, end]


class Region:
    def __init__(self, t, x, z, y, done):
        self.t, self.done = t, {ring.axis: ring.me for ring in done}
        self.x, self.z, self.y = x, z, y

    def index(self, ring, place, half):
        known = {**self.done, ring.axis: place}
        split, out = half, []
        for one in (self.y, self.z):
            if one.axis in known:
                out.append(known[one.axis])
            elif split < 2:
                out.append(pl.ds(2 * split, 2))
                split = 2
            else:
                out.append(pl.ds(0, 4))
        inner = self.x.axis in known
        start, count = (known[self.x.axis] * self.t, self.t) if inner else (0, 4 * self.t)
        if split < 2:
            cut = count // 2
            start, count = (start, cut) if split == 0 else (start + cut, count - cut)
        return (*out, pl.ds(start, count))

    def shapes(self, ring):
        known = {*self.done, ring.axis}
        lead = [4 for one in (self.y, self.z) if one.axis not in known]
        whole = (*lead, self.t if self.x.axis in known else 4 * self.t)
        cut = whole[0] // 2
        return (cut, *whole[1:]), (whole[0] - cut, *whole[1:]), whole, whole


def region_stages(copies, ring, region, part, rooms):
    r1, r2, r3, r4 = rooms
    up, down, far = ring.up, ring.down, ring.far
    cut = r1.shape[0]
    halves = (pl.ds(0, cut), pl.ds(cut, r3.shape[0] - cut))
    made = {}

    def piece(place, half=2):
        return part.at[region.index(ring, place, half)]

    def prepare(k, src, dst, to):
        made[k] = copies.make(ring.axis, to, src, dst)

    prepare(1, piece(far, 0), r1, up)
    prepare(2, piece(far, 1), r2, down)
    prepare(3, piece(up, 1), r3.at[halves[1]], up)
    prepare(4, piece(down, 0), r4.at[halves[0]], down)
    prepare(5, piece(up, 0), r3.at[halves[0]], up)
    prepare(6, piece(down, 1), r4.at[halves[1]], down)

    def begin():
        for k in (1, 2, 3, 4):
            made[k].start()

    def middle():
        made[1].wait_recv()
        add_into(piece(up, 0), [r1])
        made[5].start()
        made[2].wait_recv()
        add_into(piece(down, 1), [r2])
        made[6].start()

    def end():
        for k in (3, 4, 5, 6):
            made[k].wait_recv()
        add_into(piece(ring.me), [r3, r4])
        for k in range(1, 7):
            made[k].wait_send()

    return [begin, middle, end]


def direct_region_stages(copies, ring, region, part, rooms):
    made = [
        copies.make(ring.axis, place, part.at[region.index(ring, place, 2)], room)
        for place, room in zip((ring.up, ring.down, ring.far), rooms, strict=False)
    ]

    def begin():
        for one in made:
            one.start()

    def end():
        for one in made:
            one.wait_recv()
        add_into(part.at[region.index(ring, ring.me, 2)], list(rooms[:3]))
        for one in made:
            one.wait_send()

    return [begin, end]


def part_stages(copies, core, x, z, y, order, t, part, out, rooms, direct=2):
    stages, done = [], []
    for k, ring in enumerate(order):
        region = Region(t, x, z, y, done)
        kind = direct_region_stages if k >= direct else region_stages
        stages += kind(copies, ring, region, part, rooms[4 * k : 4 * k + 4])
        done.append(ring)
    base = core * (4 * t)
    halves = (((0, 2),), ((2, 2),))
    pair = (((0, 2 * t),), ((2 * t, 2 * t),))

    def keep():
        out[z.me, pl.ds(base + x.me * t, t)] = part[y.me, z.me, pl.ds(x.me * t, t)]

    stages.append(keep)
    if order[0] is z:
        stages += direct_stages(x, copies, lambda place: out.at[z.me, pl.ds(base + place * t, t)])
        if direct < 2:
            return stages + direct_stages(z, copies, lambda place: out.at[place, pl.ds(base, 4 * t)])
        return stages + spread_stages(
            z, copies, lambda place, p: out.at[place, pl.ds(base + p[0], p[1])], pair
        )
    stages += direct_stages(z, copies, lambda place: out.at[place, pl.ds(base + x.me * t, t)])
    if direct < 2:
        return stages + direct_stages(x, copies, lambda place: out.at[:, pl.ds(base + place * t, t)])
    return stages + spread_stages(
        x, copies, lambda place, p: out.at[pl.ds(*p), pl.ds(base + place * t, t)], halves
    )


def swap_stages(copies, core, refs):
    made = []

    def begin():
        for ref in refs:
            made.append(copies.start("c", 1 - core, ref, ref))

    def end():
        for one in made:
            one.wait()

    return [begin, end]


def room_shapes(t, order, tile, dtype, direct=2):
    place = {axis: types.SimpleNamespace(axis=axis, me=0) for axis in order}
    x, z, y = [place[axis] for axis in ("x", "z", "fsdp")]
    shapes, done = [], []
    for axis in order:
        rooms = Region(t, x, z, y, done).shapes(place[axis])
        if order.index(axis) >= direct:
            rooms = (rooms[2],) * 3 + ((1,),)
        shapes += [pltpu.VMEM((*shape, *tile), dtype) for shape in rooms]
        done.append(place[axis])
    return shapes


COPIES = 96
ORDER_GU = ("x", "z", "fsdp")
ORDER_IN = ("z", "fsdp", "x")
ORDER_DO = ("x", "z", "fsdp")
ORDER_ME = ("fsdp", "x", "z")
ORDER_ML = ("x", "fsdp", "z")
ORDER_SM = ("fsdp", "x", "z")
ORDERS = (ORDER_IN, ORDER_DO, ORDER_ME, ORDER_ML)
SIZES = (9, 7, 3, 3)


IN, GU, MOD, DOWN, OUT, POOL = MATRICES = range(6)


class Front(typing.NamedTuple):
    given: object
    pairs: object
    cotangent: object
    counts: object
    atom_pairs: object
    aw_pair: object
    aw_mod: object
    ab_mod: object
    aw_in: object
    aw_out: object
    aw_gu: object
    aw_down: object
    b_mod: object
    w_pair: object
    results: object
    peer: object
    atoms: object
    acond: object
    abias: object
    pooled: object
    output: object
    x_turned: object
    dkv: object
    dqg: object
    gated_turned: object
    inner_turned: object
    dbranch: object
    dtrans: object
    dgates: object
    dmod: object
    dmid: object
    grad_tokens: object
    spread: object
    pair_sum: object
    gu_out: object
    w_in: object
    w_gu: object
    w_mod: object
    w_down: object
    w_out: object
    w_pool: object
    atom_out: object
    tcond: object
    tokens: object
    x_own: object
    x_mine: object
    pair_weight: object
    bias: object
    pair_rows: object
    pair_bufs: object
    packed: object
    amixed: object
    dgu: object
    probs: object
    turned: object
    gate_att: object
    mixed: object
    normal: object
    squash: object
    inverse: object
    scores_peer: object
    held: object
    scatter_rooms: object
    gu_part: object
    gu_rooms: object
    x_peer: object
    dgu_peer: object
    load: object
    pair_sems: object
    flush_sems: object
    send: object
    recv: object


FIRST_RESULT = 16


def columns(start, width):
    return pl.ds(pl.multiple_of(start, 128), width)


def rows(start, count):
    return pl.ds(pl.multiple_of(start, 16), count)


def matrix_stages(copies, full, core, x, y, z):
    moved = {name: [] for name in MATRICES}

    def block(far):
        return lax.rem(y.me + far, RING)

    def to_core(name, one):
        moved[name].append(copies.start("c", 1 - core, one, one))

    def in_y(name, first, cut, count, span, last=False):
        def view(place, p):
            return full[name].at[place, rows(first + p[0], p[1]), span]

        def landed(place, p):
            if place is not y.me:
                to_core(name, view(place, p))

        return spread_stages(y, copies, view, ([(0, cut)], [(cut, count - cut)]), landed if last else None)

    def in_plane(ring, name, place_of, count, width, last):
        def view(place, p):
            far, row, height, column, breadth = p
            first, start = place_of(place)
            return full[name].at[block(far), rows(first + row, height), columns(start + column, breadth)]

        if count >= 32:
            cut = (count // 2 + 15) // 16 * 16
            halves = (0, cut, 0, width), (cut, count - cut, 0, width)
        else:
            cut = width // 256 * 128
            halves = (0, count, 0, cut), (0, count, cut, width - cut)
        parts = [(1, 0, count, 0, width), (2, *halves[0])], [(3, 0, count, 0, width), (2, *halves[1])]
        return spread_stages(ring, copies, view, parts, (lambda place, p: to_core(name, view(place, p))) if last else None)

    def in_both(name, first_ring):
        ref, mid = full[name], core * 1536
        pieces = direct_stages(
            y,
            copies,
            lambda place: ref.at[place, rows(32 * x.me, 32), columns(mid + z.me * 384, 384)],
            lambda place: ref.at[place, rows(128 + 16 * x.me, 16), columns(mid + z.me * 384, 384)],
        )

        def x_then_z(base, height):
            one = in_plane(x, name, lambda p: (base + height * p, mid + z.me * 384), height, 384, False)
            return one, in_plane(z, name, lambda p: (base, mid + p * 384), 4 * height, 384, True)

        def z_then_x(base, height):
            one = in_plane(z, name, lambda p: (base + height * x.me, mid + p * 384), height, 384, False)
            return one, in_plane(x, name, lambda p: (base + height * p, mid), height, 1536, True)

        if first_ring is x:
            big, little = x_then_z(0, 32), z_then_x(128, 16)
        else:
            big, little = z_then_x(0, 32), x_then_z(128, 16)
        return [pieces, *([both_steps(p, q) for p, q in zip(a, b, strict=True)] for a, b in zip(big, little, strict=True))]

    def both_steps(p, q):
        def run():
            p()
            q()

        return run

    steps = {
        IN: in_both(IN, x),
        GU: in_both(GU, z),
        MOD: [
            in_y(MOD, 0, 48, 96, columns(core * 1536 + x.me * 384, 384)),
            in_plane(x, MOD, lambda place: (0, core * 1536 + place * 384), 96, 384, True),
        ],
        DOWN: [
            in_y(DOWN, 96 * z.me, 48, 96, columns(core * 384, 384)),
            in_plane(z, DOWN, lambda place: (96 * place, core * 384), 96, 384, True),
        ],
        OUT: [
            in_y(OUT, 48 * x.me, 32, 48, columns(core * 384, 384)),
            in_plane(x, OUT, lambda place: (48 * place, core * 384), 48, 384, True),
        ],
        POOL: [in_y(POOL, 0, 16, 32, columns(core * 384, 384), True)],
    }
    return steps, moved


def forward_kernel(spec, *refs):
    it = iter(refs)
    r = Front(*[next(it) if n is None else [next(it) for _ in range(n)] for n in spec])
    core = lax.axis_index("c")
    x, z, y = Ring("x"), Ring("z"), Ring("fsdp")
    me = y.me
    copies = Copies(r.send, r.recv)

    matrices = (r.w_in, r.w_gu, r.w_mod, r.w_down, r.w_out, r.w_pool)
    middle = pl.ds(REACH, OWN)
    targets = [ref.at[me] for ref in matrices] + [r.atoms.at[:, middle], r.acond.at[:, middle]]
    targets += [r.tcond.at[me], r.tokens.at[me]]
    loads = []
    for k, target in enumerate(targets):
        loads.append(pltpu.make_async_copy(r.given[k], target, r.load.at[k]))
        loads[-1].start()

    def fetch(chunk, slot):
        src = r.pairs.at[pl.ds(pl.multiple_of(core * 64 + chunk * 8, 8), 8)]
        return pltpu.make_async_copy(src, r.pair_bufs.at[slot], r.pair_sems.at[slot])

    for slot in range(2):
        fetch(slot, slot).start()
    meet((x, z, y), core)

    jobs, moved = matrix_stages(copies, matrices, core, x, y, z)
    late = []
    for ref in (r.tcond, r.tokens):
        parts = ([pl.ds(0, 1)], [pl.ds(1, 1)])
        late.append(spread_stages(y, copies, lambda place, p, ref=ref: ref.at[place, p], parts))
    atom_out = direct_stages(y, copies, lambda place: r.atom_out.at[place])
    halo = []

    def halo_begin():
        for ref in (r.atoms, r.acond):
            first, last = ref.at[:, pl.ds(REACH, REACH)], ref.at[:, pl.ds(OWN, REACH)]
            halo.append(copies.start("fsdp", y.up, last, ref.at[:, pl.ds(0, REACH)]))
            halo.append(copies.start("fsdp", y.down, first, ref.at[:, pl.ds(REACH + OWN, REACH)]))
        halo.append(copies.start("fsdp", y.up, r.abias.at[pl.ds(5, 2)], r.abias.at[pl.ds(0, 2)]))
        halo.append(copies.start("fsdp", y.down, r.abias.at[pl.ds(2, 2)], r.abias.at[pl.ds(7, 2)]))

    def halo_end():
        for one in halo:
            one.wait()

    def step(kind, stage, *which):
        for name in which:
            jobs[name][kind][stage]()

    def cores(name):
        for one in moved[name]:
            one.wait()

    def bias_steps(first, last):
        pair_rows, pair_bufs = r.pair_rows, r.pair_bufs

        @pl.loop(first, last)
        def _(i):
            for slot in range(2):
                fetch(2 * i + slot, slot).wait()
                for q in range(0, 8, 2):
                    both = jnp.concatenate([pair_bufs[slot, q], pair_bufs[slot, q + 1]], axis=1)
                    value = dot_nt(r.pair_weight[...], both)
                    pair_rows[:, 8 * slot + q, :] = value[:16]
                    pair_rows[:, 8 * slot + q + 1, :] = value[16:]

                @pl.when(i < 3)
                def _():
                    fetch(2 * i + 2 + slot, slot).start()

            r.bias[:, rows(core * 64 + i * 16, 16), :] = low(pair_rows[...])

    flushed, staged = [], r[FIRST_RESULT:]

    def flush(*which):
        for ref in which:
            k = next(i for i, one in enumerate(staged) if one is ref)
            some = ref.at[me] if ref is r.pooled else ref
            flushed.append(pltpu.make_async_copy(some, r.results[k], r.flush_sems.at[k]))
            flushed[-1].start()
            hand_over(ref)

    theirs = (r.x_turned, r.gated_turned, r.inner_turned, r.dkv, r.dqg, r.dbranch, r.dtrans, r.dgates)
    theirs = (*theirs, None, None, r.dmod, r.dmid)

    def hand_over(ref):
        for k, one in enumerate(theirs):
            if one is ref:
                width = ref.shape[-1] // 2
                lead = (slice(None),) * (len(ref.shape) - 1)
                some = ref if k < 3 else ref.at[(*lead, columns((1 - core) * width, width))]
                flushed.append(copies.start("c", 1 - core, some, r.peer[k]))

    def first_step(*which):
        for name in which:
            loads[name].wait()
            step(0, 0, name)

    def plane_step(*which):
        for name in which:
            step(0, 2, name)
            step(1, 0, name)

    first_step(IN)
    atom_row_bias(r.aw_pair, r.atom_pairs, r.abias)
    for k in (6, 7):
        loads[k].wait()
    halo_begin()
    first_step(MOD, GU, POOL, OUT, DOWN)
    step(0, 1, IN)
    step(1, 0, IN)
    for k in (8, 9):
        loads[k].wait()
    flushed.append(copies.start("c", 1 - core, r.tcond.at[me], r.peer[8]))
    turned = wide(r.w_pair[...])
    blank = jnp.zeros_like(turned)
    r.pair_weight[pl.ds(0, 16), :] = low(jnp.concatenate([turned, blank], axis=1))
    r.pair_weight[pl.ds(16, 16), :] = low(jnp.concatenate([blank, turned], axis=1))
    ranges = token_ranges(r.counts)
    step(1, 1, IN)
    halo_end()
    atom_weights = (r.aw_mod, r.ab_mod, r.aw_in, r.aw_out, r.aw_gu, r.aw_down)
    atom_room = (r.atom_out, r.packed, r.amixed)
    atom_forward(0, me, r.atoms, r.acond, r.abias, *atom_weights, *atom_room)
    step(1, 2, IN)
    step(2, 0, IN)
    step(0, 1, MOD)
    step(0, 1, GU)
    step(1, 0, GU)
    atom_forward(1, me, r.atoms, r.acond, r.abias, *atom_weights, *atom_room)
    atom_out[0]()
    flush(r.atoms, r.acond, r.abias)
    step(0, 1, POOL, OUT, DOWN)
    plane_step(MOD)
    for steps in late:
        steps[0]()
    bias_steps(0, 2)
    step(1, 1, GU)
    step(2, 1, IN)
    step(0, 2, POOL)
    plane_step(OUT, DOWN)
    step(1, 1, MOD)
    step(1, 2, GU)
    step(2, 0, GU)
    bias_steps(2, 4)
    half_bias = r.bias.at[:, rows(core * 64, 64), :]
    bias_moved = copies.start("c", 1 - core, half_bias, half_bias)
    atom_out[1]()
    for s in range(2):
        pool_atoms(s, r.atom_out, ranges, r.pooled)
    flush(r.pooled)
    flushed.append(copies.start("c", 1 - core, r.pooled.at[me], r.peer[9]))
    step(1, 2, MOD)
    step(1, 1, OUT, DOWN)
    step(2, 2, IN)
    for name in (POOL, MOD, IN):
        cores(name)

    def own_done():
        for steps in late:
            steps[1]()
        step(2, 1, GU)
        step(1, 2, OUT, DOWN)
        step(2, 2, GU)
        cores(GU)

    def transition():
        cores(DOWN)

    def rows_ready():
        for steps in late:
            steps[2]()
        cores(OUT)
        bias_moved.wait()
        for slot in range(2):
            fetch(slot, slot).start()

    scores_moved = []

    def scores():
        theirs = r.bias.at[:, rows((1 - core) * 64, 64)]
        scores_moved.append(copies.start("c", 1 - core, theirs, r.scores_peer))

    def pair_steps(first, last):
        if first == 0:
            r.pair_sum[...] = jnp.zeros_like(r.pair_sum)
            scores_moved[0].wait()
        for i in range(first, last):
            span = pl.ds(16 * i, 16)
            own_part = wide(r.bias[:, rows(core * 64 + 16 * i, 16)])
            r.pair_rows[...] = own_part + wide(r.scores_peer[:, span])
            total = jnp.zeros(r.pair_sum.shape, jnp.float32)
            for slot in range(2):
                fetch(2 * i + slot, slot).wait()
                for q in range(0, 8, 2):
                    at = 8 * slot + q
                    both = jnp.concatenate([r.pair_bufs[slot, q], r.pair_bufs[slot, q + 1]], axis=1)
                    left = jnp.concatenate([r.pair_rows[:, at, :], r.pair_rows[:, at + 1, :]], axis=0)
                    total = total + dot(low(left), both)
                if i < 3:
                    fetch(2 * i + 2 + slot, slot).start()
            r.pair_sum[...] += total

    gu_moved = []

    def swap_gu():
        gu_moved.append(copies.start("c", 1 - core, r.x_mine, r.x_peer))
        some = r.dgu.at[:, columns((1 - core) * 1536, 1536)]
        gu_moved.append(copies.start("c", 1 - core, some, r.dgu_peer))

    def weights_gu():
        for one in gu_moved:
            one.wait()
        for k in range(2):
            own = r.dgu[:, columns(core * 1536 + k * 768, 768)]
            value = dot(r.x_mine[...], own)
            value = low(value + dot(r.x_peer[...], r.dgu_peer[:, pl.ds(k * 768, 768)]))
            for n in range(6):
                tiles = value[:, n * 128 : (n + 1) * 128].reshape(4, 4, 3, 16, 128)
                r.gu_part[:, :, pl.ds((6 * k + n) * 3, 3)] = tiles

    gu_steps = part_stages(copies, core, x, z, y, (x, z, y), 9, r.gu_part, r.gu_out, r.gu_rooms, 1)
    gu_steps += swap_stages(copies, core, [r.gu_out.at[:, pl.ds(core * 36, 36)]])

    def gu(count):
        for _ in range(count):
            gu_steps.pop(0)()

    scatter, spread = [], []
    for s in range(2):
        rooms = r.scatter_rooms[4 * s : 4 * s + 4]
        scatter.append(scatter_stages(y, copies, r.held.at[s], rooms[:2], rooms[2:]))
        part = pl.ds(s * 128, 128)
        spread.append(direct_stages(y, copies, lambda place, part=part: r.spread.at[place, part]))
    token_block(
        r, me, Steps(own_done, transition, rows_ready, swap_gu, weights_gu, gu, scatter, scores, spread, pair_steps), flush
    )
    for one in flushed:
        one.wait()
    assert not gu_steps
    assert copies.used == FRONT_COPIES


FRONT_COPIES = 360


def forward_pass(given, pairs, cotangent, counts, atom_pairs, aw_pair, atom_weights, b_mod, w_pair):
    bf, f32 = jnp.bfloat16, jnp.float32
    full = [((4, *a.shape), a.dtype) for a in given]
    results = (
        ((2, REGION, ATOM), bf),
        ((2, REGION, ATOM), bf),
        ((9, 128, 128), bf),
        ((4, 2, 128, 128), bf),
        ((2, 128, 768), f32),
        ((768, 1024), bf),
        ((4, 2, 128, 1536), bf),
        ((2, 128, 1536), bf),
        ((768, 256), bf),
        ((1536, 256), bf),
        ((256, 768), bf),
        ((256, 768), bf),
        ((256, 1536), bf),
        ((256, 1536), bf),
        ((256, 768), bf),
        ((2, 128, 768), f32),
        ((4, 256, 128), bf),
        ((32, 256), f32),
        ((4, 72, 16, 128), bf),
    )
    peer = (
        ((768, 1024), bf),
        ((768, 256), bf),
        ((1536, 256), bf),
        ((4, 2, 128, 768), bf),
        ((2, 128, 768), bf),
        ((256, 384), bf),
        ((256, 384), bf),
        ((256, 768), bf),
        ((2, 128, 384), bf),
        ((2, 128, 128), bf),
        ((256, 768), bf),
        ((256, 384), bf),
    )
    rooms = [((64, 768), bf), ((64, 768), bf), ((128, 768), bf), ((128, 768), bf)]
    outs = (*results[:3], ((2, 128, 128), bf), *results[4:], *peer)
    scratch = (
        *results,
        *full[:6],
        full[6],
        *full[8:],
        ((256, 768), bf),
        ((768, 256), bf),
        ((32, 256), bf),
        ((16, 128, 512), bf),
        ((16, 16, 512), f32),
        ((2, 8, 512, 128), bf),
        ((OWN + 2 * RIM, 512), bf),
        ((OWN, ATOM), f32),
        ((256, 3072), bf),
        ((2, 16, 128, 512), bf),
        ((2, SPAN, 512), bf),
        ((256, 768), f32),
        ((2, 128, 768), f32),
        ((256, 768), f32),
        ((256, 768), f32),
        ((256, 128), f32),
        ((16, 64, 512), bf),
        ((2, 4, 128, 768), bf),
        *rooms,
        *rooms,
        ((4, 4, 36, 16, 128), bf),
    )
    gu_rooms = room_shapes(9, ORDER_GU, (16, 128), bf, 1)
    last = [pltpu.VMEM((768, 256), bf), pltpu.VMEM((256, 1536), bf)]
    semaphores = [
        pltpu.SemaphoreType.DMA((n,)) for n in (10, 2, len(results), FRONT_COPIES, FRONT_COPIES)
    ]
    spec = [10] + [None] * 13 + [len(results), len(peer)]
    spec += [None] * (len(scratch) - 9) + [8, None, len(gu_rooms), None, None] + [None] * len(semaphores)
    return pl.pallas_call(
        functools.partial(forward_kernel, spec),
        out_shape=[jax.ShapeDtypeStruct(*o) for o in outs],
        in_specs=hbm(11) + vmem(12),
        out_specs=hbm(len(outs)),
        scratch_shapes=[pltpu.VMEM(*s) for s in scratch] + gu_rooms + last + semaphores,
        compiler_params=params(62, collective_id=1, has_side_effects=True),
        name="forward_pass",
    )(*given, pairs, cotangent, counts, atom_pairs, aw_pair, *atom_weights, b_mod, w_pair)


class Back(typing.NamedTuple):
    given: object
    peer_given: object
    pooled_grad: object
    pair_sum: object
    atoms: object
    acond: object
    abias: object
    counts: object
    aw_mod: object
    ab_mod: object
    aw_in: object
    aw_out: object
    aw_gu: object
    aw_down: object
    atom_pairs: object
    tiles: object
    small_sums: object
    grad_atoms_out: object
    own: object
    peer: object
    parts: object
    outs: object
    rooms: object
    small: object
    small_low: object
    small_peer: object
    small_out: object
    small_rooms: object
    grad_atoms: object
    packed: object
    mixed: object
    grad_mixed: object
    akv: object
    aq: object
    ascores: object
    load: object
    keep: object
    send: object
    recv: object


class Rows(typing.NamedTuple):
    x: object
    gated: object
    inner: object
    dkv: object
    dqg: object
    dbranch: object
    dtrans: object
    dgates: object
    cond: object
    pooled: object
    dmod: object
    dmid: object


def backward_kernel(spec, *refs):
    it = iter(refs)
    r = Back(*[next(it) if n is None else [next(it) for _ in range(n)] for n in spec])
    core = lax.axis_index("c")
    x, z, y = Ring("x"), Ring("z"), Ring("fsdp")
    me = y.me
    copies = Copies(r.send, r.recv)
    own, peer = Rows(*r.own), Rows(*r.peer)
    span_of = {ref.shape[-1]: columns(core * (ref.shape[-1] // 2), ref.shape[-1] // 2) for ref in own[3:8]}
    loads = {}
    for n, k in enumerate((0, 4, 3, 2, 6, 1, 5, 8, 7, 10, 9, 11)):
        loads[k] = [
            pltpu.make_async_copy(r.given[k], own[k], r.load.at[2 * n]),
            pltpu.make_async_copy(r.peer_given[k], peer[k], r.load.at[2 * n + 1]),
        ]
        for one in loads[k]:
            one.start()
    r.small[...] = jnp.zeros_like(r.small)
    meet((x, z, y), core)

    def ready(*which):
        for k in which:
            for one in loads.pop(k, ()):
                one.wait()

    mine = columns(me * 256, 256)
    part_in, part_do, part_me, part_ml = r.parts

    def place_columns(part, value, first, row_tiles, step, offset=0):
        value = low(value)
        for n in range(value.shape[1] // 128):
            tiles = value[:, n * 128 : (n + 1) * 128].reshape(4, 4, row_tiles, 16, 128)
            part[:, :, pl.ds((first + n) * step + offset, row_tiles)] = tiles

    def flat(ref):
        return ref[...].reshape(-1, ref.shape[-1])

    def mine_of(ref):
        some = ref[(*(slice(None),) * (len(ref.shape) - 1), span_of[ref.shape[-1]])]
        return some.reshape(-1, some.shape[-1])

    def weights_do():
        ready(1, 2, 5, 6)
        value = dot(own.inner[...], mine_of(own.dtrans)) + dot(peer.inner[...], peer.dtrans[...])
        place_columns(part_do, value, 0, 6, 9)
        value = dot(own.gated[...], mine_of(own.dbranch)) + dot(peer.gated[...], peer.dbranch[...])
        place_columns(part_do, value, 0, 3, 9, 6)

    def weights_in():
        ready(0, 3, 4)
        value = dot(own.x[:, mine], mine_of(own.dqg)) + dot(peer.x[:, mine], flat(peer.dqg))
        place_columns(part_in, value, 6 * core, 3, 3)
        value = dot(own.x[...], mine_of(own.dkv)) + dot(peer.x[...], flat(peer.dkv))
        place_columns(part_in, value, 6 * (1 - core), 3, 3)

    def place_mod(part, value):
        value = low(value)
        for n in range(6):
            tiles = value[:, n * 128 : (n + 1) * 128].reshape(4, 6, 16, 128)
            for k in range(2):
                at = 6 * n + 3 * k
                part[:, at // 9, pl.ds(at % 9, 3)] = tiles[:, 3 * k : 3 * k + 3]

    def weights_me():
        ready(8, 7)
        own_turned, peer_turned = flat(own.cond).T, flat(peer.cond).T
        place_mod(part_me, dot(own_turned, mine_of(own.dgates)) + dot(peer_turned, peer.dgates[...]))

    def weights_ml():
        ready(8, 10, 9, 11)
        own_turned, peer_turned = flat(own.cond).T, flat(peer.cond).T
        place_mod(part_ml, dot(own_turned, mine_of(own.dmod)) + dot(peer_turned, peer.dmod[...]))
        left = (flat(own.pooled).T, flat(peer.pooled).T)
        value = low(dot(left[0], mine_of(own.dmid)) + dot(left[1], peer.dmid[...]))
        for n in range(3):
            part_ml[:, n, pl.ds(9, 2)] = value[:, n * 128 : (n + 1) * 128].reshape(4, 2, 16, 128)

    stages = []
    rings = {"x": x, "z": z, "fsdp": y}
    for k, order in enumerate(ORDERS):
        order = [rings[axis] for axis in order]
        rooms = r.rooms[12 * k : 12 * k + 12]
        some = part_stages(copies, core, x, z, y, order, SIZES[k], r.parts[k], r.outs[k], rooms, 1)
        stages.append(some)
        span = pl.ds(core * 4 * SIZES[k], 4 * SIZES[k])
        stages[-1] += swap_stages(copies, core, [r.outs[k].at[:, span]])
    s_in, s_do, s_me, s_ml = stages

    kept = []

    def out_copy(src, dst):
        kept.append(pltpu.make_async_copy(src, dst, r.keep.at[len(kept)]))
        kept[-1].start()

    def go(*which):
        for some in which:
            some.pop(0)()

    room = (r.packed, r.mixed, r.grad_mixed, r.akv, r.aq)
    weights = (r.aw_mod, r.ab_mod, r.aw_in, r.aw_out, r.aw_gu, r.aw_down)
    ranges = token_ranges(r.counts)
    r.ascores[...] = jnp.zeros_like(r.ascores)

    def atoms_of(s):
        rows_in = (r.atoms, r.acond, r.abias, r.pooled_grad, ranges)
        atom_backward(s, me, *rows_in, *weights, r.grad_atoms, r.small, r.ascores, *room)

    weights_in()
    go(s_in)
    atoms_of(0)
    weights_do()
    go(s_do)
    atoms_of(1)
    out_copy(r.grad_atoms, r.grad_atoms_out)
    r.small[3, 3, 1] = atom_pair_grad(r.ascores, r.atom_pairs)
    total = r.pair_sum[:16, :128] + r.pair_sum[16:, 128:]
    r.small[3, 3, pl.ds(3, 2)] = total.reshape(2, 8, 128)
    ready(10, 7)
    sums = jnp.sum(wide(own.dmod[...]), axis=0, keepdims=True)
    sums = jnp.concatenate([sums, jnp.sum(wide(own.dgates[...]), axis=0, keepdims=True)], axis=1)
    for n in range(24):
        r.small[3, 3, 5 + n // 8, pl.ds(n % 8, 1), :] = sums[:, n * 128 : (n + 1) * 128]

    order = [rings[axis] for axis in ORDER_SM]
    r.small_low[...] = low(r.small[...].reshape(4, 4, 8, 16, 128))
    theirs, ours = r.small_low.at[:, :, pl.ds((1 - core) * 4, 4)], r.small_low.at[:, :, pl.ds(core * 4, 4)]
    small_moved = []

    def small_begin():
        small_moved.append(copies.start("c", 1 - core, theirs, r.small_peer))

    def small_merge():
        small_moved[0].wait()
        add_into(ours, [r.small_peer])

    s_small = [small_begin, small_merge]
    s_small += part_stages(
        copies, core, x, z, y, order, 1, ours, r.small_out.at[me], r.small_rooms, 0
    )
    span = pl.ds(core * 4, 4)
    s_small += direct_stages(y, copies, lambda place: r.small_out.at[place, :, span])
    s_small += swap_stages(copies, core, [r.small_out.at[:, :, span]])
    go(s_small, s_in)
    weights_ml()
    go(s_small, s_small, s_ml)
    weights_me()
    go(s_me, s_do, s_small, s_small, s_in, s_in, s_small, s_small)
    go(s_do, s_do, s_ml, s_me, s_small, s_small, s_small, s_ml, s_ml, s_in, s_in)
    for k, some in enumerate(stages):
        some.append(lambda k=k: out_copy(r.outs[k], r.tiles[k]))
    s_small.append(lambda: out_copy(r.small_out, r.small_sums))
    run_stages([s_small, s_ml, s_in, s_do, s_me])
    for one in kept:
        one.wait()
    assert copies.used == COPIES


def atom_pair_grad(scores, pairs):
    total = jnp.zeros((128, 512), jnp.float32)
    for b in range(OWN // WQ):
        some = pairs[pl.ds(b * WQ, WQ)].reshape(WQ * CP, WK)
        total = total + dot_nt(low(scores[b]), some)
    total = total * same_query()
    heads = [jnp.sum(total[h * WQ : (h + 1) * WQ], axis=0, keepdims=True) for h in range(HA)]
    heads = jnp.concatenate([*heads, jnp.zeros((8 - HA, 512), jnp.float32)], axis=0)
    row = lax.broadcasted_iota(jnp.int32, (512, 128), 0)
    lane = lax.broadcasted_iota(jnp.int32, (512, 128), 1)
    pick = low(jnp.where(lax.rem(row, CP) == lane, 1.0, 0.0))
    return dot(low(heads), pick)


def backward_pass(given, peer_given, in_vmem):
    bf, f32 = jnp.bfloat16, jnp.float32
    tile = (16, 128)
    rows_own = [
        ((768, 1024), bf),
        ((768, 256), bf),
        ((1536, 256), bf),
        ((4, 2, 128, 1536), bf),
        ((2, 128, 1536), bf),
        ((256, 768), bf),
        ((256, 768), bf),
        ((256, 1536), bf),
        ((2, 128, 384), bf),
        ((2, 128, 128), bf),
        ((256, 1536), bf),
        ((256, 768), bf),
    ]
    rows_peer = [
        ((*shape[:-1], shape[-1] // 2) if 3 <= k <= 7 or k > 9 else shape, dtype)
        for k, (shape, dtype) in enumerate(rows_own)
    ]
    sums = [((4, 8 * t, *tile), bf) for t in SIZES]
    outs = [*sums, ((4, 4, 8, *tile), bf), ((2, OWN, ATOM), f32)]
    groups = [
        rows_own,
        rows_peer,
        [((4, 4, 4 * t, *tile), bf) for t in SIZES],
        sums,
        [
            room
            for t, order in zip(SIZES, ORDERS, strict=True)
            for room in room_shapes(t, order, tile, bf, 1)
        ],
        ((4, 4, 16, 8, 128), f32),
        ((4, 4, 8, *tile), bf),
        ((4, 4, 4, *tile), bf),
        ((4, 4, 8, *tile), bf),
        room_shapes(1, ORDER_SM, tile, bf, 0),
        outs[-1],
        ((REGION, 512), bf),
        ((OWN, ATOM), f32),
        ((REGION, ATOM), bf),
        ((REGION, 2 * ATOM), f32),
        ((OWN, ATOM), f32),
        ((OWN // WQ, 128, WK), f32),
    ]
    spec = [len(given), len(peer_given)] + [None] * len(in_vmem) + [len(SIZES), None, None]
    scratch = []
    for group in groups:
        some = group if isinstance(group, list) else [group]
        spec.append(len(some) if isinstance(group, list) else None)
        scratch += [one if not isinstance(one, tuple) else pltpu.VMEM(*one) for one in some]
    spec += [None] * 4
    scratch += [pltpu.SemaphoreType.DMA((n,)) for n in (24, 8, COPIES, COPIES)]
    return pl.pallas_call(
        functools.partial(backward_kernel, spec),
        out_shape=[jax.ShapeDtypeStruct(*o) for o in outs],
        in_specs=hbm(len(given) + len(peer_given)) + vmem(len(in_vmem)),
        out_specs=hbm(len(outs)),
        scratch_shapes=scratch,
        compiler_params=params(62, collective_id=0, has_side_effects=True),
        name="backward_pass",
    )(*given, *peer_given, *in_vmem)


class Final(typing.NamedTuple):
    tiles: object
    small: object
    plain: object
    big: object
    mod: object
    bias: object
    heads_in: object
    heads_out: object
    pair: object
    gate_up: object
    down: object
    token_pair: object
    token_bias: object
    plain_out: object
    stage: object
    sems: object
    plain_sems: object


def unpack_kernel(spec, *refs):
    it = iter(refs)
    r = Final(*[next(it) if n is None else [next(it) for _ in range(n)] for n in spec])
    kept = []
    for k, (src, dst) in enumerate(zip(r.plain, r.plain_out, strict=True)):
        kept.append(pltpu.make_async_copy(src, dst, r.plain_sems.at[k]))
        kept[-1].start()

    def out_copy(k):
        kept.append(pltpu.make_async_copy(r.stage[k], r.big[k], r.sems.at[k]))
        kept[-1].start()

    for k in range(2):
        for n in range(24):
            r.stage[k][:, pl.ds(n * 128, 128)] = wide(r.tiles[k][:, pl.ds(3 * n, 3)].reshape(192, 128))
        out_copy(k)
    for n in range(6):
        at = n // 3 * 28 + n % 3 * 9
        r.stage[2][:, pl.ds(n * 128, 128)] = wide(r.tiles[2][:, pl.ds(at, 6)].reshape(384, 128))
        r.stage[3][:, pl.ds(n * 128, 128)] = wide(r.tiles[2][:, pl.ds(at + 6, 3)].reshape(192, 128))
    out_copy(2)
    out_copy(3)
    for n in range(24):
        source = r.tiles[4 - n // 12]
        for part in range(2):
            at = n % 6 * 6 + 3 * part
            tiles = source[at // 9, pl.ds(n % 12 // 6 * 12 + at % 9, 3)].reshape(48, 128)
            r.stage[4][pl.ds(48 * part, 48), pl.ds(n * 128, 128)] = wide(tiles)
    for n in range(6):
        tiles = r.tiles[4][n % 3, pl.ds(n // 3 * 12 + 9, 2)].reshape(32, 128)
        r.stage[5][:, pl.ds(n * 128, 128)] = wide(tiles)
    out_copy(4)
    out_copy(5)

    def block(k):
        return wide(r.small[k // 4, k % 4]).reshape(128, 128)

    for target, first in ((r.mod, 0), (r.heads_in, 4), (r.gate_up, 9)):
        for n in range(4):
            target[:, pl.ds(n * 128, 128)] = block(first + n)
    r.heads_out[...] = block(8)
    r.down[pl.ds(0, 128), :] = block(13)
    r.down[pl.ds(128, 128), :] = block(14)
    rest = block(15)
    r.bias[...] = rest[:4]
    r.pair[...] = rest[8 : 8 + HA, :CP]
    r.token_pair[...] = rest[24:40]
    r.token_bias[...] = rest[40:64]
    for one in kept:
        one.wait()


def unpack(tiles, small, plain):
    f32 = jnp.float32
    big = [((192, 3072), f32), ((192, 3072), f32), ((384, 768), f32), ((192, 768), f32), ((96, 3072), f32)]
    big.append(((32, 768), f32))
    rest = [((128, 512), f32), ((4, 128), f32), ((128, 512), f32), ((128, 128), f32), ((HA, CP), f32)]
    rest += [((128, 512), f32), ((256, 128), f32), ((H, 128), f32), ((24, 128), f32)]
    outs = big + rest + [(one.shape, one.dtype) for one in plain]
    spec = [len(tiles), None, len(plain), len(big)] + [None] * len(rest) + [len(plain), len(big), None, None]
    return pl.pallas_call(
        functools.partial(unpack_kernel, spec),
        out_shape=[jax.ShapeDtypeStruct(*o) for o in outs],
        in_specs=vmem(len(tiles) + 1 + len(plain)),
        out_specs=hbm(len(big)) + vmem(len(rest)) + hbm(len(plain)),
        scratch_shapes=[
            *[pltpu.VMEM(*o) for o in big],
            pltpu.SemaphoreType.DMA((len(big),)),
            pltpu.SemaphoreType.DMA((len(plain),)),
        ],
        compiler_params=params(60),
        name="unpack",
    )(*tiles, small, *plain)


def per_device(
    atoms,
    atom_cond,
    atom_pairs,
    atom_counts,
    tokens,
    token_cond,
    token_pairs,
    cotangent,
    atom_mod,
    atom_mod_bias,
    atom_heads_in,
    atom_heads_out,
    atom_pair_proj,
    atom_gate_up,
    atom_down,
    pool_proj,
    token_mod,
    token_mod_bias,
    token_heads_in,
    token_heads_out,
    token_pair_proj,
    token_gate_up,
    token_down,
):
    given = (token_heads_in, token_gate_up, token_mod, token_down, token_heads_out, pool_proj)
    given = (*given, atoms, atom_cond, token_cond, tokens)
    atom_bias = atom_mod_bias.reshape(4, 128)
    atom_weights = (atom_mod, atom_bias, atom_heads_in, atom_heads_out, atom_gate_up, atom_down)
    turned_pairs = atom_pairs.transpose(0, 2, 1)
    (
        all_atoms,
        all_atom_cond,
        all_bias,
        pooled,
        output,
        x_turned,
        dkv,
        dqg,
        gated_turned,
        inner_turned,
        dbranch,
        dtrans,
        dgates,
        dmod,
        dmid,
        grad_tokens,
        grad_pooled,
        pair_sum,
        gate_up_tiles,
        *peer_given,
    ) = forward_pass(
        given,
        token_pairs,
        cotangent,
        atom_counts,
        turned_pairs,
        atom_pair_proj.T,
        atom_weights,
        token_mod_bias.reshape(24, 128),
        token_pair_proj.T,
    )
    own = (x_turned, gated_turned, inner_turned, dkv, dqg, dbranch, dtrans, dgates, token_cond, pooled)
    in_vmem = (grad_pooled, pair_sum, all_atoms, all_atom_cond, all_bias, atom_counts)
    *tiles, small, grad_atoms = backward_pass(
        (*own, dmod, dmid), peer_given, (*in_vmem, *atom_weights, turned_pairs)
    )
    (
        grad_gu,
        grad_in,
        grad_down,
        grad_out,
        grad_mod,
        grad_pool,
        grad_atom_mod,
        grad_atom_bias,
        grad_atom_in,
        grad_atom_out,
        grad_atom_pair,
        grad_atom_gu,
        grad_atom_down,
        grad_token_pair,
        grad_token_bias,
        output,
        grad_tokens,
        grad_atoms,
    ) = unpack((gate_up_tiles, *tiles), small, (output, grad_tokens, grad_atoms))
    return (
        output,
        grad_tokens,
        grad_atoms,
        grad_atom_mod,
        grad_atom_bias.reshape(512),
        grad_atom_in,
        grad_atom_out,
        grad_atom_pair.T,
        grad_atom_gu,
        grad_atom_down,
        grad_pool,
        grad_mod,
        grad_token_bias.reshape(3072),
        grad_in,
        grad_out,
        grad_token_pair.T,
        grad_gu,
        grad_down,
    )


def solution(mesh):
    shape = (4, 4, 2, 4) if mesh.devices.size == 128 else (1, 1, 1, mesh.devices.size)
    mesh = Mesh(mesh.devices.reshape(shape), (*DP, "fsdp"))
    in_specs = (
        P(DP, "fsdp", None),
        P(DP, "fsdp", None),
        P("fsdp", None, None),
        P(DP, None),
        P(DP, "fsdp", None),
        P(DP, "fsdp", None),
        P("fsdp", None, None),
        P(DP, "fsdp", None),
        P(),
        P(),
        P(),
        P(),
        P(),
        P(),
        P(),
        P("fsdp", None),
        P("fsdp", None),
        P(),
        P("fsdp", None),
        P("fsdp", None),
        P(),
        P("fsdp", None),
        P("fsdp", None),
    )
    out_specs = (
        P(DP, "fsdp", None),
        P(DP, "fsdp", None),
        P(DP, "fsdp", None),
        P(),
        P(),
        P(),
        P(),
        P(),
        P(),
        P(),
        P("fsdp", None),
        P("fsdp", None),
        P(),
        P("fsdp", None),
        P("fsdp", None),
        P(),
        P("fsdp", None),
        P("fsdp", None),
    )
    return jax.shard_map(
        per_device, mesh=mesh, in_specs=in_specs, out_specs=out_specs, check_vma=False
    )
```

```python
import functools
import math
import types
import typing

import jax
import jax.numpy as jnp
from jax import lax
from jax.experimental import pallas as pl
from jax.experimental.pallas import tpu as pltpu
from jax.sharding import Mesh, PartitionSpec as P

MESH = pl.DeviceIdType.MESH
DP = ("x", "z", "c")
HA = 4
CP = 16
WQ = 32
WK = 128
H = 16

epsilon = 1e-05
masked = -1e30


def dot(left, right):
    return jnp.dot(left, right, preferred_element_type=jnp.float32)


def dot_nt(left, right):
    return lax.dot_general(left, right, (((1,), (1,)), ((), ())), preferred_element_type=jnp.float32)


def dot_tn(left, right):
    return lax.dot_general(left, right, (((0,), (0,)), ((), ())), preferred_element_type=jnp.float32)


def dot_both(left, right, other_left, other_right):
    return dot(jnp.concatenate([left, other_left], axis=1), jnp.concatenate([right, other_right], axis=0))


def low(value):
    return value.astype(jnp.bfloat16)


def wide(value):
    return value.astype(jnp.float32)


def normalize(hidden):
    center = hidden - jnp.mean(hidden, axis=-1, keepdims=True)
    inverse = lax.rsqrt(jnp.mean(center * center, axis=-1, keepdims=True) + epsilon)
    return center * inverse, inverse


def lane_mask(first, last, width, dtype):
    lane = lax.broadcasted_iota(jnp.int32, (1, width), 1)
    return jnp.where((lane >= first) & (lane < last), 1.0, 0.0).astype(dtype)


def vmem(count):
    return [pl.BlockSpec(memory_space=pltpu.VMEM)] * count


def hbm(count):
    return [pl.BlockSpec(memory_space=pl.ANY)] * count


def params(megabytes, **more):
    return pltpu.CompilerParams(vmem_limit_bytes=megabytes * 1024 * 1024, **more)


HEAD = 48
GROUP = 8
SPAN = HEAD * GROUP


class Whole:
    def __init__(self, ref):
        self.ref = ref

    def __getitem__(self, index):
        some = self.ref[...] if index is Ellipsis else self.ref[:, :, index[1]]
        return some.reshape(-1, some.shape[-1])

    def blocks(self, first, count):
        return self.ref[pl.ds(first, count)].reshape(-1, self.ref.shape[-1])


def token_block(r, me, steps, flush):
    tokens, cond, pooled, cotangent, bias, b_mod = r.tokens, r.tcond, r.pooled, r.cotangent, r.bias, r.b_mod
    w_pool, w_mod, w_in = Whole(r.w_pool), Whole(r.w_mod), Whole(r.w_in)
    w_out, w_gu, w_down = Whole(r.w_out), Whole(r.w_gu), Whole(r.w_down)
    output, dkv, dqg, dbranch, dtrans = r.output, r.dkv, r.dqg, r.dbranch, r.dtrans
    dgu, dgates, dx_own, normal, squash = r.dgu, r.dgates, r.gate_att, r.normal, r.squash
    inverse, probs, gate_att, mixed = r.inverse, r.probs, r.gate_att, r.mixed
    kv, qg, ssum = dkv, dqg, bias
    scale = HEAD ** (-0.5)

    def rows_of(ref, y):
        return ref[y].reshape(256, ref.shape[-1])

    def modulation(c, k):
        part = pl.ds(k * 768, 768)
        bias = wide(b_mod[...])
        bias = jnp.concatenate([bias[i : i + 1] for i in range(6 * k, 6 * k + 6)], axis=1)
        return dot(c, w_mod[:, part]) + bias

    def normed(y, own):
        hidden = wide(rows_of(tokens, y)) + dot(rows_of(pooled, y), w_pool[...])
        c = rows_of(cond, y)
        scales, shifts, parts = modulation(c, 0), modulation(c, 1), []
        for at in range(0, 256, 32):
            part = slice(at, at + 32)
            n, inv = normalize(hidden[part])
            sq = jax.nn.sigmoid(scales[part])
            parts.append(low(n * sq + shifts[part]))
            if own:
                normal[pl.ds(at, 32), :] = n
                squash[pl.ds(at, 32), :] = sq
                inverse[pl.ds(at, 32), :] = jnp.broadcast_to(inv, (32, 128))
        x = jnp.concatenate(parts, axis=0)
        kv[y] = low(dot(x, w_in[:, pl.ds(768, 1536)])).reshape(2, 128, 1536)
        turned = x.T
        if own:
            r.x_own[...] = x
            r.x_mine[...] = turned
            output[...] = hidden.reshape(2, 128, 768)
            gate_att[...] = jax.nn.sigmoid(modulation(c, 2))
            mixed[...] = jax.nn.sigmoid(modulation(c, 3)).reshape(2, 128, 768)
            qg[:, :, pl.ds(0, 768)] = low(dot(x, w_in[:, pl.ds(0, 768)])).reshape(2, 128, 768)
            qg[:, :, pl.ds(768, 768)] = low(dot(x, w_in[:, pl.ds(2304, 768)])).reshape(2, 128, 768)
        r.x_turned[:, pl.ds(pl.multiple_of(y * 256, 256), 256)] = turned

    normed(me, True)
    steps.own_done()

    x = r.x_own[...]
    for k in range(4):
        part = pl.ds(k * 768, 768)
        dgu[:, part] = low(dot(x, w_gu[:, part]))
    steps.transition()
    dy = wide(cotangent[...].reshape(256, 768))
    trans = None
    for k in range(2):
        parts = []
        for at in range(0, 256, 32):
            a = wide(dgu[pl.ds(at, 32), pl.ds(k * 768, 768)])
            b = wide(dgu[pl.ds(at, 32), pl.ds(1536 + k * 768, 768)])
            parts.append(low(a * jax.nn.sigmoid(a) * b))
        inner = jnp.concatenate(parts, axis=0)
        r.inner_turned[pl.ds(k * 768, 768), :] = inner.T
        some = dot(inner, w_down.blocks(2 * k, 2))
        trans = some if trans is None else trans + some
    sgf = mixed[...].reshape(256, 768)
    output[...] += (sgf * trans).reshape(2, 128, 768)
    dgates[:, pl.ds(768, 768)] = low(dy * trans * sgf * (1.0 - sgf))
    dtrans[...] = low(dy * sgf)
    for k in range(2):
        dinner = dot_nt(dtrans[...], w_down.blocks(2 * k, 2))
        for at in range(0, 256, 32):
            part, some = pl.ds(at, 32), dinner[at : at + 32]
            a = wide(dgu[part, pl.ds(k * 768, 768)])
            b = wide(dgu[part, pl.ds(1536 + k * 768, 768)])
            sq = jax.nn.sigmoid(a)
            dgu[part, pl.ds(k * 768, 768)] = low(some * b * sq * (1.0 + a * (1.0 - sq)))
            dgu[part, pl.ds(1536 + k * 768, 768)] = low(some * a * sq)
    flush(r.inner_turned, dtrans)
    steps.swap_gu()
    steps.rows_ready()

    @pl.loop(1, 4)
    def _(k):
        normed(lax.rem(me + k, 4), False)

    flush(r.x_turned)
    steps.weights_gu()
    steps.gu(1)

    def windows():
        for j in range(GROUP):
            first, last = HEAD * j, HEAD * (j + 1)
            t0, t1 = first // 128, (last - 1) // 128 + 1
            yield j, slice(t0 * 128, t1 * 128), first - t0 * 128, last - t0 * 128, range(t0, t1)

    def group_of(ref, s, at):
        return ref[:, s, :, pl.ds(pl.multiple_of(at, 128), SPAN)].reshape(512, SPAN)

    @pl.loop(0, 2)
    def _(s):
        @pl.loop(0, 2)
        def _(half):
            lanes = pl.ds(pl.multiple_of(half * SPAN, 128), SPAN)
            q = qg[s, :, lanes]
            k = group_of(kv, s, half * SPAN)
            v = group_of(kv, s, 768 + half * SPAN)
            tiles = [None] * 3
            for j, span, a, b, covers in windows():
                width = span.stop - span.start
                masked_q = q[:, span] * lane_mask(a, b, width, jnp.bfloat16)
                scores, parts = dot_nt(masked_q, k[:, span]), []
                for at in range(0, 128, 32):
                    score = scores[at : at + 32] * scale + wide(bias[half * GROUP + j, pl.ds(at, 32)])
                    score = jnp.exp(score - jnp.max(score, axis=-1, keepdims=True))
                    parts.append(low(score * (1.0 / jnp.sum(score, axis=-1, keepdims=True))))
                p = jnp.concatenate(parts, axis=0)
                probs[s, half * GROUP + j] = p
                o = dot(p, v[:, span]) * lane_mask(a, b, width, jnp.float32)
                for t in covers:
                    piece = o[:, t * 128 - span.start : (t + 1) * 128 - span.start]
                    tiles[t] = piece if tiles[t] is None else tiles[t] + piece
            mixed[s, :, lanes] = jnp.concatenate(tiles, axis=1)

    mix = mixed[...].reshape(256, 768)
    sg = jax.nn.sigmoid(wide(qg[:, :, pl.ds(768, 768)].reshape(256, 768)))
    gated = low(mix * sg)
    r.gated_turned[...] = gated.T
    branch = dot(gated, w_out[...])
    sga = gate_att[...]
    dgates[:, pl.ds(0, 768)] = low(dy * branch * sga * (1.0 - sga))
    dbranch[...] = low(dy * sga)
    output[...] += (sga * branch).reshape(2, 128, 768)
    flush(r.gated_turned, dbranch, output, dgates)
    steps.gu(1)
    ssum[...] = jnp.zeros_like(ssum)
    dgated = dot_nt(dbranch[...], w_out[...])
    dqg[:, :, pl.ds(768, 768)] = low(dgated * mix * sg * (1.0 - sg)).reshape(2, 128, 768)
    mixed[...] = (dgated * sg).reshape(2, 128, 768)

    def attend_back(s, half):
        lanes = pl.ds(pl.multiple_of(half * SPAN, 128), SPAN)
        q = qg[s, :, lanes]
        do = low(mixed[s, :, lanes])
        k = group_of(kv, s, half * SPAN)
        v = group_of(kv, s, 768 + half * SPAN)
        q_turned, do_turned = q.T, do.T
        tiles = [None] * 3
        for j, span, a, b, covers in windows():
            width = span.stop - span.start
            masked_do = do[:, span] * lane_mask(a, b, width, jnp.bfloat16)
            dp = dot_nt(masked_do, v[:, span])
            p_low, parts = probs[s, half * GROUP + j], []
            for at in range(0, 128, 32):
                p, some = wide(probs[s, half * GROUP + j, pl.ds(at, 32)]), dp[at : at + 32]
                parts.append(low(p * (some - jnp.sum(p * some, axis=-1, keepdims=True))))
                ssum[half * GROUP + j, pl.ds(at, 32)] += parts[-1]
            ds = jnp.concatenate(parts, axis=0)
            head = slice(HEAD * j, HEAD * (j + 1))
            r.turned[0, head] = low(dot(q_turned[head], ds) * scale)
            r.turned[1, head] = low(dot(do_turned[head], p_low))
            dq = dot(ds, k[:, span]) * (lane_mask(a, b, width, jnp.float32) * scale)
            for t in covers:
                piece = dq[:, t * 128 - span.start : (t + 1) * 128 - span.start]
                tiles[t] = piece if tiles[t] is None else tiles[t] + piece
        dqg[s, :, lanes] = low(jnp.concatenate(tiles, axis=1))
        for i in range(2):
            lanes = pl.ds(pl.multiple_of(768 * i + half * SPAN, 128), SPAN)
            dkv[:, s, :, lanes] = r.turned[i].T.reshape(4, 128, SPAN)

    def far_rows(s):
        some = dkv[:, s].reshape(512, 1536)
        for k in range(2):
            weight = r.w_in[pl.ds(2 * k, 2), :, pl.ds(768, 1536)].reshape(384, 1536)
            r.held[s, :, :, pl.ds(k * 384, 384)] = low(dot_nt(some, weight)).reshape(4, 128, 384)

    def finish(s):
        part = pl.ds(s * 128, 128)
        dx = dx_own[part, :] + wide(r.held[s, me])
        n, sq = normal[part, :], squash[part, :]
        dn = dx * sq
        r.dmod[part, pl.ds(0, 768)] = low(dx * n * sq * (1.0 - sq))
        r.dmod[part, pl.ds(768, 768)] = low(dx)
        grad = wide(cotangent[s]) + inverse[part, :1] * (
            dn - jnp.mean(dn, axis=-1, keepdims=True) - n * jnp.mean(dn * n, axis=-1, keepdims=True)
        )
        r.grad_tokens[s] = grad
        r.dmid[part, :] = low(grad)
        r.spread[me, part] = low(dot_nt(low(grad), w_pool[...]))

    for some in steps.scatter:
        some[3]()

    @pl.loop(0, 2)
    def _(s):
        @pl.loop(0, 2)
        def _(half):
            attend_back(s, half)

        far_rows(s)

        @pl.when(s == 0)
        def _():
            steps.scatter[0][0]()
            steps.gu(2)

    steps.scatter[1][0]()
    steps.scores()
    steps.gu(2)
    steps.scatter[0][1]()
    flush(dqg, dkv)
    dx = dot_nt(dgu[...], w_gu[...])
    dx = dx + dot_nt(dqg[:, :, pl.ds(0, 768)].reshape(256, 768), w_in[:, pl.ds(0, 768)])
    dx_own[...] = dx + dot_nt(dqg[:, :, pl.ds(768, 768)].reshape(256, 768), w_in[:, pl.ds(2304, 768)])
    steps.scatter[1][1]()
    steps.gu(3)
    steps.scatter[0][2]()
    finish(0)
    steps.spread[0][0]()
    steps.pairs(0, 2)
    steps.gu(2)
    steps.pairs(2, 4)
    steps.scatter[1][2]()
    finish(1)
    steps.spread[1][0]()
    steps.gu(2)
    flush(r.dmod, r.dmid, r.grad_tokens, r.pair_sum)
    for some in steps.spread:
        some[1]()
    steps.gu(1)
    flush(r.spread, r.gu_out)


class Steps(typing.NamedTuple):
    own_done: object
    transition: object
    rows_ready: object
    swap_gu: object
    weights_gu: object
    gu: object
    scatter: object
    scores: object
    spread: object
    pairs: object


RIM = (WK - WQ) // 2
ATOM = 128
OWN = 160
REACH = 112
REGION = OWN + 2 * REACH
A_HEAD = ATOM // HA


def atom_modulation(c, w_mod, b_mod, k):
    return dot(c, w_mod[:, pl.ds(k * ATOM, ATOM)]) + wide(b_mod[...])[k : k + 1]


def stacked_heads(rows, dtype):
    return jnp.concatenate(
        [rows * lane_mask(A_HEAD * h, A_HEAD * (h + 1), ATOM, dtype) for h in range(HA)], axis=0
    )


def unstacked_heads(rows):
    total = None
    for h in range(HA):
        own = rows[WQ * h : WQ * (h + 1)] * lane_mask(A_HEAD * h, A_HEAD * (h + 1), ATOM, jnp.float32)
        total = own if total is None else total + own
    return total


def window_probs(stacked, keys, bias, first_key, count):
    place = first_key + lax.broadcasted_iota(jnp.int32, (1, WK), 1)
    valid = (place >= 0) & (place < count)
    scores = dot_nt(stacked, keys) * A_HEAD ** (-0.5) + wide(bias)
    scores = jnp.where(valid, scores, masked)
    scores = jnp.exp(scores - jnp.max(scores, axis=-1, keepdims=True))
    return scores * (1.0 / jnp.sum(scores, axis=-1, keepdims=True))


def token_ranges(counts):
    wide_counts = jnp.concatenate([wide(counts[...]), jnp.zeros((6, 512), jnp.float32)], axis=0)
    row = lax.broadcasted_iota(jnp.int32, (512, 512), 0)
    lane = lax.broadcasted_iota(jnp.int32, (512, 512), 1)
    before = low(jnp.where(lane < row, 1.0, 0.0))
    until = low(jnp.where(lane <= row, 1.0, 0.0))
    some = low(wide_counts)
    return dot_nt(before, some), dot_nt(until, some), dot_nt(some, before), dot_nt(some, until)


def atom_row_bias(w_pair, pairs, bias):
    w = wide(w_pair[...])
    stacked = jnp.concatenate([jnp.broadcast_to(w[h : h + 1], (WQ, CP)) for h in range(HA)], axis=0)
    row = lax.broadcasted_iota(jnp.int32, (CP, 512), 0)
    lane = lax.broadcasted_iota(jnp.int32, (CP, 512), 1)
    spread = dot(low(stacked), low(jnp.where(row == lax.rem(lane, CP), 1.0, 0.0)))
    weight = low(spread * same_query())
    for b in range(OWN // WQ):
        some = pairs[pl.ds(b * WQ, WQ)].reshape(WQ * CP, WK)
        bias[b + 2] = low(dot(weight, some))


def same_query():
    row = lax.broadcasted_iota(jnp.int32, (128, 512), 0)
    lane = lax.broadcasted_iota(jnp.int32, (128, 512), 1)
    return jnp.where(lax.rem(row, WQ) == lax.div(lane, CP), 1.0, 0.0)


def atom_forward(s, me, atoms, cond, bias, w_mod, b_mod, w_in, w_out, w_gu, w_down, out, packed, mixed):
    region = pl.ds(REACH - RIM, OWN + 2 * RIM)
    own = slice(RIM, RIM + OWN)
    hidden = wide(atoms[s, region, :])
    c = cond[s, region, :]
    normal, _ = normalize(hidden)
    squash = jax.nn.sigmoid(atom_modulation(c, w_mod, b_mod, 0))
    x = low(normal * squash + atom_modulation(c, w_mod, b_mod, 1))
    packed[...] = low(dot(x, w_in[...]))
    results = []
    for w in range(OWN // WQ):
        at = w * WQ
        q = packed[pl.ds(at + RIM, WQ), pl.ds(0, ATOM)]
        k = packed[pl.ds(at, WK), pl.ds(ATOM, ATOM)]
        v = packed[pl.ds(at, WK), pl.ds(2 * ATOM, ATOM)]
        stacked = stacked_heads(q, jnp.bfloat16)
        p = window_probs(stacked, k, bias[w + 2], me * OWN + at - RIM, 4 * OWN)
        results.append(unstacked_heads(dot(low(p), v)))
    for w, result in enumerate(results):
        mixed[pl.ds(w * WQ, WQ), :] = result
    hidden, c, x = hidden[own], c[own], x[own]
    gate = jax.nn.sigmoid(wide(packed[pl.ds(RIM, OWN), pl.ds(3 * ATOM, ATOM)]))
    branch = dot(low(mixed[...] * gate), w_out[...])
    both = low(dot(x, w_gu[...]))
    a, b = wide(both[:, :256]), wide(both[:, 256:])
    trans = dot(low(a * jax.nn.sigmoid(a) * b), w_down[...])
    total = hidden + jax.nn.sigmoid(atom_modulation(c, w_mod, b_mod, 2)) * branch
    out[me, s] = low(total + jax.nn.sigmoid(atom_modulation(c, w_mod, b_mod, 3)) * trans)


def pool_atoms(s, rows, ranges, pooled):
    total = 4 * OWN
    place = wide(lax.broadcasted_iota(jnp.int32, (1, total), 1))
    start, end = ranges[0][:, s : s + 1], ranges[1][:, s : s + 1]
    member = jnp.where((place >= start) & (place < end), 1.0, 0.0)
    sums = dot(low(member), rows[:, s].reshape(total, ATOM)) / (end - start)
    pooled[:, s] = low(sums).reshape(4, 128, ATOM)


def atom_backward(
    s,
    me,
    atoms,
    cond,
    bias,
    grad_pooled,
    ranges,
    w_mod,
    b_mod,
    w_in,
    w_out,
    w_gu,
    w_down,
    grad_atoms,
    small,
    ssum,
    packed,
    mixed,
    grad_mixed,
    dkv,
    dq,
):
    total = 640
    first = me * OWN - REACH
    own = slice(REACH, REACH + OWN)
    scale = A_HEAD ** (-0.5)

    def add_small(block, value):
        for k in range(value.shape[0] // 128):
            for n in range(value.shape[1] // 128):
                tile = value[k * 128 : (k + 1) * 128, n * 128 : (n + 1) * 128]
                at = block + k + n
                small[at // 4, at % 4] += tile.reshape(16, 8, 128)

    hidden = wide(atoms[s])
    c = cond[s]
    normal, inverse = normalize(hidden)
    squash = jax.nn.sigmoid(atom_modulation(c, w_mod, b_mod, 0))
    x = low(normal * squash + atom_modulation(c, w_mod, b_mod, 1))
    packed[...] = low(dot(x, w_in[...]))

    place = wide(first + lax.broadcasted_iota(jnp.int32, (REGION, 1), 0))
    start, end = ranges[2][s : s + 1], ranges[3][s : s + 1]
    member = jnp.where((place >= start) & (place < end), 1.0, 0.0)
    owner = jnp.sum(member * (end - start), axis=-1, keepdims=True)
    dy = dot(low(member), grad_pooled[:, pl.ds(s * 128, 128)].reshape(512, ATOM)) / jnp.maximum(owner, 1.0)
    sga = jax.nn.sigmoid(atom_modulation(c, w_mod, b_mod, 2))
    dbranch = low(dy * sga)
    dgated = dot_nt(dbranch, w_out[...])
    gate = jax.nn.sigmoid(wide(packed[:, pl.ds(3 * ATOM, ATOM)]))
    grad_mixed[...] = low(dgated * gate)
    dkv[...] = jnp.zeros_like(dkv)

    def window(w, own):
        at = pl.multiple_of(w * WQ, WQ)
        query = pl.ds(at + RIM, WQ)
        q = stacked_heads(packed[query, pl.ds(0, ATOM)], jnp.bfloat16)
        k = packed[pl.ds(at, WK), pl.ds(ATOM, ATOM)]
        v = packed[pl.ds(at, WK), pl.ds(2 * ATOM, ATOM)]
        do = stacked_heads(grad_mixed[query, :], jnp.bfloat16)
        p = window_probs(q, k, bias[w], first + at, total)
        dp = dot_nt(do, v)
        ds = low(p * (dp - jnp.sum(p * dp, axis=-1, keepdims=True)))
        out = [dot_tn(ds, q) * scale, dot_tn(low(p), do)]
        if own:
            out += [unstacked_heads(dot(low(p), v)), unstacked_heads(dot(ds, k)) * scale, wide(ds)]
        return out

    for group in ((0, 1, 7, 8), (2, 3, 4, 5, 6)):
        results = {w: window(w, 2 <= w < 7) for w in group}
        for w, result in results.items():
            keys = pl.ds(w * WQ, WK)
            dkv[keys, pl.ds(0, ATOM)] += result[0]
            dkv[keys, pl.ds(ATOM, ATOM)] += result[1]
            if 2 <= w < 7:
                rows = pl.ds((w - 2) * WQ, WQ)
                mixed[rows, :] = result[2]
                dq[rows, :] = result[3]
                ssum[w - 2] += result[4]

    x, c, hidden, normal, inverse = x[own], c[own], hidden[own], normal[own], inverse[own]
    squash, dy, sga, dbranch, dgated = squash[own], dy[own], sga[own], dbranch[own], dgated[own]
    gate = gate[own]
    gated = low(mixed[...] * gate)
    branch = dot(gated, w_out[...])
    both = low(dot(x, w_gu[...]))
    a, b = wide(both[:, :256]), wide(both[:, 256:])
    sq = jax.nn.sigmoid(a)
    inner = low(a * sq * b)
    trans = dot(inner, w_down[...])
    sgf = jax.nn.sigmoid(atom_modulation(c, w_mod, b_mod, 3))
    dga = dy * branch * sga * (1.0 - sga)
    dgf = dy * trans * sgf * (1.0 - sgf)
    dtrans = low(dy * sgf)
    dinner = dot_nt(dtrans, w_down[...])
    dgu = low(jnp.concatenate([dinner * b * sq * (1.0 + a * (1.0 - sq)), dinner * a * sq], axis=1))
    dg = dgated * mixed[...] * gate * (1.0 - gate)
    dpacked = low(jnp.concatenate([dq[...], dkv[pl.ds(REACH, OWN), :], dg], axis=1))
    dx = dot_nt(dpacked, w_in[...]) + dot_nt(dgu, w_gu[...])
    dn = dx * squash
    dscale = dx * normal * squash * (1.0 - squash)
    dmod = low(jnp.concatenate([dscale, dx, dga, dgf], axis=1))
    grad_atoms[s] = dy + inverse * (
        dn
        - jnp.mean(dn, axis=-1, keepdims=True)
        - normal * jnp.mean(dn * normal, axis=-1, keepdims=True)
    )
    add_small(0, dot_tn(c, dmod))
    add_small(4, dot_tn(x, dpacked))
    add_small(8, dot_tn(gated, dbranch))
    add_small(9, dot_tn(x, dgu))
    add_small(13, dot_tn(inner, dtrans))
    sums = jnp.sum(wide(dmod), axis=0, keepdims=True)
    for n in range(4):
        small[3, 3, 0, pl.ds(n, 1), :] += sums[:, n * 128 : (n + 1) * 128]


RING = 4


class Ring:
    def __init__(self, axis):
        self.axis = axis
        self.me = lax.axis_index(axis)
        self.up = lax.rem(self.me + 1, RING)
        self.down = lax.rem(self.me + 3, RING)
        self.far = lax.rem(self.me + 2, RING)


class Copies:
    def __init__(self, send, recv):
        self.send, self.recv, self.used = send, recv, 0

    def make(self, axis, place, src, dst):
        made = pltpu.make_async_remote_copy(
            src_ref=src,
            dst_ref=dst,
            send_sem=self.send.at[self.used],
            recv_sem=self.recv.at[self.used],
            device_id={axis: place},
            device_id_type=MESH,
        )
        self.used += 1
        return made

    def start(self, *what):
        made = self.make(*what)
        made.start()
        return made


def meet(rings, core=None):
    barrier = pltpu.get_barrier_semaphore()
    for ring in rings:
        for place in (ring.up, ring.down, ring.far):
            pl.semaphore_signal(barrier, 1, device_id={ring.axis: place}, device_id_type=MESH)
    if core is not None:
        pl.semaphore_signal(barrier, 1, device_id={"c": 1 - core}, device_id_type=MESH)
    pl.semaphore_wait(barrier, 3 * len(rings) + (core is not None))


def run_stages(parts):
    for k in range(max(len(stages) for stages in parts)):
        for stages in parts:
            if k < len(stages):
                stages[k]()


def nothing():
    pass


def add_into(target, others):
    def one(index):
        total = target[index]
        if len(others) > 1:
            total = total.astype(jnp.float32)
        for other in others:
            total = total + other[index].astype(total.dtype)
        target[index] = total.astype(target.dtype)

    lead = target.shape[:-3]

    def nest(index):
        if len(index) == len(lead):
            one(index or Ellipsis)
            return

        @pl.loop(0, lead[len(index)])
        def _(i):
            nest((*index, i))

    nest(())


def scatter_stages(ring, copies, held, first, second):
    half = held.shape[1] // 2
    low_part, high_part = pl.ds(0, half), pl.ds(half, held.shape[1] - half)
    r1, r2 = first
    r3, r4 = second
    up, down, far = ring.up, ring.down, ring.far
    made = {}

    def send(k, src, dst, to):
        made[k] = copies.start(ring.axis, to, src, dst)

    def prepare():
        made[1] = copies.make(ring.axis, up, held.at[far, low_part], r1)
        made[2] = copies.make(ring.axis, down, held.at[far, high_part], r2)
        made[3] = copies.make(ring.axis, up, held.at[up, high_part], r3.at[high_part])
        made[4] = copies.make(ring.axis, down, held.at[down, low_part], r4.at[low_part])

    def begin():
        for k in (1, 2, 3, 4):
            made[k].start()

    def middle():
        made[1].wait_recv()
        add_into(held.at[up, low_part], [r1])
        send(5, held.at[up, low_part], r3.at[low_part], up)
        made[2].wait_recv()
        add_into(held.at[down, high_part], [r2])
        send(6, held.at[down, high_part], r4.at[high_part], down)

    def end():
        for k in (3, 4, 5, 6):
            made[k].wait_recv()
        add_into(held.at[ring.me], [r3, r4])
        for k in range(1, 7):
            made[k].wait_send()

    return [begin, middle, end, prepare]


def spread_stages(ring, copies, view, parts, landed=None):
    low_parts, high_parts = parts
    made = {}

    def send(k, place, some, to):
        made[k] = [copies.start(ring.axis, to, view(place, p), view(place, p)) for p in some]

    def arrived(*what):
        for k, place, some in what:
            for one in made[k]:
                one.wait_recv()
            tell(place, some)

    def tell(place, some):
        if landed is not None:
            for p in some:
                landed(place, p)

    def begin():
        send(0, ring.me, low_parts, ring.up)
        send(1, ring.me, high_parts, ring.down)
        send(2, ring.me, high_parts, ring.up)
        send(3, ring.me, low_parts, ring.down)
        tell(ring.me, (*low_parts, *high_parts))

    def middle():
        arrived((0, ring.down, low_parts))
        send(4, ring.down, low_parts, ring.up)
        arrived((1, ring.up, high_parts))
        send(5, ring.up, high_parts, ring.down)

    def end():
        arrived((2, ring.down, high_parts), (3, ring.up, low_parts))
        arrived((4, ring.far, low_parts), (5, ring.far, high_parts))
        for some in made.values():
            for one in some:
                one.wait_send()

    return [begin, middle, end]


def direct_stages(ring, copies, *views):
    made = []

    def begin():
        for place in (ring.up, ring.down, ring.far):
            for view in views:
                made.append(copies.start(ring.axis, place, view(ring.me), view(ring.me)))

    def end():
        for one in made:
            one.wait()

    return [begin, end]


class Region:
    def __init__(self, t, x, z, y, done):
        self.t, self.done = t, {ring.axis: ring.me for ring in done}
        self.x, self.z, self.y = x, z, y

    def index(self, ring, place, half):
        known = {**self.done, ring.axis: place}
        split, out = half, []
        for one in (self.y, self.z):
            if one.axis in known:
                out.append(known[one.axis])
            elif split < 2:
                out.append(pl.ds(2 * split, 2))
                split = 2
            else:
                out.append(pl.ds(0, 4))
        inner = self.x.axis in known
        start, count = (known[self.x.axis] * self.t, self.t) if inner else (0, 4 * self.t)
        if split < 2:
            cut = count // 2
            start, count = (start, cut) if split == 0 else (start + cut, count - cut)
        return (*out, pl.ds(start, count))

    def shapes(self, ring):
        known = {*self.done, ring.axis}
        lead = [4 for one in (self.y, self.z) if one.axis not in known]
        whole = (*lead, self.t if self.x.axis in known else 4 * self.t)
        cut = whole[0] // 2
        return (cut, *whole[1:]), (whole[0] - cut, *whole[1:]), whole, whole


def region_stages(copies, ring, region, part, rooms):
    r1, r2, r3, r4 = rooms
    up, down, far = ring.up, ring.down, ring.far
    cut = r1.shape[0]
    halves = (pl.ds(0, cut), pl.ds(cut, r3.shape[0] - cut))
    made = {}

    def piece(place, half=2):
        return part.at[region.index(ring, place, half)]

    def prepare(k, src, dst, to):
        made[k] = copies.make(ring.axis, to, src, dst)

    prepare(1, piece(far, 0), r1, up)
    prepare(2, piece(far, 1), r2, down)
    prepare(3, piece(up, 1), r3.at[halves[1]], up)
    prepare(4, piece(down, 0), r4.at[halves[0]], down)
    prepare(5, piece(up, 0), r3.at[halves[0]], up)
    prepare(6, piece(down, 1), r4.at[halves[1]], down)

    def begin():
        for k in (1, 2, 3, 4):
            made[k].start()

    def middle():
        made[1].wait_recv()
        add_into(piece(up, 0), [r1])
        made[5].start()
        made[2].wait_recv()
        add_into(piece(down, 1), [r2])
        made[6].start()

    def end():
        for k in (3, 4, 5, 6):
            made[k].wait_recv()
        add_into(piece(ring.me), [r3, r4])
        for k in range(1, 7):
            made[k].wait_send()

    return [begin, middle, end]


def direct_region_stages(copies, ring, region, part, rooms):
    made = [
        copies.make(ring.axis, place, part.at[region.index(ring, place, 2)], room)
        for place, room in zip((ring.up, ring.down, ring.far), rooms, strict=False)
    ]

    def begin():
        for one in made:
            one.start()

    def end():
        for one in made:
            one.wait_recv()
        add_into(part.at[region.index(ring, ring.me, 2)], list(rooms[:3]))
        for one in made:
            one.wait_send()

    return [begin, end]


def part_stages(copies, core, x, z, y, order, t, part, out, rooms, direct=2):
    stages, done = [], []
    for k, ring in enumerate(order):
        region = Region(t, x, z, y, done)
        kind = direct_region_stages if k >= direct else region_stages
        stages += kind(copies, ring, region, part, rooms[4 * k : 4 * k + 4])
        done.append(ring)
    base = core * (4 * t)
    halves = (((0, 2),), ((2, 2),))
    pair = (((0, 2 * t),), ((2 * t, 2 * t),))

    def keep():
        out[z.me, pl.ds(base + x.me * t, t)] = part[y.me, z.me, pl.ds(x.me * t, t)]

    stages.append(keep)
    if order[0] is z:
        stages += direct_stages(x, copies, lambda place: out.at[z.me, pl.ds(base + place * t, t)])
        if direct < 2:
            return stages + direct_stages(z, copies, lambda place: out.at[place, pl.ds(base, 4 * t)])
        return stages + spread_stages(
            z, copies, lambda place, p: out.at[place, pl.ds(base + p[0], p[1])], pair
        )
    stages += direct_stages(z, copies, lambda place: out.at[place, pl.ds(base + x.me * t, t)])
    if direct < 2:
        return stages + direct_stages(x, copies, lambda place: out.at[:, pl.ds(base + place * t, t)])
    return stages + spread_stages(
        x, copies, lambda place, p: out.at[pl.ds(*p), pl.ds(base + place * t, t)], halves
    )


def swap_stages(copies, core, refs):
    made = []

    def begin():
        for ref in refs:
            made.append(copies.start("c", 1 - core, ref, ref))

    def end():
        for one in made:
            one.wait()

    return [begin, end]


def room_shapes(t, order, tile, dtype, direct=2):
    place = {axis: types.SimpleNamespace(axis=axis, me=0) for axis in order}
    x, z, y = [place[axis] for axis in ("x", "z", "fsdp")]
    shapes, done = [], []
    for axis in order:
        rooms = Region(t, x, z, y, done).shapes(place[axis])
        if order.index(axis) >= direct:
            rooms = (rooms[2],) * 3 + ((1,),)
        shapes += [pltpu.VMEM((*shape, *tile), dtype) for shape in rooms]
        done.append(place[axis])
    return shapes


COPIES = 96
ORDER_GU = ("x", "z", "fsdp")
ORDER_IN = ("z", "fsdp", "x")
ORDER_DO = ("x", "z", "fsdp")
ORDER_ME = ("fsdp", "x", "z")
ORDER_ML = ("x", "fsdp", "z")
ORDER_SM = ("fsdp", "x", "z")
ORDERS = (ORDER_IN, ORDER_DO, ORDER_ME, ORDER_ML)
SIZES = (9, 7, 3, 3)


IN, GU, MOD, DOWN, OUT, POOL = MATRICES = range(6)


class Front(typing.NamedTuple):
    given: object
    pairs: object
    cotangent: object
    counts: object
    atom_pairs: object
    aw_pair: object
    aw_mod: object
    ab_mod: object
    aw_in: object
    aw_out: object
    aw_gu: object
    aw_down: object
    b_mod: object
    w_pair: object
    results: object
    peer: object
    atoms: object
    acond: object
    abias: object
    pooled: object
    output: object
    x_turned: object
    dkv: object
    dqg: object
    gated_turned: object
    inner_turned: object
    dbranch: object
    dtrans: object
    dgates: object
    dmod: object
    dmid: object
    grad_tokens: object
    spread: object
    pair_sum: object
    gu_out: object
    w_in: object
    w_gu: object
    w_mod: object
    w_down: object
    w_out: object
    w_pool: object
    atom_out: object
    tcond: object
    tokens: object
    x_own: object
    x_mine: object
    pair_weight: object
    bias: object
    pair_rows: object
    pair_bufs: object
    packed: object
    amixed: object
    dgu: object
    probs: object
    turned: object
    gate_att: object
    mixed: object
    normal: object
    squash: object
    inverse: object
    scores_peer: object
    held: object
    scatter_rooms: object
    gu_part: object
    gu_rooms: object
    x_peer: object
    dgu_peer: object
    load: object
    pair_sems: object
    flush_sems: object
    send: object
    recv: object


FIRST_RESULT = 16


def columns(start, width):
    return pl.ds(pl.multiple_of(start, 128), width)


def rows(start, count):
    return pl.ds(pl.multiple_of(start, 16), count)


def matrix_stages(copies, full, core, x, y, z):
    moved = {name: [] for name in MATRICES}

    def block(far):
        return lax.rem(y.me + far, RING)

    def to_core(name, one):
        moved[name].append(copies.start("c", 1 - core, one, one))

    def in_y(name, first, cut, count, span, last=False):
        def view(place, p):
            return full[name].at[place, rows(first + p[0], p[1]), span]

        def landed(place, p):
            if place is not y.me:
                to_core(name, view(place, p))

        return spread_stages(y, copies, view, ([(0, cut)], [(cut, count - cut)]), landed if last else None)

    def in_plane(ring, name, place_of, count, width, last):
        def view(place, p):
            far, row, height, column, breadth = p
            first, start = place_of(place)
            return full[name].at[block(far), rows(first + row, height), columns(start + column, breadth)]

        if count >= 32:
            cut = (count // 2 + 15) // 16 * 16
            halves = (0, cut, 0, width), (cut, count - cut, 0, width)
        else:
            cut = width // 256 * 128
            halves = (0, count, 0, cut), (0, count, cut, width - cut)
        parts = [(1, 0, count, 0, width), (2, *halves[0])], [(3, 0, count, 0, width), (2, *halves[1])]
        return spread_stages(ring, copies, view, parts, (lambda place, p: to_core(name, view(place, p))) if last else None)

    def in_both(name, first_ring):
        ref, mid = full[name], core * 1536
        pieces = direct_stages(
            y,
            copies,
            lambda place: ref.at[place, rows(32 * x.me, 32), columns(mid + z.me * 384, 384)],
            lambda place: ref.at[place, rows(128 + 16 * x.me, 16), columns(mid + z.me * 384, 384)],
        )

        def x_then_z(base, height):
            one = in_plane(x, name, lambda p: (base + height * p, mid + z.me * 384), height, 384, False)
            return one, in_plane(z, name, lambda p: (base, mid + p * 384), 4 * height, 384, True)

        def z_then_x(base, height):
            one = in_plane(z, name, lambda p: (base + height * x.me, mid + p * 384), height, 384, False)
            return one, in_plane(x, name, lambda p: (base + height * p, mid), height, 1536, True)

        if first_ring is x:
            big, little = x_then_z(0, 32), z_then_x(128, 16)
        else:
            big, little = z_then_x(0, 32), x_then_z(128, 16)
        return [pieces, *([both_steps(p, q) for p, q in zip(a, b, strict=True)] for a, b in zip(big, little, strict=True))]

    def both_steps(p, q):
        def run():
            p()
            q()

        return run

    steps = {
        IN: in_both(IN, x),
        GU: in_both(GU, z),
        MOD: [
            in_y(MOD, 0, 48, 96, columns(core * 1536 + x.me * 384, 384)),
            in_plane(x, MOD, lambda place: (0, core * 1536 + place * 384), 96, 384, True),
        ],
        DOWN: [
            in_y(DOWN, 96 * z.me, 48, 96, columns(core * 384, 384)),
            in_plane(z, DOWN, lambda place: (96 * place, core * 384), 96, 384, True),
        ],
        OUT: [
            in_y(OUT, 48 * x.me, 32, 48, columns(core * 384, 384)),
            in_plane(x, OUT, lambda place: (48 * place, core * 384), 48, 384, True),
        ],
        POOL: [in_y(POOL, 0, 16, 32, columns(core * 384, 384), True)],
    }
    return steps, moved


def forward_kernel(spec, *refs):
    it = iter(refs)
    r = Front(*[next(it) if n is None else [next(it) for _ in range(n)] for n in spec])
    core = lax.axis_index("c")
    x, z, y = Ring("x"), Ring("z"), Ring("fsdp")
    me = y.me
    copies = Copies(r.send, r.recv)

    matrices = (r.w_in, r.w_gu, r.w_mod, r.w_down, r.w_out, r.w_pool)
    middle = pl.ds(REACH, OWN)
    targets = [ref.at[me] for ref in matrices] + [r.atoms.at[:, middle], r.acond.at[:, middle]]
    targets += [r.tcond.at[me], r.tokens.at[me]]
    loads = []
    for k, target in enumerate(targets):
        loads.append(pltpu.make_async_copy(r.given[k], target, r.load.at[k]))
        loads[-1].start()

    def fetch(chunk, slot):
        src = r.pairs.at[pl.ds(pl.multiple_of(core * 64 + chunk * 8, 8), 8)]
        return pltpu.make_async_copy(src, r.pair_bufs.at[slot], r.pair_sems.at[slot])

    for slot in range(2):
        fetch(slot, slot).start()
    meet((x, z, y), core)

    jobs, moved = matrix_stages(copies, matrices, core, x, y, z)
    late = []
    for ref in (r.tcond, r.tokens):
        parts = ([pl.ds(0, 1)], [pl.ds(1, 1)])
        late.append(spread_stages(y, copies, lambda place, p, ref=ref: ref.at[place, p], parts))
    atom_out = direct_stages(y, copies, lambda place: r.atom_out.at[place])
    halo = []

    def halo_begin():
        for ref in (r.atoms, r.acond):
            first, last = ref.at[:, pl.ds(REACH, REACH)], ref.at[:, pl.ds(OWN, REACH)]
            halo.append(copies.start("fsdp", y.up, last, ref.at[:, pl.ds(0, REACH)]))
            halo.append(copies.start("fsdp", y.down, first, ref.at[:, pl.ds(REACH + OWN, REACH)]))
        halo.append(copies.start("fsdp", y.up, r.abias.at[pl.ds(5, 2)], r.abias.at[pl.ds(0, 2)]))
        halo.append(copies.start("fsdp", y.down, r.abias.at[pl.ds(2, 2)], r.abias.at[pl.ds(7, 2)]))

    def halo_end():
        for one in halo:
            one.wait()

    def step(kind, stage, *which):
        for name in which:
            jobs[name][kind][stage]()

    def cores(name):
        for one in moved[name]:
            one.wait()

    def bias_steps(first, last):
        pair_rows, pair_bufs = r.pair_rows, r.pair_bufs

        @pl.loop(first, last)
        def _(i):
            for slot in range(2):
                fetch(2 * i + slot, slot).wait()
                for q in range(0, 8, 2):
                    both = jnp.concatenate([pair_bufs[slot, q], pair_bufs[slot, q + 1]], axis=1)
                    value = dot_nt(r.pair_weight[...], both)
                    pair_rows[:, 8 * slot + q, :] = value[:16]
                    pair_rows[:, 8 * slot + q + 1, :] = value[16:]

                @pl.when(i < 3)
                def _():
                    fetch(2 * i + 2 + slot, slot).start()

            r.bias[:, rows(core * 64 + i * 16, 16), :] = low(pair_rows[...])

    flushed, staged = [], r[FIRST_RESULT:]

    def flush(*which):
        for ref in which:
            k = next(i for i, one in enumerate(staged) if one is ref)
            some = ref.at[me] if ref is r.pooled else ref
            flushed.append(pltpu.make_async_copy(some, r.results[k], r.flush_sems.at[k]))
            flushed[-1].start()
            hand_over(ref)

    theirs = (r.x_turned, r.gated_turned, r.inner_turned, r.dkv, r.dqg, r.dbranch, r.dtrans, r.dgates)
    theirs = (*theirs, None, None, r.dmod, r.dmid)

    def hand_over(ref):
        for k, one in enumerate(theirs):
            if one is ref:
                width = ref.shape[-1] // 2
                lead = (slice(None),) * (len(ref.shape) - 1)
                some = ref if k < 3 else ref.at[(*lead, columns((1 - core) * width, width))]
                flushed.append(copies.start("c", 1 - core, some, r.peer[k]))

    def first_step(*which):
        for name in which:
            loads[name].wait()
            step(0, 0, name)

    def plane_step(*which):
        for name in which:
            step(0, 2, name)
            step(1, 0, name)

    first_step(IN)
    atom_row_bias(r.aw_pair, r.atom_pairs, r.abias)
    for k in (6, 7):
        loads[k].wait()
    halo_begin()
    first_step(MOD, GU, POOL, OUT, DOWN)
    step(0, 1, IN)
    step(1, 0, IN)
    for k in (8, 9):
        loads[k].wait()
    flushed.append(copies.start("c", 1 - core, r.tcond.at[me], r.peer[8]))
    turned = wide(r.w_pair[...])
    blank = jnp.zeros_like(turned)
    r.pair_weight[pl.ds(0, 16), :] = low(jnp.concatenate([turned, blank], axis=1))
    r.pair_weight[pl.ds(16, 16), :] = low(jnp.concatenate([blank, turned], axis=1))
    ranges = token_ranges(r.counts)
    step(1, 1, IN)
    halo_end()
    atom_weights = (r.aw_mod, r.ab_mod, r.aw_in, r.aw_out, r.aw_gu, r.aw_down)
    atom_room = (r.atom_out, r.packed, r.amixed)
    atom_forward(0, me, r.atoms, r.acond, r.abias, *atom_weights, *atom_room)
    step(1, 2, IN)
    step(2, 0, IN)
    step(0, 1, MOD)
    step(0, 1, GU)
    step(1, 0, GU)
    atom_forward(1, me, r.atoms, r.acond, r.abias, *atom_weights, *atom_room)
    atom_out[0]()
    flush(r.atoms, r.acond, r.abias)
    step(0, 1, POOL, OUT, DOWN)
    plane_step(MOD)
    for steps in late:
        steps[0]()
    bias_steps(0, 2)
    step(1, 1, GU)
    step(2, 1, IN)
    step(0, 2, POOL)
    plane_step(OUT, DOWN)
    step(1, 1, MOD)
    step(1, 2, GU)
    step(2, 0, GU)
    bias_steps(2, 4)
    half_bias = r.bias.at[:, rows(core * 64, 64), :]
    bias_moved = copies.start("c", 1 - core, half_bias, half_bias)
    atom_out[1]()
    for s in range(2):
        pool_atoms(s, r.atom_out, ranges, r.pooled)
    flush(r.pooled)
    flushed.append(copies.start("c", 1 - core, r.pooled.at[me], r.peer[9]))
    step(1, 2, MOD)
    step(1, 1, OUT, DOWN)
    step(2, 2, IN)
    for name in (POOL, MOD, IN):
        cores(name)

    def own_done():
        for steps in late:
            steps[1]()
        step(2, 1, GU)
        step(1, 2, OUT, DOWN)
        step(2, 2, GU)
        cores(GU)

    def transition():
        cores(DOWN)

    def rows_ready():
        for steps in late:
            steps[2]()
        cores(OUT)
        bias_moved.wait()
        for slot in range(2):
            fetch(slot, slot).start()

    scores_moved = []

    def scores():
        theirs = r.bias.at[:, rows((1 - core) * 64, 64)]
        scores_moved.append(copies.start("c", 1 - core, theirs, r.scores_peer))

    def pair_steps(first, last):
        if first == 0:
            r.pair_sum[...] = jnp.zeros_like(r.pair_sum)
            scores_moved[0].wait()
        for i in range(first, last):
            span = pl.ds(16 * i, 16)
            own_part = wide(r.bias[:, rows(core * 64 + 16 * i, 16)])
            r.pair_rows[...] = own_part + wide(r.scores_peer[:, span])
            total = jnp.zeros(r.pair_sum.shape, jnp.float32)
            for slot in range(2):
                fetch(2 * i + slot, slot).wait()
                for q in range(0, 8, 2):
                    at = 8 * slot + q
                    both = jnp.concatenate([r.pair_bufs[slot, q], r.pair_bufs[slot, q + 1]], axis=1)
                    left = jnp.concatenate([r.pair_rows[:, at, :], r.pair_rows[:, at + 1, :]], axis=0)
                    total = total + dot(low(left), both)
                if i < 3:
                    fetch(2 * i + 2 + slot, slot).start()
            r.pair_sum[...] += total

    gu_moved = []

    def swap_gu():
        gu_moved.append(copies.start("c", 1 - core, r.x_mine, r.x_peer))
        some = r.dgu.at[:, columns((1 - core) * 1536, 1536)]
        gu_moved.append(copies.start("c", 1 - core, some, r.dgu_peer))

    def weights_gu():
        for one in gu_moved:
            one.wait()
        for k in range(2):
            own = r.dgu[:, columns(core * 1536 + k * 768, 768)]
            value = low(dot_both(r.x_mine[...], own, r.x_peer[...], r.dgu_peer[:, pl.ds(k * 768, 768)]))
            for n in range(6):
                tiles = value[:, n * 128 : (n + 1) * 128].reshape(4, 4, 3, 16, 128)
                r.gu_part[:, :, pl.ds((6 * k + n) * 3, 3)] = tiles

    gu_steps = part_stages(copies, core, x, z, y, (x, z, y), 9, r.gu_part, r.gu_out, r.gu_rooms, 1)
    gu_steps += swap_stages(copies, core, [r.gu_out.at[:, pl.ds(core * 36, 36)]])

    def gu(count):
        for _ in range(count):
            gu_steps.pop(0)()

    scatter, spread = [], []
    for s in range(2):
        rooms = r.scatter_rooms[4 * s : 4 * s + 4]
        scatter.append(scatter_stages(y, copies, r.held.at[s], rooms[:2], rooms[2:]))
        part = pl.ds(s * 128, 128)
        spread.append(direct_stages(y, copies, lambda place, part=part: r.spread.at[place, part]))
    token_block(
        r, me, Steps(own_done, transition, rows_ready, swap_gu, weights_gu, gu, scatter, scores, spread, pair_steps), flush
    )
    for one in flushed:
        one.wait()
    assert not gu_steps
    assert copies.used == FRONT_COPIES


FRONT_COPIES = 360


def forward_pass(given, pairs, cotangent, counts, atom_pairs, aw_pair, atom_weights, b_mod, w_pair):
    bf, f32 = jnp.bfloat16, jnp.float32
    full = [((4, *a.shape), a.dtype) for a in given]
    results = (
        ((2, REGION, ATOM), bf),
        ((2, REGION, ATOM), bf),
        ((9, 128, 128), bf),
        ((4, 2, 128, 128), bf),
        ((2, 128, 768), f32),
        ((768, 1024), bf),
        ((4, 2, 128, 1536), bf),
        ((2, 128, 1536), bf),
        ((768, 256), bf),
        ((1536, 256), bf),
        ((256, 768), bf),
        ((256, 768), bf),
        ((256, 1536), bf),
        ((256, 1536), bf),
        ((256, 768), bf),
        ((2, 128, 768), f32),
        ((4, 256, 128), bf),
        ((32, 256), f32),
        ((4, 72, 16, 128), bf),
    )
    peer = (
        ((768, 1024), bf),
        ((768, 256), bf),
        ((1536, 256), bf),
        ((4, 2, 128, 768), bf),
        ((2, 128, 768), bf),
        ((256, 384), bf),
        ((256, 384), bf),
        ((256, 768), bf),
        ((2, 128, 384), bf),
        ((2, 128, 128), bf),
        ((256, 768), bf),
        ((256, 384), bf),
    )
    rooms = [((64, 768), bf), ((64, 768), bf), ((128, 768), bf), ((128, 768), bf)]
    outs = (*results[:3], ((2, 128, 128), bf), *results[4:], *peer)
    scratch = (
        *results,
        *full[:6],
        full[6],
        *full[8:],
        ((256, 768), bf),
        ((768, 256), bf),
        ((32, 256), bf),
        ((16, 128, 512), bf),
        ((16, 16, 512), f32),
        ((2, 8, 512, 128), bf),
        ((OWN + 2 * RIM, 512), bf),
        ((OWN, ATOM), f32),
        ((256, 3072), bf),
        ((2, 16, 128, 512), bf),
        ((2, SPAN, 512), bf),
        ((256, 768), f32),
        ((2, 128, 768), f32),
        ((256, 768), f32),
        ((256, 768), f32),
        ((256, 128), f32),
        ((16, 64, 512), bf),
        ((2, 4, 128, 768), bf),
        *rooms,
        *rooms,
        ((4, 4, 36, 16, 128), bf),
    )
    gu_rooms = room_shapes(9, ORDER_GU, (16, 128), bf, 1)
    last = [pltpu.VMEM((768, 256), bf), pltpu.VMEM((256, 1536), bf)]
    semaphores = [
        pltpu.SemaphoreType.DMA((n,)) for n in (10, 2, len(results), FRONT_COPIES, FRONT_COPIES)
    ]
    spec = [10] + [None] * 13 + [len(results), len(peer)]
    spec += [None] * (len(scratch) - 9) + [8, None, len(gu_rooms), None, None] + [None] * len(semaphores)
    return pl.pallas_call(
        functools.partial(forward_kernel, spec),
        out_shape=[jax.ShapeDtypeStruct(*o) for o in outs],
        in_specs=hbm(11) + vmem(12),
        out_specs=hbm(len(outs)),
        scratch_shapes=[pltpu.VMEM(*s) for s in scratch] + gu_rooms + last + semaphores,
        compiler_params=params(62, collective_id=1, has_side_effects=True),
        name="forward_pass",
    )(*given, pairs, cotangent, counts, atom_pairs, aw_pair, *atom_weights, b_mod, w_pair)


class Back(typing.NamedTuple):
    given: object
    peer_given: object
    pooled_grad: object
    pair_sum: object
    atoms: object
    acond: object
    abias: object
    counts: object
    aw_mod: object
    ab_mod: object
    aw_in: object
    aw_out: object
    aw_gu: object
    aw_down: object
    atom_pairs: object
    tiles: object
    small_sums: object
    grad_atoms_out: object
    own: object
    peer: object
    parts: object
    outs: object
    rooms: object
    small: object
    small_low: object
    small_peer: object
    small_out: object
    small_rooms: object
    grad_atoms: object
    packed: object
    mixed: object
    grad_mixed: object
    akv: object
    aq: object
    ascores: object
    load: object
    keep: object
    send: object
    recv: object


class Rows(typing.NamedTuple):
    x: object
    gated: object
    inner: object
    dkv: object
    dqg: object
    dbranch: object
    dtrans: object
    dgates: object
    cond: object
    pooled: object
    dmod: object
    dmid: object


def backward_kernel(spec, *refs):
    it = iter(refs)
    r = Back(*[next(it) if n is None else [next(it) for _ in range(n)] for n in spec])
    core = lax.axis_index("c")
    x, z, y = Ring("x"), Ring("z"), Ring("fsdp")
    me = y.me
    copies = Copies(r.send, r.recv)
    own, peer = Rows(*r.own), Rows(*r.peer)
    span_of = {ref.shape[-1]: columns(core * (ref.shape[-1] // 2), ref.shape[-1] // 2) for ref in own[3:8]}
    loads = {}
    for n, k in enumerate((0, 4, 3, 2, 6, 1, 5, 8, 7, 10, 9, 11)):
        loads[k] = [
            pltpu.make_async_copy(r.given[k], own[k], r.load.at[2 * n]),
            pltpu.make_async_copy(r.peer_given[k], peer[k], r.load.at[2 * n + 1]),
        ]
        for one in loads[k]:
            one.start()
    r.small[...] = jnp.zeros_like(r.small)
    meet((x, z, y), core)

    def ready(*which):
        for k in which:
            for one in loads.pop(k, ()):
                one.wait()

    mine = columns(me * 256, 256)
    part_in, part_do, part_me, part_ml = r.parts

    def place_columns(part, value, first, row_tiles, step, offset=0):
        value = low(value)
        for n in range(value.shape[1] // 128):
            tiles = value[:, n * 128 : (n + 1) * 128].reshape(4, 4, row_tiles, 16, 128)
            part[:, :, pl.ds((first + n) * step + offset, row_tiles)] = tiles

    def flat(ref):
        return ref[...].reshape(-1, ref.shape[-1])

    def mine_of(ref):
        some = ref[(*(slice(None),) * (len(ref.shape) - 1), span_of[ref.shape[-1]])]
        return some.reshape(-1, some.shape[-1])

    def weights_do():
        ready(1, 2, 5, 6)
        value = dot_both(own.inner[...], mine_of(own.dtrans), peer.inner[...], peer.dtrans[...])
        place_columns(part_do, value, 0, 6, 9)
        value = dot_both(own.gated[...], mine_of(own.dbranch), peer.gated[...], peer.dbranch[...])
        place_columns(part_do, value, 0, 3, 9, 6)

    def weights_in():
        ready(0, 3, 4)
        value = dot_both(own.x[:, mine], mine_of(own.dqg), peer.x[:, mine], flat(peer.dqg))
        place_columns(part_in, value, 6 * core, 3, 3)
        value = dot_both(own.x[...], mine_of(own.dkv), peer.x[...], flat(peer.dkv))
        place_columns(part_in, value, 6 * (1 - core), 3, 3)

    def place_mod(part, value):
        value = low(value)
        for n in range(6):
            tiles = value[:, n * 128 : (n + 1) * 128].reshape(4, 6, 16, 128)
            for k in range(2):
                at = 6 * n + 3 * k
                part[:, at // 9, pl.ds(at % 9, 3)] = tiles[:, 3 * k : 3 * k + 3]

    def weights_me():
        ready(8, 7)
        own_turned, peer_turned = flat(own.cond).T, flat(peer.cond).T
        place_mod(part_me, dot_both(own_turned, mine_of(own.dgates), peer_turned, peer.dgates[...]))

    def weights_ml():
        ready(8, 10, 9, 11)
        own_turned, peer_turned = flat(own.cond).T, flat(peer.cond).T
        place_mod(part_ml, dot_both(own_turned, mine_of(own.dmod), peer_turned, peer.dmod[...]))
        left = (flat(own.pooled).T, flat(peer.pooled).T)
        value = low(dot_both(left[0], mine_of(own.dmid), left[1], peer.dmid[...]))
        for n in range(3):
            part_ml[:, n, pl.ds(9, 2)] = value[:, n * 128 : (n + 1) * 128].reshape(4, 2, 16, 128)

    stages = []
    rings = {"x": x, "z": z, "fsdp": y}
    for k, order in enumerate(ORDERS):
        order = [rings[axis] for axis in order]
        rooms = r.rooms[12 * k : 12 * k + 12]
        some = part_stages(copies, core, x, z, y, order, SIZES[k], r.parts[k], r.outs[k], rooms, 1)
        stages.append(some)
        span = pl.ds(core * 4 * SIZES[k], 4 * SIZES[k])
        stages[-1] += swap_stages(copies, core, [r.outs[k].at[:, span]])
    s_in, s_do, s_me, s_ml = stages

    kept = []

    def out_copy(src, dst):
        kept.append(pltpu.make_async_copy(src, dst, r.keep.at[len(kept)]))
        kept[-1].start()

    def go(*which):
        for some in which:
            some.pop(0)()

    room = (r.packed, r.mixed, r.grad_mixed, r.akv, r.aq)
    weights = (r.aw_mod, r.ab_mod, r.aw_in, r.aw_out, r.aw_gu, r.aw_down)
    ranges = token_ranges(r.counts)
    r.ascores[...] = jnp.zeros_like(r.ascores)

    def atoms_of(s):
        rows_in = (r.atoms, r.acond, r.abias, r.pooled_grad, ranges)
        atom_backward(s, me, *rows_in, *weights, r.grad_atoms, r.small, r.ascores, *room)

    weights_in()
    go(s_in)
    atoms_of(0)
    weights_do()
    go(s_do)
    atoms_of(1)
    out_copy(r.grad_atoms, r.grad_atoms_out)
    r.small[3, 3, 1] = atom_pair_grad(r.ascores, r.atom_pairs)
    total = r.pair_sum[:16, :128] + r.pair_sum[16:, 128:]
    r.small[3, 3, pl.ds(3, 2)] = total.reshape(2, 8, 128)
    ready(10, 7)
    sums = jnp.sum(wide(own.dmod[...]), axis=0, keepdims=True)
    sums = jnp.concatenate([sums, jnp.sum(wide(own.dgates[...]), axis=0, keepdims=True)], axis=1)
    for n in range(24):
        r.small[3, 3, 5 + n // 8, pl.ds(n % 8, 1), :] = sums[:, n * 128 : (n + 1) * 128]

    order = [rings[axis] for axis in ORDER_SM]
    r.small_low[...] = low(r.small[...].reshape(4, 4, 8, 16, 128))
    theirs, ours = r.small_low.at[:, :, pl.ds((1 - core) * 4, 4)], r.small_low.at[:, :, pl.ds(core * 4, 4)]
    small_moved = []

    def small_begin():
        small_moved.append(copies.start("c", 1 - core, theirs, r.small_peer))

    def small_merge():
        small_moved[0].wait()
        add_into(ours, [r.small_peer])

    s_small = [small_begin, small_merge]
    s_small += part_stages(
        copies, core, x, z, y, order, 1, ours, r.small_out.at[me], r.small_rooms, 0
    )
    span = pl.ds(core * 4, 4)
    s_small += direct_stages(y, copies, lambda place: r.small_out.at[place, :, span])
    s_small += swap_stages(copies, core, [r.small_out.at[:, :, span]])
    go(s_small, s_in)
    weights_ml()
    go(s_small, s_small, s_ml)
    weights_me()
    go(s_me, s_do, s_small, s_small, s_in, s_in, s_small, s_small)
    go(s_do, s_do, s_ml, s_me, s_small, s_small, s_small, s_ml, s_ml, s_in, s_in)
    for k, some in enumerate(stages):
        some.append(lambda k=k: out_copy(r.outs[k], r.tiles[k]))
    s_small.append(lambda: out_copy(r.small_out, r.small_sums))
    run_stages([s_small, s_ml, s_in, s_do, s_me])
    for one in kept:
        one.wait()
    assert copies.used == COPIES


def atom_pair_grad(scores, pairs):
    total = jnp.zeros((128, 512), jnp.float32)
    for b in range(OWN // WQ):
        some = pairs[pl.ds(b * WQ, WQ)].reshape(WQ * CP, WK)
        total = total + dot_nt(low(scores[b]), some)
    total = total * same_query()
    heads = [jnp.sum(total[h * WQ : (h + 1) * WQ], axis=0, keepdims=True) for h in range(HA)]
    heads = jnp.concatenate([*heads, jnp.zeros((8 - HA, 512), jnp.float32)], axis=0)
    row = lax.broadcasted_iota(jnp.int32, (512, 128), 0)
    lane = lax.broadcasted_iota(jnp.int32, (512, 128), 1)
    pick = low(jnp.where(lax.rem(row, CP) == lane, 1.0, 0.0))
    return dot(low(heads), pick)


def backward_pass(given, peer_given, in_vmem):
    bf, f32 = jnp.bfloat16, jnp.float32
    tile = (16, 128)
    rows_own = [
        ((768, 1024), bf),
        ((768, 256), bf),
        ((1536, 256), bf),
        ((4, 2, 128, 1536), bf),
        ((2, 128, 1536), bf),
        ((256, 768), bf),
        ((256, 768), bf),
        ((256, 1536), bf),
        ((2, 128, 384), bf),
        ((2, 128, 128), bf),
        ((256, 1536), bf),
        ((256, 768), bf),
    ]
    rows_peer = [
        ((*shape[:-1], shape[-1] // 2) if 3 <= k <= 7 or k > 9 else shape, dtype)
        for k, (shape, dtype) in enumerate(rows_own)
    ]
    sums = [((4, 8 * t, *tile), bf) for t in SIZES]
    outs = [*sums, ((4, 4, 8, *tile), bf), ((2, OWN, ATOM), f32)]
    groups = [
        rows_own,
        rows_peer,
        [((4, 4, 4 * t, *tile), bf) for t in SIZES],
        sums,
        [
            room
            for t, order in zip(SIZES, ORDERS, strict=True)
            for room in room_shapes(t, order, tile, bf, 1)
        ],
        ((4, 4, 16, 8, 128), f32),
        ((4, 4, 8, *tile), bf),
        ((4, 4, 4, *tile), bf),
        ((4, 4, 8, *tile), bf),
        room_shapes(1, ORDER_SM, tile, bf, 0),
        outs[-1],
        ((REGION, 512), bf),
        ((OWN, ATOM), f32),
        ((REGION, ATOM), bf),
        ((REGION, 2 * ATOM), f32),
        ((OWN, ATOM), f32),
        ((OWN // WQ, 128, WK), f32),
    ]
    spec = [len(given), len(peer_given)] + [None] * len(in_vmem) + [len(SIZES), None, None]
    scratch = []
    for group in groups:
        some = group if isinstance(group, list) else [group]
        spec.append(len(some) if isinstance(group, list) else None)
        scratch += [one if not isinstance(one, tuple) else pltpu.VMEM(*one) for one in some]
    spec += [None] * 4
    scratch += [pltpu.SemaphoreType.DMA((n,)) for n in (24, 8, COPIES, COPIES)]
    return pl.pallas_call(
        functools.partial(backward_kernel, spec),
        out_shape=[jax.ShapeDtypeStruct(*o) for o in outs],
        in_specs=hbm(len(given) + len(peer_given)) + vmem(len(in_vmem)),
        out_specs=hbm(len(outs)),
        scratch_shapes=scratch,
        compiler_params=params(62, collective_id=0, has_side_effects=True),
        name="backward_pass",
    )(*given, *peer_given, *in_vmem)


class Final(typing.NamedTuple):
    tiles: object
    small: object
    plain: object
    big: object
    mod: object
    bias: object
    heads_in: object
    heads_out: object
    pair: object
    gate_up: object
    down: object
    token_pair: object
    token_bias: object
    plain_out: object
    stage: object
    sems: object
    plain_sems: object


def unpack_kernel(spec, *refs):
    it = iter(refs)
    r = Final(*[next(it) if n is None else [next(it) for _ in range(n)] for n in spec])
    kept = []
    for k, (src, dst) in enumerate(zip(r.plain, r.plain_out, strict=True)):
        kept.append(pltpu.make_async_copy(src, dst, r.plain_sems.at[k]))
        kept[-1].start()

    def out_copy(k):
        kept.append(pltpu.make_async_copy(r.stage[k], r.big[k], r.sems.at[k]))
        kept[-1].start()

    for k in range(2):
        for n in range(24):
            r.stage[k][:, pl.ds(n * 128, 128)] = wide(r.tiles[k][:, pl.ds(3 * n, 3)].reshape(192, 128))
        out_copy(k)
    for n in range(6):
        at = n // 3 * 28 + n % 3 * 9
        r.stage[2][:, pl.ds(n * 128, 128)] = wide(r.tiles[2][:, pl.ds(at, 6)].reshape(384, 128))
        r.stage[3][:, pl.ds(n * 128, 128)] = wide(r.tiles[2][:, pl.ds(at + 6, 3)].reshape(192, 128))
    out_copy(2)
    out_copy(3)
    for n in range(24):
        source = r.tiles[4 - n // 12]
        for part in range(2):
            at = n % 6 * 6 + 3 * part
            tiles = source[at // 9, pl.ds(n % 12 // 6 * 12 + at % 9, 3)].reshape(48, 128)
            r.stage[4][pl.ds(48 * part, 48), pl.ds(n * 128, 128)] = wide(tiles)
    for n in range(6):
        tiles = r.tiles[4][n % 3, pl.ds(n // 3 * 12 + 9, 2)].reshape(32, 128)
        r.stage[5][:, pl.ds(n * 128, 128)] = wide(tiles)
    out_copy(4)
    out_copy(5)

    def block(k):
        return wide(r.small[k // 4, k % 4]).reshape(128, 128)

    for target, first in ((r.mod, 0), (r.heads_in, 4), (r.gate_up, 9)):
        for n in range(4):
            target[:, pl.ds(n * 128, 128)] = block(first + n)
    r.heads_out[...] = block(8)
    r.down[pl.ds(0, 128), :] = block(13)
    r.down[pl.ds(128, 128), :] = block(14)
    rest = block(15)
    r.bias[...] = rest[:4]
    r.pair[...] = rest[8 : 8 + HA, :CP]
    r.token_pair[...] = rest[24:40]
    r.token_bias[...] = rest[40:64]
    for one in kept:
        one.wait()


def unpack(tiles, small, plain):
    f32 = jnp.float32
    big = [((192, 3072), f32), ((192, 3072), f32), ((384, 768), f32), ((192, 768), f32), ((96, 3072), f32)]
    big.append(((32, 768), f32))
    rest = [((128, 512), f32), ((4, 128), f32), ((128, 512), f32), ((128, 128), f32), ((HA, CP), f32)]
    rest += [((128, 512), f32), ((256, 128), f32), ((H, 128), f32), ((24, 128), f32)]
    outs = big + rest + [(one.shape, one.dtype) for one in plain]
    spec = [len(tiles), None, len(plain), len(big)] + [None] * len(rest) + [len(plain), len(big), None, None]
    return pl.pallas_call(
        functools.partial(unpack_kernel, spec),
        out_shape=[jax.ShapeDtypeStruct(*o) for o in outs],
        in_specs=vmem(len(tiles) + 1 + len(plain)),
        out_specs=hbm(len(big)) + vmem(len(rest)) + hbm(len(plain)),
        scratch_shapes=[
            *[pltpu.VMEM(*o) for o in big],
            pltpu.SemaphoreType.DMA((len(big),)),
            pltpu.SemaphoreType.DMA((len(plain),)),
        ],
        compiler_params=params(60),
        name="unpack",
    )(*tiles, small, *plain)


def per_device(
    atoms,
    atom_cond,
    atom_pairs,
    atom_counts,
    tokens,
    token_cond,
    token_pairs,
    cotangent,
    atom_mod,
    atom_mod_bias,
    atom_heads_in,
    atom_heads_out,
    atom_pair_proj,
    atom_gate_up,
    atom_down,
    pool_proj,
    token_mod,
    token_mod_bias,
    token_heads_in,
    token_heads_out,
    token_pair_proj,
    token_gate_up,
    token_down,
):
    given = (token_heads_in, token_gate_up, token_mod, token_down, token_heads_out, pool_proj)
    given = (*given, atoms, atom_cond, token_cond, tokens)
    atom_bias = atom_mod_bias.reshape(4, 128)
    atom_weights = (atom_mod, atom_bias, atom_heads_in, atom_heads_out, atom_gate_up, atom_down)
    turned_pairs = atom_pairs.transpose(0, 2, 1)
    (
        all_atoms,
        all_atom_cond,
        all_bias,
        pooled,
        output,
        x_turned,
        dkv,
        dqg,
        gated_turned,
        inner_turned,
        dbranch,
        dtrans,
        dgates,
        dmod,
        dmid,
        grad_tokens,
        grad_pooled,
        pair_sum,
        gate_up_tiles,
        *peer_given,
    ) = forward_pass(
        given,
        token_pairs,
        cotangent,
        atom_counts,
        turned_pairs,
        atom_pair_proj.T,
        atom_weights,
        token_mod_bias.reshape(24, 128),
        token_pair_proj.T,
    )
    own = (x_turned, gated_turned, inner_turned, dkv, dqg, dbranch, dtrans, dgates, token_cond, pooled)
    in_vmem = (grad_pooled, pair_sum, all_atoms, all_atom_cond, all_bias, atom_counts)
    *tiles, small, grad_atoms = backward_pass(
        (*own, dmod, dmid), peer_given, (*in_vmem, *atom_weights, turned_pairs)
    )
    (
        grad_gu,
        grad_in,
        grad_down,
        grad_out,
        grad_mod,
        grad_pool,
        grad_atom_mod,
        grad_atom_bias,
        grad_atom_in,
        grad_atom_out,
        grad_atom_pair,
        grad_atom_gu,
        grad_atom_down,
        grad_token_pair,
        grad_token_bias,
        output,
        grad_tokens,
        grad_atoms,
    ) = unpack((gate_up_tiles, *tiles), small, (output, grad_tokens, grad_atoms))
    return (
        output,
        grad_tokens,
        grad_atoms,
        grad_atom_mod,
        grad_atom_bias.reshape(512),
        grad_atom_in,
        grad_atom_out,
        grad_atom_pair.T,
        grad_atom_gu,
        grad_atom_down,
        grad_pool,
        grad_mod,
        grad_token_bias.reshape(3072),
        grad_in,
        grad_out,
        grad_token_pair.T,
        grad_gu,
        grad_down,
    )


def solution(mesh):
    shape = (4, 4, 2, 4) if mesh.devices.size == 128 else (1, 1, 1, mesh.devices.size)
    mesh = Mesh(mesh.devices.reshape(shape), (*DP, "fsdp"))
    in_specs = (
        P(DP, "fsdp", None),
        P(DP, "fsdp", None),
        P("fsdp", None, None),
        P(DP, None),
        P(DP, "fsdp", None),
        P(DP, "fsdp", None),
        P("fsdp", None, None),
        P(DP, "fsdp", None),
        P(),
        P(),
        P(),
        P(),
        P(),
        P(),
        P(),
        P("fsdp", None),
        P("fsdp", None),
        P(),
        P("fsdp", None),
        P("fsdp", None),
        P(),
        P("fsdp", None),
        P("fsdp", None),
    )
    out_specs = (
        P(DP, "fsdp", None),
        P(DP, "fsdp", None),
        P(DP, "fsdp", None),
        P(),
        P(),
        P(),
        P(),
        P(),
        P(),
        P(),
        P("fsdp", None),
        P("fsdp", None),
        P(),
        P("fsdp", None),
        P("fsdp", None),
        P(),
        P("fsdp", None),
        P("fsdp", None),
    )
    return jax.shard_map(
        per_device, mesh=mesh, in_specs=in_specs, out_specs=out_specs, check_vma=False
    )
```
